32 devices in a mesh: wide: 16 (over z, y, core), tp: 2 (over x).
Axes of the slice: x: 2, y: 2, z: 4, core: 2. Of those that a mesh axis runs over, the one named last changes fastest.
Arguments:
- clips: bfloat16 [32, 512, 1024], P('wide', 'tp'), may hold values from -6 to 6
- cotangent: bfloat16 [32, 512, 1024], P('wide', 'tp'), may hold values from -6 to 6
- clip_live: int32 [32], P('wide'), may hold values from 0 to 1, as said below
- qkv_weight: bfloat16 [1024, 3, 1024], P('wide', None, 'tp'), may hold values from -0.1875 to 0.1875
- q_bias: float32 [1024], P('tp'), may hold values from -5 to 5
- v_bias: float32 [1024], P('tp'), may hold values from -0.4375 to 0.4375
- proj_weight: bfloat16 [1024, 1024], P('tp', 'wide'), may hold values from -2 to 2
- fc1_weight: bfloat16 [1024, 4096], P('wide', 'tp'), may hold values from -0.1875 to 0.1875
- fc1_bias: float32 [4096], P('tp'), may hold values from -4 to 4
- fc2_weight: bfloat16 [4096, 1024], P('tp', 'wide'), may hold values from -0.09375 to 0.09375
- ln_gains: float32 [2, 1024], replicated, may hold values from 0.25 to 1.75
- ln_biases: float32 [2, 1024], replicated, may hold values from -4 to 4
- out_bias: float32 [2, 1024], replicated, may hold values from -4 to 4
Outputs:
- block_out: bfloat16 [32, 512, 1024], P('wide', 'tp')
- clips_grad: float32 [32, 512, 1024], P('wide', 'tp')
- qkv_grad: float32 [1024, 3, 1024], P('wide', None, 'tp')
- q_bias_grad: float32 [1024], P('tp')
- v_bias_grad: float32 [1024], P('tp')
- proj_grad: float32 [1024, 1024], P('tp', 'wide')
- fc1_grad: float32 [1024, 4096], P('wide', 'tp')
- fc1_bias_grad: float32 [4096], P('tp')
- fc2_grad: float32 [4096, 1024], P('tp', 'wide')
- ln_gains_grad: float32 [2, 1024], replicated
- ln_biases_grad: float32 [2, 1024], replicated
- out_bias_grad: float32 [2, 1024], replicated
The draws below stay inside these ranges and needn't reach their ends.
Inputs may be any that keep to these rules, and one draw needn't show every extreme that they name: `clip_live`: in each group's 2 consecutive slots the live ones come first; every group has at least one live slot, and some group has all 2 live.
All inputs are finite; a program needn't handle non-finite values.
Results may differ from the reference program's by a relative error of at most 0.015.
The reference program's roundings to bfloat16 on the way count: a program that leaves them out, or rounds other values in their place, can miss the bound.
Values may be sent and summed in bfloat16 or wider, within the bound.
No kernel may reach another device: no remote copies, remote signals or barrier semaphores. Data moves between devices by JAX's collectives and lax.ppermute only.
A program may use at most 128 MiB of HBM per device.

```python
import math
from functools import partial
import jax
import jax.numpy as jnp
from jax import lax

D = 1024
HEADS = 16
HEAD_DIM = 64
FF = 4096
L = 512
MB = 2
GROUPS = 16
SLOTS = 32
TOKENS = 16384


def draw_clip_live(key, part):
    counts = jax.random.randint(jax.random.fold_in(key, 11), (GROUPS,), 1, MB + 1)
    fullest = jax.random.randint(jax.random.fold_in(key, 12), (), 0, GROUPS)
    counts = jnp.where(jnp.arange(GROUPS) == fullest, MB, counts)
    slot_index = jnp.arange(MB)
    return (slot_index[None, :] < counts[:, None]).astype(jnp.int32).reshape(GROUPS * MB)


def block_scale(key, shape, split, smallest, largest):
    loudness, own = 1.0, jax.random.fold_in(key, 6)
    for dim, shards_of in split:
        steps = jnp.exp(jax.random.uniform(jax.random.fold_in(own, dim), (shards_of,), jnp.float32, smallest / len(split), largest / len(split)))
        loudness = loudness * jnp.repeat(steps, shape[dim] // shards_of).reshape([-1 if axis == dim else 1 for axis in range(len(shape))])
    return loudness


def scatter_about(rng, dims, scale, bound, cuts=(), kind=jnp.bfloat16):
    result = jax.random.normal(rng, dims, jnp.float32) * scale
    if len(cuts) > 0:
        result = block_scale(rng, dims, cuts, -0.22, 0.18) * result
    return jnp.clip(result, min=-bound, max=bound).astype(kind)


def setup_inputs(seed: int = 0) -> dict:
    seeds = jax.random.split(jax.random.key(seed), 14)
    clips = scatter_about(seeds[0], (SLOTS, L, D), 1.0, 6.0, ((0, 16), (1, 2)))
    cotangent = scatter_about(seeds[1], (SLOTS, L, D), 1.0, 6.0, ((0, 16), (1, 2)))
    clip_live = draw_clip_live(jax.random.fold_in(seeds[13], 71), 0)
    qkv_weight = scatter_about(seeds[3], (D, 3, D), D ** -0.5, 0.1875, ((0, 16), (2, 2)))
    q_bias = scatter_about(seeds[4], (D,), 1.0, 5.0, ((0, 2),), jnp.float32)
    v_bias = scatter_about(seeds[5], (D,), 0.03, 0.4375, ((0, 2),), jnp.float32)
    proj_weight = scatter_about(seeds[6], (D, D), (max(1, 4 * D // L)) ** -0.5, 2.0, ((0, 2), (1, 16)))
    fc1_weight = scatter_about(seeds[7], (D, FF), D ** -0.5, 0.1875, ((0, 16), (1, 2)))
    fc1_bias = scatter_about(seeds[8], (FF,), 0.5, 4.0, ((0, 2),), jnp.float32)
    fc2_weight = scatter_about(seeds[9], (FF, D), FF ** -0.5, 0.09375, ((0, 2), (1, 16)))
    ln_gains = jnp.clip(1.0 + 0.15 * jax.random.normal(seeds[10], (2, D), jnp.float32), 0.25, 1.75)
    ln_biases = scatter_about(seeds[11], (2, D), 0.3, 4.0, (), jnp.float32)
    out_bias = scatter_about(seeds[12], (2, D), 0.3, 4.0, (), jnp.float32)
    return dict(clips=clips, cotangent=cotangent, clip_live=clip_live, qkv_weight=qkv_weight, q_bias=q_bias, v_bias=v_bias, proj_weight=proj_weight, fc1_weight=fc1_weight, fc1_bias=fc1_bias, fc2_weight=fc2_weight, ln_gains=ln_gains, ln_biases=ln_biases, out_bias=out_bias)


@jax.custom_vjp
def low(v):
    return lax.optimization_barrier(v.astype(jnp.bfloat16)).astype(jnp.float32)

@jax.custom_vjp
def low_back(v):
    return v

def low_keep(v):
    return (low(v), None)

def low_pass(kept, grad):
    return (grad,)

def back_keep(v):
    return (v, None)

def back_low(kept, grad):
    return (low(grad),)
low.defvjp(low_keep, low_pass)
low_back.defvjp(back_keep, back_low)
norm_eps = 1e-06

def matmul(left_op, right_op):
    return jnp.dot(left_op, right_op, precision=lax.Precision.HIGHEST)

def layer_norm(in_rows, gain_row, shift_row):
    row_mean = lax.optimization_barrier(jnp.mean(in_rows, axis=-1, keepdims=True))
    centred = in_rows - row_mean
    spread = lax.optimization_barrier(jnp.mean(centred * centred, axis=-1, keepdims=True))
    return centred * lax.rsqrt(spread + norm_eps) * gain_row + shift_row

def attend(query_block, key_rows, value_rows):
    scores = low_back(jnp.einsum('qhd,khd->hqk', query_block, key_rows, precision=lax.Precision.HIGHEST))
    weights = jax.nn.softmax(scores, axis=-1)
    return jnp.einsum('hqk,khd->qhd', low(weights), value_rows, precision=lax.Precision.HIGHEST)

def clip_layer(live_flag, in_rows, qkv_w, q_b, v_b, proj_w, fc1_w, fc1_b, fc2_w, gain_rows, shift_rows, bias_rows):
    length = in_rows.shape[0]
    block_rows = 512 if length % 512 == 0 else length
    q_scale = 1.0 / math.sqrt(HEAD_DIM)
    h_one = low(layer_norm(in_rows, gain_rows[0], shift_rows[0]))
    part_q = low_back(matmul(h_one, qkv_w[:, 0, :]))
    part_k = low_back(matmul(h_one, qkv_w[:, 1, :]))
    part_v = low_back(matmul(h_one, qkv_w[:, 2, :]))
    query = low((part_q + q_b) * q_scale).reshape(length // block_rows, block_rows, HEADS, HEAD_DIM)
    key_rows = low(part_k).reshape(length, HEADS, HEAD_DIM)
    value_rows = low(part_v + v_b).reshape(length, HEADS, HEAD_DIM)
    mixed = lax.map(jax.checkpoint(partial(attend, key_rows=key_rows, value_rows=value_rows)), query)
    attn_in = low(low_back(mixed.reshape(length, HEADS * HEAD_DIM)))
    mid_rows = in_rows + low_back(matmul(attn_in, proj_w)) + bias_rows[0]
    h_two = low(layer_norm(mid_rows, gain_rows[1], shift_rows[1]))
    pre_act = low_back(matmul(h_two, fc1_w)) + fc1_b
    hidden = low(jax.nn.gelu(pre_act, approximate=False))
    return live_flag * (mid_rows + low_back(matmul(hidden, fc2_w)) + bias_rows[1])

def reference(clips, cotangent, clip_live, qkv_weight, q_bias, v_bias, proj_weight, fc1_weight, fc1_bias, fc2_weight, ln_gains, ln_biases, out_bias):
    params = tuple((weight_in.astype(jnp.float32) for weight_in in (qkv_weight, q_bias, v_bias, proj_weight, fc1_weight, fc1_bias, fc2_weight, ln_gains, ln_biases, out_bias)))
    live_flags = clip_live.astype(jnp.float32)

    def one_clip(totals, inputs):
        in_rows, cot_rows, live_flag = inputs
        layer_out, pullback = jax.vjp(partial(clip_layer, live_flag), in_rows.astype(jnp.float32), *params)
        grads = pullback(cot_rows.astype(jnp.float32))
        totals = jax.tree.map(jnp.add, totals, tuple(grads[1:]))
        return (totals, (layer_out.astype(jnp.bfloat16), grads[0]))
    zeros = tuple((jnp.zeros_like(weight_in) for weight_in in params))
    totals, (block_out, clips_grad) = lax.scan(one_clip, zeros, (clips, cotangent, live_flags))
    factor = 1.0 / math.sqrt(TOKENS)
    return (block_out, clips_grad, totals[0] * factor, totals[1] * factor, totals[2] * factor, totals[3] * factor, totals[4] * factor, totals[5] * factor, totals[6] * factor, totals[7] * factor, totals[8] * factor, totals[9] * factor)
```

```python
from functools import partial
import math

import jax
import jax.numpy as jnp
from jax import lax
from jax.experimental import pallas as pl
from jax.experimental.pallas import tpu as pltpu
from jax.sharding import PartitionSpec as P

HEAD_DIM = 64


norm_eps = 1e-06
root_half = 1.0 / math.sqrt(2.0)
inv_root_two_pi = 1.0 / math.sqrt(2.0 * math.pi)


def layer_norm(in_rows, gain_row, shift_row):
    row_mean = jnp.mean(in_rows, axis=-1, keepdims=True)
    centred = in_rows - row_mean
    spread = jnp.mean(centred * centred, axis=-1, keepdims=True)
    inverse = lax.rsqrt(spread + norm_eps)
    unit_rows = centred * inverse
    return (unit_rows * gain_row + shift_row, unit_rows, inverse)


def norm_back(grad_rows, unit_rows, inverse, gain_row):
    scaled = grad_rows * gain_row
    mean_one = jnp.mean(scaled, axis=-1, keepdims=True)
    second = jnp.mean(scaled * unit_rows, axis=-1, keepdims=True)
    return inverse * (scaled - mean_one - unit_rows * second)


def contract_last(left_op, right_op):
    return lax.dot_general(
        left_op, right_op, (((1,), (1,)), ((), ())), preferred_element_type=jnp.float32
    )


def contract_first(left_op, right_op):
    return lax.dot_general(
        left_op, right_op, (((0,), (0,)), ((), ())), preferred_element_type=jnp.float32
    )


def attend_block(query, key_rows, value_rows):
    scores = jnp.einsum("qhd,khd->hqk", query, key_rows, preferred_element_type=jnp.float32)
    row_max = jnp.max(scores, axis=-1, keepdims=True)
    weights = jnp.exp(scores - row_max)
    row_sum = jnp.sum(weights, axis=-1, keepdims=True)
    prob_rows = (weights / row_sum).astype(jnp.bfloat16)
    mixed_rows = jnp.einsum(
        "hqk,khd->qhd", prob_rows, value_rows, preferred_element_type=jnp.float32
    )
    return (mixed_rows, row_max[..., 0] + jnp.log(row_sum[..., 0]))


def attend_back(query, grad_rows, log_total, key_rows, value_rows):
    scores = jnp.einsum("qhd,khd->hqk", query, key_rows, preferred_element_type=jnp.float32)
    prob_rows = jnp.exp(scores - log_total[..., None])
    dprobs = jnp.einsum("qhd,khd->hqk", grad_rows, value_rows, preferred_element_type=jnp.float32)
    row_delta = jnp.sum(prob_rows * dprobs, axis=-1, keepdims=True)
    dscores = (prob_rows * (dprobs - row_delta)).astype(jnp.bfloat16)
    dquery = jnp.einsum("hqk,khd->qhd", dscores, key_rows, preferred_element_type=jnp.float32)
    d_keys = jnp.einsum("hqk,qhd->khd", dscores, query, preferred_element_type=jnp.float32)
    dvalues = jnp.einsum(
        "hqk,qhd->khd",
        prob_rows.astype(jnp.bfloat16),
        grad_rows,
        preferred_element_type=jnp.float32,
    )
    return (dquery, d_keys, dvalues)


def shared_slots(
    clips,
    cotangent,
    clip_live,
    qkv_weight,
    q_bias,
    v_bias,
    proj_weight,
    fc1_weight,
    fc1_bias,
    fc2_weight,
    ln_gains,
    ln_biases,
    out_bias,
):
    tp_count = lax.axis_size("tp")
    wide_count = lax.axis_size("wide")
    slot_count, shard_rows, width = clips.shape
    length = shard_rows * tp_count
    local_cols = qkv_weight.shape[2]
    heads_here = local_cols // HEAD_DIM
    hidden_here = fc1_weight.shape[1]
    q_scale = 1.0 / math.sqrt(HEAD_DIM)
    grad_scale = 1.0 / math.sqrt(wide_count * slot_count * length)
    block_rows = 512
    blocks = length // block_rows
    tp_place = lax.axis_index("tp")
    live_slots = clip_live.astype(jnp.float32)
    qv_bias = jnp.stack([q_bias, v_bias])
    own_weights = (qkv_weight, proj_weight, fc1_weight, fc2_weight)

    def one_slot(state_in, inputs):
        rows_in, cot_in, live_one = inputs
        tied_weights = lax.optimization_barrier((own_weights, rows_in))[0]
        w_qkv, w_proj, w_fc1, w_fc2 = (
            lax.all_gather(tied_weights[0], "wide", axis=0, tiled=True),
            lax.all_gather(tied_weights[1], "wide", axis=1, tiled=True),
            lax.all_gather(tied_weights[2], "wide", axis=0, tiled=True),
            lax.all_gather(tied_weights[3], "wide", axis=1, tiled=True),
        )
        x_rows = rows_in.astype(jnp.float32)
        norm_one, unit_one, inv_one = layer_norm(x_rows, ln_gains[0], ln_biases[0])
        h1_full = lax.all_gather(norm_one.astype(jnp.bfloat16), "tp", axis=0, tiled=True)
        qkv_flat = w_qkv.reshape(width, 3 * local_cols)
        projected = jnp.dot(h1_full, qkv_flat, preferred_element_type=jnp.float32).reshape(
            length, 3, local_cols
        )
        query = (
            ((projected[:, 0] + qv_bias[0]) * q_scale)
            .astype(jnp.bfloat16)
            .reshape(length, heads_here, HEAD_DIM)
        )
        key_rows = projected[:, 1].astype(jnp.bfloat16).reshape(length, heads_here, HEAD_DIM)
        value_rows = (
            (projected[:, 2] + qv_bias[1])
            .astype(jnp.bfloat16)
            .reshape(length, heads_here, HEAD_DIM)
        )
        query_blocks = query.reshape(blocks, block_rows, heads_here, HEAD_DIM)
        mixed_blocks, log_totals = lax.map(
            partial(attend_block, key_rows=key_rows, value_rows=value_rows), query_blocks
        )
        attn_out = mixed_blocks.reshape(length, local_cols).astype(jnp.bfloat16)
        attn_sum = lax.psum_scatter(
            jnp.dot(attn_out, w_proj, preferred_element_type=jnp.float32),
            "tp",
            scatter_dimension=0,
            tiled=True,
        )
        mid_rows = x_rows + attn_sum + out_bias[0]
        norm_two, unit_two, inv_two = layer_norm(mid_rows, ln_gains[1], ln_biases[1])
        h2_full = lax.all_gather(norm_two.astype(jnp.bfloat16), "tp", axis=0, tiled=True)
        pre_act = jnp.dot(h2_full, w_fc1, preferred_element_type=jnp.float32) + fc1_bias
        cdf_part = 0.5 * (1.0 + lax.erf(pre_act * root_half))
        hidden = (pre_act * cdf_part).astype(jnp.bfloat16)
        mlp_sum = lax.psum_scatter(
            jnp.dot(hidden, w_fc2, preferred_element_type=jnp.float32).astype(jnp.bfloat16),
            "tp",
            scatter_dimension=0,
            tiled=True,
        ).astype(jnp.float32)
        block_out = (live_one * (mid_rows + mlp_sum + out_bias[1])).astype(jnp.bfloat16)
        out_grad = live_one * cot_in.astype(jnp.float32)
        out_full = lax.all_gather(out_grad.astype(jnp.bfloat16), "tp", axis=0, tiled=True)
        g_fc2 = contract_first(hidden, out_full)
        act_grad = contract_last(out_full, w_fc2)
        slope = cdf_part + pre_act * jnp.exp(-0.5 * pre_act * pre_act) * inv_root_two_pi
        pre_grad = act_grad * slope
        pre_grad_b = pre_grad.astype(jnp.bfloat16)
        g_fc1 = contract_first(h2_full, pre_grad_b)
        g_fc1b = jnp.sum(pre_grad, axis=0)
        norm_two_grad = lax.psum_scatter(
            contract_last(pre_grad_b, w_fc1), "tp", scatter_dimension=0, tiled=True
        )
        mid_grad = out_grad + norm_back(norm_two_grad, unit_two, inv_two, ln_gains[1])
        attn_full = lax.all_gather(mid_grad.astype(jnp.bfloat16), "tp", axis=0, tiled=True)
        g_proj = contract_first(attn_out, attn_full)
        mixed_grad = (
            contract_last(attn_full, w_proj)
            .astype(jnp.bfloat16)
            .reshape(blocks, block_rows, heads_here, HEAD_DIM)
        )

        def back_block(block_state, pieces):
            query_b, grad_b, lse_b = pieces
            d_query, d_keys, d_values = attend_back(query_b, grad_b, lse_b, key_rows, value_rows)
            return ((block_state[0] + d_keys, block_state[1] + d_values), d_query)

        empty_kv = jnp.zeros((length, heads_here, HEAD_DIM), jnp.float32)
        (key_grad, value_grad), query_grad = lax.scan(
            back_block, (empty_kv, empty_kv), (query_blocks, mixed_grad, log_totals)
        )
        query_grad = query_grad.reshape(length, local_cols) * q_scale
        key_grad = key_grad.reshape(length, local_cols)
        value_grad = value_grad.reshape(length, local_cols)
        g_qvb = jnp.stack([jnp.sum(query_grad, axis=0), jnp.sum(value_grad, axis=0)])
        proj_grads = (
            jnp.stack([query_grad, key_grad, value_grad], axis=1)
            .astype(jnp.bfloat16)
            .reshape(length, 3 * local_cols)
        )
        g_qkv = contract_first(h1_full, proj_grads).reshape(width, 3, local_cols)
        norm_one_grad = lax.psum_scatter(
            contract_last(proj_grads, qkv_flat).astype(jnp.bfloat16),
            "tp",
            scatter_dimension=0,
            tiled=True,
        ).astype(jnp.float32)
        in_grad = mid_grad + norm_back(norm_one_grad, unit_one, inv_one, ln_gains[0])
        gain_part = jnp.stack(
            [jnp.sum(norm_one_grad * unit_one, axis=0), jnp.sum(norm_two_grad * unit_two, axis=0)]
        )
        shift_part = jnp.stack([jnp.sum(norm_one_grad, axis=0), jnp.sum(norm_two_grad, axis=0)])
        bias_part = jnp.stack([jnp.sum(mid_grad, axis=0), jnp.sum(out_grad, axis=0)])
        summed = (
            lax.psum_scatter(
                g_qkv.astype(jnp.bfloat16), "wide", scatter_dimension=0, tiled=True
            ).astype(jnp.float32),
            lax.psum_scatter(
                g_proj.astype(jnp.bfloat16), "wide", scatter_dimension=1, tiled=True
            ).astype(jnp.float32),
            lax.psum_scatter(
                g_fc1.astype(jnp.bfloat16), "wide", scatter_dimension=0, tiled=True
            ).astype(jnp.float32),
            lax.psum_scatter(
                g_fc2.astype(jnp.bfloat16), "wide", scatter_dimension=1, tiled=True
            ).astype(jnp.float32),
        )
        weight_acc = jax.tree.map(jnp.add, state_in[0], summed)
        vector_acc = jax.tree.map(
            jnp.add, state_in[1], (gain_part, shift_part, bias_part, g_qvb, g_fc1b)
        )
        return ((weight_acc, vector_acc), (block_out, in_grad))

    weight_zero = tuple((jnp.zeros(shard_in.shape, jnp.float32) for shard_in in own_weights))
    vector_zero = (
        jnp.zeros((2, width), jnp.float32),
        jnp.zeros((2, width), jnp.float32),
        jnp.zeros((2, width), jnp.float32),
        jnp.zeros((2, local_cols), jnp.float32),
        jnp.zeros((hidden_here,), jnp.float32),
    )
    (weight_sums, vector_acc), (block_out, clips_grad) = lax.scan(
        one_slot, (weight_zero, vector_zero), (clips, cotangent, live_slots)
    )
    gain_acc, shift_acc, bias_acc, qvb_acc, fc1b_acc = vector_acc
    qvb_pad = lax.dynamic_update_slice(
        jnp.zeros((2, width), jnp.float32), qvb_acc, (0, tp_place * local_cols)
    )
    fc1b_pad = lax.dynamic_update_slice(
        jnp.zeros((hidden_here * tp_count,), jnp.float32), fc1b_acc, (tp_place * hidden_here,)
    )
    gain_sum, shift_sum, bias_sum, qvb_sum, fc1b_sum = lax.psum(
        (gain_acc, shift_acc, bias_acc, qvb_pad, fc1b_pad), ("wide", "tp")
    )
    qvb_own = lax.dynamic_slice_in_dim(qvb_sum, tp_place * local_cols, local_cols, 1)
    fc1b_own = lax.dynamic_slice_in_dim(fc1b_sum, tp_place * hidden_here, hidden_here, 0)
    return (
        block_out,
        clips_grad,
        weight_sums[0] * grad_scale,
        qvb_own[0] * grad_scale,
        qvb_own[1] * grad_scale,
        weight_sums[1] * grad_scale,
        weight_sums[2] * grad_scale,
        fc1b_own * grad_scale,
        weight_sums[3] * grad_scale,
        gain_sum * grad_scale,
        shift_sum * grad_scale,
        bias_sum * grad_scale,
    )


AXES = ("wide", "tp")
PAIR = 128


def fits_own_slot(mesh):
    return mesh.shape["tp"] == 2 and mesh.shape["wide"] % 4 == 0


def nt_dot(left_op, right_op):
    return lax.dot_general(
        left_op, right_op, (((1,), (1,)), ((), ())), preferred_element_type=jnp.float32
    )


def nn_dot(left_op, right_op):
    return lax.dot_general(
        left_op, right_op, (((1,), (0,)), ((), ())), preferred_element_type=jnp.float32
    )


def attend_kernel(q_ref, k_ref, v_ref, o_ref, lse_ref):
    pair = pl.program_id(0)
    rows = q_ref.shape[0]
    lanes = lax.broadcasted_iota(jnp.int32, (rows, PAIR), 1)
    keys = k_ref[...]
    values = v_ref[...]
    total = jnp.zeros((rows, PAIR), jnp.float32)
    for half in range(2):
        mask = (lanes // HEAD_DIM) == half
        query = jnp.where(mask, q_ref[...], jnp.zeros_like(keys))
        scores = nt_dot(query, keys)
        row_max = jnp.max(scores, axis=-1, keepdims=True)
        weights = jnp.exp(scores - row_max)
        row_sum = jnp.sum(weights, axis=-1, keepdims=True)
        probs = (weights * (1.0 / row_sum)).astype(jnp.bfloat16)
        mixed = nn_dot(probs, values)
        total = jnp.where(mask, mixed, total)
        lse = row_max + jnp.log(row_sum)
        lse_ref[...] = jnp.where(lanes == 2 * pair + half, lse, lse_ref[...])
    o_ref[...] = total.astype(jnp.bfloat16)


def attend_fwd(query, keys, values):
    length, width = query.shape
    block = pl.BlockSpec((length, PAIR), lambda i: (0, i))
    return pl.pallas_call(
        attend_kernel,
        grid=(width // PAIR,),
        in_specs=[block, block, block],
        out_specs=[block, pl.BlockSpec((length, PAIR), lambda i: (0, 0))],
        out_shape=[
            jax.ShapeDtypeStruct((length, width), jnp.bfloat16),
            jax.ShapeDtypeStruct((length, PAIR), jnp.float32),
        ],
        compiler_params=pltpu.CompilerParams(vmem_limit_bytes=40 * 1024 * 1024),
        cost_estimate=pl.CostEstimate(
            flops=8 * length * length * width,
            bytes_accessed=8 * length * width,
            transcendentals=length * length * (width // HEAD_DIM),
        ),
        name="attend_fwd",
    )(query, keys, values)


def attend_back_kernel(q_ref, k_ref, v_ref, g_ref, lse_ref, dq_ref, dk_ref, dv_ref, qs_ref, vs_ref):
    pair = pl.program_id(0)
    rows = q_ref.shape[0]
    lanes = lax.broadcasted_iota(jnp.int32, (rows, PAIR), 1)
    query = q_ref[...]
    keys = k_ref[...]
    values = v_ref[...]
    grads = g_ref[...]
    blank = jnp.zeros_like(keys)
    keys_t = keys.T
    dq_t = jnp.zeros((PAIR, rows), jnp.float32)
    dk = jnp.zeros((rows, PAIR), jnp.float32)
    dv = jnp.zeros((rows, PAIR), jnp.float32)
    for half in range(2):
        mask = (lanes // HEAD_DIM) == half
        scores_t = nt_dot(jnp.where(mask, keys, blank), query)
        lse = lse_ref[pl.ds(2 * pair + half, 1), :]
        probs_t = jnp.exp(scores_t - lse)
        dprobs_t = nt_dot(jnp.where(mask, values, blank), grads)
        delta = jnp.sum(probs_t * dprobs_t, axis=0, keepdims=True)
        ds_t = (probs_t * (dprobs_t - delta)).astype(jnp.bfloat16)
        dv = jnp.where(mask, nn_dot(probs_t.astype(jnp.bfloat16), grads), dv)
        dk = jnp.where(mask, nn_dot(ds_t, query), dk)
        sub = lax.broadcasted_iota(jnp.int32, (PAIR, rows), 0)
        dq_t = jnp.where((sub // HEAD_DIM) == half, nn_dot(keys_t, ds_t), dq_t)
    dq = dq_t.T * (1.0 / math.sqrt(HEAD_DIM))
    dq_ref[...] = dq.astype(jnp.bfloat16)
    dk_ref[...] = dk.astype(jnp.bfloat16)
    dv_ref[...] = dv.astype(jnp.bfloat16)
    qs_ref[...] = jnp.sum(dq, axis=0, keepdims=True)
    vs_ref[...] = jnp.sum(dv, axis=0, keepdims=True)


def attend_bwd(query, keys, values, grads, lse_rows):
    length, width = query.shape
    block = pl.BlockSpec((length, PAIR), lambda i: (0, i))
    row = pl.BlockSpec((1, PAIR), lambda i: (0, i))
    shape = jax.ShapeDtypeStruct((length, width), jnp.bfloat16)
    sums = jax.ShapeDtypeStruct((1, width), jnp.float32)
    return pl.pallas_call(
        attend_back_kernel,
        grid=(width // PAIR,),
        in_specs=[block] * 4 + [pl.BlockSpec((PAIR, length), lambda i: (0, 0))],
        out_specs=[block] * 3 + [row] * 2,
        out_shape=[shape] * 3 + [sums] * 2,
        compiler_params=pltpu.CompilerParams(vmem_limit_bytes=40 * 1024 * 1024),
        cost_estimate=pl.CostEstimate(
            flops=20 * length * length * width,
            bytes_accessed=14 * length * width,
            transcendentals=length * length * (width // HEAD_DIM),
        ),
        name="attend_bwd",
    )(query, keys, values, grads, lse_rows)


class Links:
    def __init__(self):
        self.nz = lax.axis_size("wide") // 4
        self.across = self.table(lambda z, y, c, x: (z, y, c, 1 - x))
        self.beside = self.table(lambda z, y, c, x: (z, 1 - y, c, x))
        self.twin = self.table(lambda z, y, c, x: (z, y, 1 - c, x))

    def table(self, source):
        pairs = []
        for z in range(self.nz):
            for y in range(2):
                for c in range(2):
                    for x in range(2):
                        zs, ys, cs, xs = source(z, y, c, x)
                        pairs.append(
                            (((zs * 2 + ys) * 2 + cs) * 2 + xs, ((z * 2 + y) * 2 + c) * 2 + x)
                        )
        return pairs

    def from_z(self, rows, step):
        shift = self.table(lambda z, y, c, x: ((z + step) % self.nz, y, c, x))
        return lax.ppermute(rows, AXES, shift)

    def x(self, rows):
        return lax.ppermute(rows, AXES, self.across)

    def y(self, rows):
        return lax.ppermute(rows, AXES, self.beside)

    def c(self, rows):
        return lax.ppermute(rows, AXES, self.twin)


def gather_chunk(links, shard):
    along = jnp.concatenate([shard] + [links.from_z(shard, k) for k in range(1, links.nz)], axis=0)
    half = along.shape[0] // 2
    by_x = links.x(along)
    by_y = links.y(along)
    far_a = links.x(by_y[:half])
    far_b = links.y(by_x[half:])
    mine = (along, by_x, by_y, far_a, far_b)
    other = tuple(links.c(piece) for piece in mine)
    own_half = jnp.concatenate([along, by_y, other[0], other[2]], axis=0)
    far_half = jnp.concatenate(
        [by_x, far_a, far_b, other[1], other[3], other[4]], axis=0
    )
    return own_half, far_half


def scatter_chunk(links, make_piece, rows_all):
    half_rows = rows_all // 2
    quarter = rows_all // 4
    sent = [make_piece(half_rows, half_rows, kx, None) for kx in range(2)]
    got = [links.c(piece) for piece in sent]
    keep = {
        (kx, ky): make_piece(ky * quarter, quarter, kx, got[kx][ky * quarter : (ky + 1) * quarter])
        for kx, ky in ((1, 1), (1, 0), (0, 1), (0, 0))
    }
    mid = quarter // 2
    f32 = jnp.float32
    far_a = links.x(keep[1, 1][:mid])
    far_b = links.y(keep[1, 1][mid:])
    out_y = (
        keep[0, 1]
        .astype(f32)
        .at[:mid]
        .add(far_a.astype(f32))
        .astype(jnp.bfloat16)
    )
    out_x = (
        keep[1, 0]
        .astype(f32)
        .at[mid:]
        .add(far_b.astype(f32))
        .astype(jnp.bfloat16)
    )
    total = (
        keep[0, 0].astype(f32) + links.x(out_x).astype(f32) + links.y(out_y).astype(f32)
    )
    shard_rows = quarter // links.nz
    total_b = total.astype(jnp.bfloat16)
    final = total[:shard_rows]
    for k in range(1, links.nz):
        block = total_b[k * shard_rows : (k + 1) * shard_rows]
        back = links.from_z(block, links.nz - k)
        final = final + back.astype(f32)
    return final


def own_slot(
    clips,
    cotangent,
    clip_live,
    qkv_weight,
    q_bias,
    v_bias,
    proj_weight,
    fc1_weight,
    fc1_bias,
    fc2_weight,
    ln_gains,
    ln_biases,
    out_bias,
):
    f32 = jnp.float32
    bf16 = jnp.bfloat16
    links = Links()
    slot_count, shard_rows, width = clips.shape
    wide_count = lax.axis_size("wide")
    length = 2 * shard_rows
    block = qkv_weight.shape[0]
    heads_cols = qkv_weight.shape[2]
    hidden_here = fc1_weight.shape[1]
    q_scale = 1.0 / math.sqrt(HEAD_DIM)
    grad_scale = 1.0 / math.sqrt(wide_count * slot_count * length)
    wide_at = lax.axis_index("wide")
    t = lax.axis_index("tp")
    z_at, y_at, c_at = wide_at // 4, (wide_at // 2) % 2, wide_at % 2

    spot = jnp.arange(width)
    rel = spot // block
    kc, ky, kz = rel // (2 * links.nz), (rel // links.nz) % 2, rel % links.nz
    source = (((z_at + kz) % links.nz * 2 + (y_at ^ ky)) * 2 + (c_at ^ kc)) * block + spot % block
    order = spot[:, None] == source[None, :]
    order_b = order.astype(bf16)
    exact = partial(jnp.dot, precision=lax.Precision.HIGHEST)
    order_f = order.astype(f32)

    pick = lambda both, at: lax.dynamic_index_in_dim(both, at, 0, keepdims=False)
    sent_rows = jnp.concatenate([pick(clips, 1 - t), pick(cotangent, 1 - t)], axis=0)
    got_rows = links.x(sent_rows)
    live = pick(clip_live, t).astype(f32)
    x_b = jnp.concatenate([pick(clips, t), got_rows[:shard_rows]], axis=0)
    cot_b = jnp.concatenate([pick(cotangent, t), got_rows[shard_rows:]], axis=0)
    x_rows = nn_dot(x_b, order_b)
    cot_rows = nn_dot(cot_b, order_b)
    vectors = exact(jnp.concatenate([ln_gains, ln_biases, out_bias], axis=0), order_f)
    gains, shifts, outs = vectors[0:2], vectors[2:4], vectors[4:6]
    far_small = jnp.concatenate([q_bias, v_bias, fc1_bias])[None]
    far_small = links.x(far_small)[0]
    q_biases = (q_bias, far_small[:heads_cols])
    v_biases = (v_bias, far_small[heads_cols : 2 * heads_cols])
    fc1_biases = (fc1_bias, far_small[2 * heads_cols :])

    chunk_one = jnp.concatenate([qkv_weight.reshape(block, 3 * heads_cols), proj_weight.T], axis=1)
    w_one = gather_chunk(links, chunk_one)
    w_fc1 = gather_chunk(links, fc1_weight)
    w_fc2 = gather_chunk(links, fc2_weight.T)
    qkv_cols = 3 * heads_cols
    w_qkv = [w[:, :qkv_cols] for w in w_one]
    w_proj = [w[:, qkv_cols:] for w in w_one]

    norm_one, unit_one, inv_one = layer_norm(x_rows, gains[0], shifts[0])
    h1 = norm_one.astype(bf16)
    queries, keys, values = [], [], []
    for kx in range(2):
        projected = nn_dot(h1, w_qkv[kx])
        queries.append(((projected[:, :heads_cols] + q_biases[kx]) * q_scale).astype(bf16))
        keys.append(projected[:, heads_cols : 2 * heads_cols].astype(bf16))
        values.append((projected[:, 2 * heads_cols :] + v_biases[kx]).astype(bf16))
    query, key_rows, value_rows = (jnp.concatenate(part, axis=1) for part in (queries, keys, values))
    attn_out, lse = attend_fwd(query, key_rows, value_rows)
    halves = lambda rows, size: (rows[:, :size], rows[:, size:])
    attn_halves = halves(attn_out, heads_cols)
    mid_rows = (
        x_rows + nt_dot(attn_halves[0], w_proj[0]) + nt_dot(attn_halves[1], w_proj[1]) + outs[0]
    )
    norm_two, unit_two, inv_two = layer_norm(mid_rows, gains[1], shifts[1])
    h2 = norm_two.astype(bf16)
    hidden, slope = [], []
    for kx in range(2):
        pre_act = nn_dot(h2, w_fc1[kx]) + fc1_biases[kx]
        cdf_part = 0.5 * (1.0 + lax.erf(pre_act * root_half))
        hidden.append((pre_act * cdf_part).astype(bf16))
        slope.append(cdf_part + pre_act * jnp.exp(-0.5 * pre_act * pre_act) * inv_root_two_pi)
    out_grad = live * cot_rows
    e_b = out_grad.astype(bf16)

    def fc2_piece(first, count, kx, extra):
        piece = contract_first(e_b[:, first : first + count], hidden[kx])
        return (piece if extra is None else piece + extra.astype(f32)).astype(bf16)

    g_fc2 = scatter_chunk(links, fc2_piece, width)
    mlp_sum = nt_dot(hidden[0], w_fc2[0]) + nt_dot(hidden[1], w_fc2[1])
    block_out = (live * (mid_rows + mlp_sum + outs[1])).astype(bf16)
    pre_grad = [nn_dot(e_b, w_fc2[kx]) * slope[kx] for kx in range(2)]
    pre_grad_b = [rows.astype(bf16) for rows in pre_grad]
    g_fc1b = [jnp.sum(rows, axis=0) for rows in pre_grad]

    def fc1_piece(first, count, kx, extra):
        piece = contract_first(h2[:, first : first + count], pre_grad_b[kx])
        return (piece if extra is None else piece + extra.astype(f32)).astype(bf16)

    g_fc1 = scatter_chunk(links, fc1_piece, width)
    norm_two_grad = nt_dot(pre_grad_b[0], w_fc1[0]) + nt_dot(pre_grad_b[1], w_fc1[1])
    mid_grad = out_grad + norm_back(norm_two_grad, unit_two, inv_two, gains[1])
    da_b = mid_grad.astype(bf16)
    mixed_grad = jnp.concatenate([nn_dot(da_b, w_proj[kx]) for kx in range(2)], axis=1).astype(bf16)
    dq, dk, dv, q_sums, v_sums = attend_bwd(query, key_rows, value_rows, mixed_grad, lse.T)
    parts = [halves(rows, heads_cols) for rows in (dq, dk, dv)]
    one_sides = [jnp.concatenate([p[kx] for p in parts], axis=1) for kx in range(2)]

    def one_piece(first, count, kx, extra):
        cols = slice(first, first + count)
        piece = jnp.concatenate(
            [
                contract_first(h1[:, cols], one_sides[kx]),
                contract_first(da_b[:, cols], attn_halves[kx]),
            ],
            axis=1,
        )
        return (piece if extra is None else piece + extra.astype(f32)).astype(bf16)

    g_one = scatter_chunk(links, one_piece, width)
    norm_one_grad = nt_dot(one_sides[0], w_qkv[0]) + nt_dot(one_sides[1], w_qkv[1])
    in_grad = mid_grad + norm_back(norm_one_grad, unit_one, inv_one, gains[0])

    sums = jnp.stack(
        [
            jnp.sum(norm_one_grad * unit_one, axis=0),
            jnp.sum(norm_two_grad * unit_two, axis=0),
            jnp.sum(norm_one_grad, axis=0),
            jnp.sum(norm_two_grad, axis=0),
            jnp.sum(mid_grad, axis=0),
            jnp.sum(out_grad, axis=0),
        ]
    )
    sums = lax.dot_general(
        sums, order_f, (((1,), (1,)), ((), ())), precision=lax.Precision.HIGHEST
    )
    placed = lambda near, far: jnp.where(
        t == 0, jnp.concatenate([near, far]), jnp.concatenate([far, near])
    )
    q_all = placed(*(q_sums[0, :heads_cols], q_sums[0, heads_cols:]))
    v_all = placed(*(v_sums[0, :heads_cols], v_sums[0, heads_cols:]))
    fc1b_all = placed(*g_fc1b)
    sums, q_all, v_all, fc1b_all = lax.psum((sums, q_all, v_all, fc1b_all), AXES)
    own = lambda full, size: lax.dynamic_slice_in_dim(full, t * size, size, 0) * grad_scale

    def back_home(rows_rel):
        rows = lax.dot_general(
            rows_rel.astype(bf16), order_b, (((1,), (1,)), ((), ())), preferred_element_type=f32
        ).astype(bf16)
        got = links.x(rows[shard_rows:])
        near = rows[:shard_rows]
        return jnp.where(t == 0, jnp.stack([near, got]), jnp.stack([got, near]))

    return (
        back_home(block_out),
        back_home(in_grad).astype(f32),
        g_one[:, :qkv_cols].reshape(block, 3, heads_cols) * grad_scale,
        own(q_all, heads_cols),
        own(v_all, heads_cols),
        g_one[:, qkv_cols:].T * grad_scale,
        g_fc1 * grad_scale,
        own(fc1b_all, hidden_here),
        g_fc2.T * grad_scale,
        sums[0:2] * grad_scale,
        sums[2:4] * grad_scale,
        sums[4:6] * grad_scale,
    )


def solution(mesh):
    body = own_slot if fits_own_slot(mesh) else shared_slots
    return jax.shard_map(
        body,
        mesh=mesh,
        in_specs=(
            P("wide", "tp", None),
            P("wide", "tp", None),
            P("wide"),
            P("wide", None, "tp"),
            P("tp"),
            P("tp"),
            P("tp", "wide"),
            P("wide", "tp"),
            P("tp"),
            P("tp", "wide"),
            P(),
            P(),
            P(),
        ),
        out_specs=(
            P("wide", "tp", None),
            P("wide", "tp", None),
            P("wide", None, "tp"),
            P("tp"),
            P("tp"),
            P("tp", "wide"),
            P("wide", "tp"),
            P("tp"),
            P("tp", "wide"),
            P(),
            P(),
            P(),
        ),
        check_vma=False,
    )
```

```python
from functools import partial
import math

import jax
import jax.numpy as jnp
from jax import lax
from jax.experimental import pallas as pl
from jax.experimental.pallas import tpu as pltpu
from jax.sharding import PartitionSpec as P

HEAD_DIM = 64


norm_eps = 1e-06
root_half = 1.0 / math.sqrt(2.0)
inv_root_two_pi = 1.0 / math.sqrt(2.0 * math.pi)


def layer_norm(in_rows, gain_row, shift_row):
    row_mean = jnp.mean(in_rows, axis=-1, keepdims=True)
    centred = in_rows - row_mean
    spread = jnp.mean(centred * centred, axis=-1, keepdims=True)
    inverse = lax.rsqrt(spread + norm_eps)
    unit_rows = centred * inverse
    return (unit_rows * gain_row + shift_row, unit_rows, inverse)


def norm_back(grad_rows, unit_rows, inverse, gain_row):
    scaled = grad_rows * gain_row
    mean_one = jnp.mean(scaled, axis=-1, keepdims=True)
    second = jnp.mean(scaled * unit_rows, axis=-1, keepdims=True)
    return inverse * (scaled - mean_one - unit_rows * second)


def contract_last(left_op, right_op):
    return lax.dot_general(
        left_op, right_op, (((1,), (1,)), ((), ())), preferred_element_type=jnp.float32
    )


def contract_first(left_op, right_op):
    return lax.dot_general(
        left_op, right_op, (((0,), (0,)), ((), ())), preferred_element_type=jnp.float32
    )


def attend_block(query, key_rows, value_rows):
    scores = jnp.einsum("qhd,khd->hqk", query, key_rows, preferred_element_type=jnp.float32)
    row_max = jnp.max(scores, axis=-1, keepdims=True)
    weights = jnp.exp(scores - row_max)
    row_sum = jnp.sum(weights, axis=-1, keepdims=True)
    prob_rows = (weights / row_sum).astype(jnp.bfloat16)
    mixed_rows = jnp.einsum(
        "hqk,khd->qhd", prob_rows, value_rows, preferred_element_type=jnp.float32
    )
    return (mixed_rows, row_max[..., 0] + jnp.log(row_sum[..., 0]))


def attend_back(query, grad_rows, log_total, key_rows, value_rows):
    scores = jnp.einsum("qhd,khd->hqk", query, key_rows, preferred_element_type=jnp.float32)
    prob_rows = jnp.exp(scores - log_total[..., None])
    dprobs = jnp.einsum("qhd,khd->hqk", grad_rows, value_rows, preferred_element_type=jnp.float32)
    row_delta = jnp.sum(prob_rows * dprobs, axis=-1, keepdims=True)
    dscores = (prob_rows * (dprobs - row_delta)).astype(jnp.bfloat16)
    dquery = jnp.einsum("hqk,khd->qhd", dscores, key_rows, preferred_element_type=jnp.float32)
    d_keys = jnp.einsum("hqk,qhd->khd", dscores, query, preferred_element_type=jnp.float32)
    dvalues = jnp.einsum(
        "hqk,qhd->khd",
        prob_rows.astype(jnp.bfloat16),
        grad_rows,
        preferred_element_type=jnp.float32,
    )
    return (dquery, d_keys, dvalues)


def shared_slots(
    clips,
    cotangent,
    clip_live,
    qkv_weight,
    q_bias,
    v_bias,
    proj_weight,
    fc1_weight,
    fc1_bias,
    fc2_weight,
    ln_gains,
    ln_biases,
    out_bias,
):
    tp_count = lax.axis_size("tp")
    wide_count = lax.axis_size("wide")
    slot_count, shard_rows, width = clips.shape
    length = shard_rows * tp_count
    local_cols = qkv_weight.shape[2]
    heads_here = local_cols // HEAD_DIM
    hidden_here = fc1_weight.shape[1]
    q_scale = 1.0 / math.sqrt(HEAD_DIM)
    grad_scale = 1.0 / math.sqrt(wide_count * slot_count * length)
    block_rows = 512
    blocks = length // block_rows
    tp_place = lax.axis_index("tp")
    live_slots = clip_live.astype(jnp.float32)
    qv_bias = jnp.stack([q_bias, v_bias])
    own_weights = (qkv_weight, proj_weight, fc1_weight, fc2_weight)

    def one_slot(state_in, inputs):
        rows_in, cot_in, live_one = inputs
        tied_weights = lax.optimization_barrier((own_weights, rows_in))[0]
        w_qkv, w_proj, w_fc1, w_fc2 = (
            lax.all_gather(tied_weights[0], "wide", axis=0, tiled=True),
            lax.all_gather(tied_weights[1], "wide", axis=1, tiled=True),
            lax.all_gather(tied_weights[2], "wide", axis=0, tiled=True),
            lax.all_gather(tied_weights[3], "wide", axis=1, tiled=True),
        )
        x_rows = rows_in.astype(jnp.float32)
        norm_one, unit_one, inv_one = layer_norm(x_rows, ln_gains[0], ln_biases[0])
        h1_full = lax.all_gather(norm_one.astype(jnp.bfloat16), "tp", axis=0, tiled=True)
        qkv_flat = w_qkv.reshape(width, 3 * local_cols)
        projected = jnp.dot(h1_full, qkv_flat, preferred_element_type=jnp.float32).reshape(
            length, 3, local_cols
        )
        query = (
            ((projected[:, 0] + qv_bias[0]) * q_scale)
            .astype(jnp.bfloat16)
            .reshape(length, heads_here, HEAD_DIM)
        )
        key_rows = projected[:, 1].astype(jnp.bfloat16).reshape(length, heads_here, HEAD_DIM)
        value_rows = (
            (projected[:, 2] + qv_bias[1])
            .astype(jnp.bfloat16)
            .reshape(length, heads_here, HEAD_DIM)
        )
        query_blocks = query.reshape(blocks, block_rows, heads_here, HEAD_DIM)
        mixed_blocks, log_totals = lax.map(
            partial(attend_block, key_rows=key_rows, value_rows=value_rows), query_blocks
        )
        attn_out = mixed_blocks.reshape(length, local_cols).astype(jnp.bfloat16)
        attn_sum = lax.psum_scatter(
            jnp.dot(attn_out, w_proj, preferred_element_type=jnp.float32),
            "tp",
            scatter_dimension=0,
            tiled=True,
        )
        mid_rows = x_rows + attn_sum + out_bias[0]
        norm_two, unit_two, inv_two = layer_norm(mid_rows, ln_gains[1], ln_biases[1])
        h2_full = lax.all_gather(norm_two.astype(jnp.bfloat16), "tp", axis=0, tiled=True)
        pre_act = jnp.dot(h2_full, w_fc1, preferred_element_type=jnp.float32) + fc1_bias
        cdf_part = 0.5 * (1.0 + lax.erf(pre_act * root_half))
        hidden = (pre_act * cdf_part).astype(jnp.bfloat16)
        mlp_sum = lax.psum_scatter(
            jnp.dot(hidden, w_fc2, preferred_element_type=jnp.float32).astype(jnp.bfloat16),
            "tp",
            scatter_dimension=0,
            tiled=True,
        ).astype(jnp.float32)
        block_out = (live_one * (mid_rows + mlp_sum + out_bias[1])).astype(jnp.bfloat16)
        out_grad = live_one * cot_in.astype(jnp.float32)
        out_full = lax.all_gather(out_grad.astype(jnp.bfloat16), "tp", axis=0, tiled=True)
        g_fc2 = contract_first(hidden, out_full)
        act_grad = contract_last(out_full, w_fc2)
        slope = cdf_part + pre_act * jnp.exp(-0.5 * pre_act * pre_act) * inv_root_two_pi
        pre_grad = act_grad * slope
        pre_grad_b = pre_grad.astype(jnp.bfloat16)
        g_fc1 = contract_first(h2_full, pre_grad_b)
        g_fc1b = jnp.sum(pre_grad, axis=0)
        norm_two_grad = lax.psum_scatter(
            contract_last(pre_grad_b, w_fc1), "tp", scatter_dimension=0, tiled=True
        )
        mid_grad = out_grad + norm_back(norm_two_grad, unit_two, inv_two, ln_gains[1])
        attn_full = lax.all_gather(mid_grad.astype(jnp.bfloat16), "tp", axis=0, tiled=True)
        g_proj = contract_first(attn_out, attn_full)
        mixed_grad = (
            contract_last(attn_full, w_proj)
            .astype(jnp.bfloat16)
            .reshape(blocks, block_rows, heads_here, HEAD_DIM)
        )

        def back_block(block_state, pieces):
            query_b, grad_b, lse_b = pieces
            d_query, d_keys, d_values = attend_back(query_b, grad_b, lse_b, key_rows, value_rows)
            return ((block_state[0] + d_keys, block_state[1] + d_values), d_query)

        empty_kv = jnp.zeros((length, heads_here, HEAD_DIM), jnp.float32)
        (key_grad, value_grad), query_grad = lax.scan(
            back_block, (empty_kv, empty_kv), (query_blocks, mixed_grad, log_totals)
        )
        query_grad = query_grad.reshape(length, local_cols) * q_scale
        key_grad = key_grad.reshape(length, local_cols)
        value_grad = value_grad.reshape(length, local_cols)
        g_qvb = jnp.stack([jnp.sum(query_grad, axis=0), jnp.sum(value_grad, axis=0)])
        proj_grads = (
            jnp.stack([query_grad, key_grad, value_grad], axis=1)
            .astype(jnp.bfloat16)
            .reshape(length, 3 * local_cols)
        )
        g_qkv = contract_first(h1_full, proj_grads).reshape(width, 3, local_cols)
        norm_one_grad = lax.psum_scatter(
            contract_last(proj_grads, qkv_flat).astype(jnp.bfloat16),
            "tp",
            scatter_dimension=0,
            tiled=True,
        ).astype(jnp.float32)
        in_grad = mid_grad + norm_back(norm_one_grad, unit_one, inv_one, ln_gains[0])
        gain_part = jnp.stack(
            [jnp.sum(norm_one_grad * unit_one, axis=0), jnp.sum(norm_two_grad * unit_two, axis=0)]
        )
        shift_part = jnp.stack([jnp.sum(norm_one_grad, axis=0), jnp.sum(norm_two_grad, axis=0)])
        bias_part = jnp.stack([jnp.sum(mid_grad, axis=0), jnp.sum(out_grad, axis=0)])
        summed = (
            lax.psum_scatter(
                g_qkv.astype(jnp.bfloat16), "wide", scatter_dimension=0, tiled=True
            ).astype(jnp.float32),
            lax.psum_scatter(
                g_proj.astype(jnp.bfloat16), "wide", scatter_dimension=1, tiled=True
            ).astype(jnp.float32),
            lax.psum_scatter(
                g_fc1.astype(jnp.bfloat16), "wide", scatter_dimension=0, tiled=True
            ).astype(jnp.float32),
            lax.psum_scatter(
                g_fc2.astype(jnp.bfloat16), "wide", scatter_dimension=1, tiled=True
            ).astype(jnp.float32),
        )
        weight_acc = jax.tree.map(jnp.add, state_in[0], summed)
        vector_acc = jax.tree.map(
            jnp.add, state_in[1], (gain_part, shift_part, bias_part, g_qvb, g_fc1b)
        )
        return ((weight_acc, vector_acc), (block_out, in_grad))

    weight_zero = tuple((jnp.zeros(shard_in.shape, jnp.float32) for shard_in in own_weights))
    vector_zero = (
        jnp.zeros((2, width), jnp.float32),
        jnp.zeros((2, width), jnp.float32),
        jnp.zeros((2, width), jnp.float32),
        jnp.zeros((2, local_cols), jnp.float32),
        jnp.zeros((hidden_here,), jnp.float32),
    )
    (weight_sums, vector_acc), (block_out, clips_grad) = lax.scan(
        one_slot, (weight_zero, vector_zero), (clips, cotangent, live_slots)
    )
    gain_acc, shift_acc, bias_acc, qvb_acc, fc1b_acc = vector_acc
    qvb_pad = lax.dynamic_update_slice(
        jnp.zeros((2, width), jnp.float32), qvb_acc, (0, tp_place * local_cols)
    )
    fc1b_pad = lax.dynamic_update_slice(
        jnp.zeros((hidden_here * tp_count,), jnp.float32), fc1b_acc, (tp_place * hidden_here,)
    )
    gain_sum, shift_sum, bias_sum, qvb_sum, fc1b_sum = lax.psum(
        (gain_acc, shift_acc, bias_acc, qvb_pad, fc1b_pad), ("wide", "tp")
    )
    qvb_own = lax.dynamic_slice_in_dim(qvb_sum, tp_place * local_cols, local_cols, 1)
    fc1b_own = lax.dynamic_slice_in_dim(fc1b_sum, tp_place * hidden_here, hidden_here, 0)
    return (
        block_out,
        clips_grad,
        weight_sums[0] * grad_scale,
        qvb_own[0] * grad_scale,
        qvb_own[1] * grad_scale,
        weight_sums[1] * grad_scale,
        weight_sums[2] * grad_scale,
        fc1b_own * grad_scale,
        weight_sums[3] * grad_scale,
        gain_sum * grad_scale,
        shift_sum * grad_scale,
        bias_sum * grad_scale,
    )


AXES = ("wide", "tp")
PAIR = 128


def fits_own_slot(mesh):
    return mesh.shape["tp"] == 2 and mesh.shape["wide"] % 4 == 0


def nt_dot(left_op, right_op):
    return lax.dot_general(
        left_op, right_op, (((1,), (1,)), ((), ())), preferred_element_type=jnp.float32
    )


def nn_dot(left_op, right_op):
    return lax.dot_general(
        left_op, right_op, (((1,), (0,)), ((), ())), preferred_element_type=jnp.float32
    )


def attend_kernel(q_ref, k_ref, v_ref, o_ref, lse_ref):
    pair = pl.program_id(0)
    rows = q_ref.shape[0]
    lanes = lax.broadcasted_iota(jnp.int32, (rows, PAIR), 1)
    keys = k_ref[...]
    values = v_ref[...]
    total = jnp.zeros((rows, PAIR), jnp.float32)
    for half in range(2):
        mask = (lanes // HEAD_DIM) == half
        query = jnp.where(mask, q_ref[...], jnp.zeros_like(keys))
        scores = nt_dot(query, keys)
        row_max = jnp.max(scores, axis=-1, keepdims=True)
        weights = jnp.exp(scores - row_max)
        row_sum = jnp.sum(weights, axis=-1, keepdims=True)
        probs = (weights * (1.0 / row_sum)).astype(jnp.bfloat16)
        mixed = nn_dot(probs, values)
        total = jnp.where(mask, mixed, total)
        lse = row_max + jnp.log(row_sum)
        lse_ref[...] = jnp.where(lanes == 2 * pair + half, lse, lse_ref[...])
    o_ref[...] = total.astype(jnp.bfloat16)


def attend_fwd(query, keys, values):
    length, width = query.shape
    block = pl.BlockSpec((length, PAIR), lambda i: (0, i))
    return pl.pallas_call(
        attend_kernel,
        grid=(width // PAIR,),
        in_specs=[block, block, block],
        out_specs=[block, pl.BlockSpec((length, PAIR), lambda i: (0, 0))],
        out_shape=[
            jax.ShapeDtypeStruct((length, width), jnp.bfloat16),
            jax.ShapeDtypeStruct((length, PAIR), jnp.float32),
        ],
        compiler_params=pltpu.CompilerParams(vmem_limit_bytes=40 * 1024 * 1024),
        cost_estimate=pl.CostEstimate(
            flops=8 * length * length * width,
            bytes_accessed=8 * length * width,
            transcendentals=length * length * (width // HEAD_DIM),
        ),
        name="attend_fwd",
    )(query, keys, values)


def attend_back_kernel(q_ref, k_ref, v_ref, g_ref, lse_ref, dq_ref, dk_ref, dv_ref, qs_ref, vs_ref):
    pair = pl.program_id(0)
    rows = q_ref.shape[0]
    lanes = lax.broadcasted_iota(jnp.int32, (rows, PAIR), 1)
    query = q_ref[...]
    keys = k_ref[...]
    values = v_ref[...]
    grads = g_ref[...]
    blank = jnp.zeros_like(keys)
    keys_t = keys.T
    dq_t = jnp.zeros((PAIR, rows), jnp.float32)
    dk = jnp.zeros((rows, PAIR), jnp.float32)
    dv = jnp.zeros((rows, PAIR), jnp.float32)
    for half in range(2):
        mask = (lanes // HEAD_DIM) == half
        scores_t = nt_dot(jnp.where(mask, keys, blank), query)
        lse = lse_ref[pl.ds(2 * pair + half, 1), :]
        probs_t = jnp.exp(scores_t - lse)
        dprobs_t = nt_dot(jnp.where(mask, values, blank), grads)
        delta = jnp.sum(probs_t * dprobs_t, axis=0, keepdims=True)
        ds_t = (probs_t * (dprobs_t - delta)).astype(jnp.bfloat16)
        dv = jnp.where(mask, nn_dot(probs_t.astype(jnp.bfloat16), grads), dv)
        dk = jnp.where(mask, nn_dot(ds_t, query), dk)
        sub = lax.broadcasted_iota(jnp.int32, (PAIR, rows), 0)
        dq_t = jnp.where((sub // HEAD_DIM) == half, nn_dot(keys_t, ds_t), dq_t)
    dq = dq_t.T * (1.0 / math.sqrt(HEAD_DIM))
    dq_ref[...] = dq.astype(jnp.bfloat16)
    dk_ref[...] = dk.astype(jnp.bfloat16)
    dv_ref[...] = dv.astype(jnp.bfloat16)
    qs_ref[...] = jnp.sum(dq, axis=0, keepdims=True)
    vs_ref[...] = jnp.sum(dv, axis=0, keepdims=True)


def attend_bwd(query, keys, values, grads, lse_rows):
    length, width = query.shape
    block = pl.BlockSpec((length, PAIR), lambda i: (0, i))
    row = pl.BlockSpec((1, PAIR), lambda i: (0, i))
    shape = jax.ShapeDtypeStruct((length, width), jnp.bfloat16)
    sums = jax.ShapeDtypeStruct((1, width), jnp.float32)
    return pl.pallas_call(
        attend_back_kernel,
        grid=(width // PAIR,),
        in_specs=[block] * 4 + [pl.BlockSpec((PAIR, length), lambda i: (0, 0))],
        out_specs=[block] * 3 + [row] * 2,
        out_shape=[shape] * 3 + [sums] * 2,
        compiler_params=pltpu.CompilerParams(vmem_limit_bytes=40 * 1024 * 1024),
        cost_estimate=pl.CostEstimate(
            flops=20 * length * length * width,
            bytes_accessed=14 * length * width,
            transcendentals=length * length * (width // HEAD_DIM),
        ),
        name="attend_bwd",
    )(query, keys, values, grads, lse_rows)


class Links:
    def __init__(self):
        self.nz = lax.axis_size("wide") // 4
        self.across = self.table(lambda z, y, c, x: (z, y, c, 1 - x))
        self.beside = self.table(lambda z, y, c, x: (z, 1 - y, c, x))
        self.twin = self.table(lambda z, y, c, x: (z, y, 1 - c, x))

    def table(self, source):
        pairs = []
        for z in range(self.nz):
            for y in range(2):
                for c in range(2):
                    for x in range(2):
                        zs, ys, cs, xs = source(z, y, c, x)
                        pairs.append(
                            (((zs * 2 + ys) * 2 + cs) * 2 + xs, ((z * 2 + y) * 2 + c) * 2 + x)
                        )
        return pairs

    def from_z(self, rows, step):
        shift = self.table(lambda z, y, c, x: ((z + step) % self.nz, y, c, x))
        return lax.ppermute(rows, AXES, shift)

    def x(self, rows):
        return lax.ppermute(rows, AXES, self.across)

    def y(self, rows):
        return lax.ppermute(rows, AXES, self.beside)

    def c(self, rows):
        return lax.ppermute(rows, AXES, self.twin)

    def flip(self, rows, bit):
        swap = self.table(lambda z, y, c, x: (z ^ bit, y, c, x))
        return lax.ppermute(rows, AXES, swap)


def after(done, *values):
    return lax.optimization_barrier((values, done))[0]


def gather_along(links, shard):
    steps = [links.from_z(shard, k) for k in range(1, links.nz)]
    return jnp.concatenate([shard] + steps, axis=0)


def gather_near(links, along):
    return links.x(along), links.y(along)


def gather_far(links, along, near):
    by_x, by_y = near
    half = along.shape[0] // 2
    far_a = links.x(by_y[:half])
    far_b = links.y(by_x[half:])
    other = [links.c(piece) for piece in (along, by_x, by_y, far_a, far_b)]
    own_half = jnp.concatenate([along, by_y, other[0], other[2]], axis=0)
    far_half = jnp.concatenate([by_x, far_a, far_b, other[1], other[3], other[4]], axis=0)
    return own_half, far_half


def scatter_keep(links, keep):
    f32 = jnp.float32
    quarter = keep[0, 0].shape[0]
    mid = quarter // 2
    far_a = links.x(keep[1, 1][:mid])
    far_b = links.y(keep[1, 1][mid:])
    out_y = keep[0, 1].astype(f32).at[:mid].add(far_a.astype(f32)).astype(jnp.bfloat16)
    out_x = keep[1, 0].astype(f32).at[mid:].add(far_b.astype(f32)).astype(jnp.bfloat16)
    total = keep[0, 0].astype(f32) + links.x(out_x).astype(f32) + links.y(out_y).astype(f32)
    shard_rows = quarter // links.nz
    total_b = total.astype(jnp.bfloat16)
    final = total[:shard_rows]
    for k in range(1, links.nz):
        block = total_b[k * shard_rows : (k + 1) * shard_rows]
        final = final + links.from_z(block, links.nz - k).astype(f32)
    return final


def total_over_all(links, rows):
    for move in (links.c, links.x, links.y):
        rows = rows + move(rows)
    bit = 1
    while bit < links.nz:
        rows = rows + links.flip(rows, bit)
        bit *= 2
    return rows


def own_slot(
    clips,
    cotangent,
    clip_live,
    qkv_weight,
    q_bias,
    v_bias,
    proj_weight,
    fc1_weight,
    fc1_bias,
    fc2_weight,
    ln_gains,
    ln_biases,
    out_bias,
):
    f32 = jnp.float32
    bf16 = jnp.bfloat16
    links = Links()
    slot_count, shard_rows, width = clips.shape
    wide_count = lax.axis_size("wide")
    length = 2 * shard_rows
    block = qkv_weight.shape[0]
    heads_cols = qkv_weight.shape[2]
    hidden_here = fc1_weight.shape[1]
    q_scale = 1.0 / math.sqrt(HEAD_DIM)
    grad_scale = 1.0 / math.sqrt(wide_count * slot_count * length)
    wide_at = lax.axis_index("wide")
    t = lax.axis_index("tp")
    z_at, y_at, c_at = wide_at // 4, (wide_at // 2) % 2, wide_at % 2

    spot = jnp.arange(width)
    rel = spot // block
    kc, ky, kz = rel // (2 * links.nz), (rel // links.nz) % 2, rel % links.nz
    source = (((z_at + kz) % links.nz * 2 + (y_at ^ ky)) * 2 + (c_at ^ kc)) * block + spot % block
    order = spot[:, None] == source[None, :]
    order_b = order.astype(bf16)
    exact = partial(jnp.dot, precision=lax.Precision.HIGHEST)
    order_f = order.astype(f32)

    pick = lambda both, at: lax.dynamic_index_in_dim(both, at, 0, keepdims=False)
    halves = lambda rows, size: (rows[:, :size], rows[:, size:])
    live = pick(clip_live, t).astype(f32)
    got_x = links.x(pick(clips, 1 - t))
    qkv_cols = 3 * heads_cols
    along_one = gather_along(links, qkv_weight.reshape(block, qkv_cols))
    got_cot = links.x(after(got_x, pick(cotangent, 1 - t))[0])
    far_small = jnp.concatenate([q_bias, v_bias, fc1_bias]).reshape(-1, 128)
    far_small = links.x(far_small).reshape(-1)
    chunk_two = jnp.concatenate([fc1_weight, proj_weight.T], axis=1)
    along_two = gather_along(links, after(got_x, chunk_two)[0])
    near_one = gather_near(links, after(got_cot, along_one)[0])
    along_three = gather_along(links, after(along_two, fc2_weight.T)[0])
    w_qkv = gather_far(links, along_one, near_one)
    near_two = gather_near(links, after(near_one, along_two)[0])
    w_two = gather_far(links, along_two, near_two)
    w_fc1 = [w[:, :hidden_here] for w in w_two]
    w_proj = [w[:, hidden_here:] for w in w_two]
    near_three = gather_near(links, after(near_two, along_three)[0])
    w_fc2 = gather_far(links, along_three, near_three)

    x_b = jnp.concatenate([pick(clips, t), got_x], axis=0)
    cot_b = jnp.concatenate([pick(cotangent, t), got_cot], axis=0)
    x_rows = nn_dot(x_b, order_b)
    cot_rows = nn_dot(cot_b, order_b)
    vectors = exact(jnp.concatenate([ln_gains, ln_biases, out_bias], axis=0), order_f)
    gains, shifts, outs = vectors[0:2], vectors[2:4], vectors[4:6]
    q_biases = (q_bias, far_small[:heads_cols])
    v_biases = (v_bias, far_small[heads_cols : 2 * heads_cols])
    fc1_biases = (fc1_bias, far_small[2 * heads_cols :])

    norm_one, unit_one, inv_one = layer_norm(x_rows, gains[0], shifts[0])
    h1 = norm_one.astype(bf16)
    queries, keys, values = [], [], []
    for kx in range(2):
        projected = nn_dot(h1, w_qkv[kx])
        queries.append(((projected[:, :heads_cols] + q_biases[kx]) * q_scale).astype(bf16))
        keys.append(projected[:, heads_cols : 2 * heads_cols].astype(bf16))
        values.append((projected[:, 2 * heads_cols :] + v_biases[kx]).astype(bf16))
    query, key_rows, value_rows = (jnp.concatenate(part, axis=1) for part in (queries, keys, values))
    attn_out, lse = attend_fwd(query, key_rows, value_rows)
    attn_halves = halves(attn_out, heads_cols)
    mid_rows = (
        x_rows + nt_dot(attn_halves[0], w_proj[0]) + nt_dot(attn_halves[1], w_proj[1]) + outs[0]
    )
    norm_two, unit_two, inv_two = layer_norm(mid_rows, gains[1], shifts[1])
    h2 = norm_two.astype(bf16)
    hidden, slope = [], []
    for kx in range(2):
        pre_act = nn_dot(h2, w_fc1[kx]) + fc1_biases[kx]
        cdf_part = 0.5 * (1.0 + lax.erf(pre_act * root_half))
        hidden.append((pre_act * cdf_part).astype(bf16))
        slope.append(cdf_part + pre_act * jnp.exp(-0.5 * pre_act * pre_act) * inv_root_two_pi)
    out_grad = live * cot_rows
    e_b = out_grad.astype(bf16)
    half_rows, quarter = width // 2, width // 4

    def pieces_sent(left, right):
        return [contract_first(left[:, half_rows:], right[kx]).astype(bf16) for kx in range(2)]

    def pieces_kept(left, right, got):
        keep = {}
        for kx, ky in ((1, 1), (1, 0), (0, 1), (0, 0)):
            rows = slice(ky * quarter, (ky + 1) * quarter)
            piece = contract_first(left[:, rows], right[kx]) + got[kx][rows].astype(f32)
            keep[kx, ky] = piece.astype(bf16)
        return keep

    sent_fc2 = pieces_sent(e_b, hidden)
    got_fc2 = [links.c(piece) for piece in sent_fc2]
    (hold_e,) = after((sent_fc2, w_fc2), e_b)
    pre_grad = [nn_dot(hold_e, w_fc2[kx]) * slope[kx] for kx in range(2)]
    pre_grad_b = [rows.astype(bf16) for rows in pre_grad]
    g_fc1b = [jnp.sum(rows, axis=0) for rows in pre_grad]
    keep_fc2 = pieces_kept(*after(pre_grad_b, e_b), hidden, got_fc2)
    sent_fc1 = pieces_sent(*after(keep_fc2, h2), pre_grad_b)
    got_fc1 = [links.c(piece) for piece in sent_fc1]
    hold_du = after(sent_fc1, *pre_grad_b)
    norm_two_grad = nt_dot(hold_du[0], w_fc1[0]) + nt_dot(hold_du[1], w_fc1[1])
    mid_grad = out_grad + norm_back(norm_two_grad, unit_two, inv_two, gains[1])
    keep_fc1 = pieces_kept(*after(mid_grad, h2), pre_grad_b, got_fc1)
    da_b = after(keep_fc1, mid_grad)[0].astype(bf16)
    mixed_grad = jnp.concatenate([nn_dot(da_b, w_proj[kx]) for kx in range(2)], axis=1).astype(bf16)
    g_fc2 = scatter_keep(links, keep_fc2)
    g_fc1 = scatter_keep(links, keep_fc1)
    dq, dk, dv, q_sums, v_sums = attend_bwd(query, key_rows, value_rows, mixed_grad, lse.T)
    parts = [halves(rows, heads_cols) for rows in (dq, dk, dv)]
    one_sides = [jnp.concatenate([p[kx] for p in parts], axis=1) for kx in range(2)]

    def one_piece(rows, kx):
        return jnp.concatenate(
            [
                contract_first(h1[:, rows], one_sides[kx]),
                contract_first(da_b[:, rows], attn_halves[kx]),
            ],
            axis=1,
        )

    sent_one = [one_piece(slice(half_rows, width), kx).astype(bf16) for kx in range(2)]
    got_one = [links.c(piece) for piece in sent_one]
    hold_dp = after(sent_one, *one_sides)
    norm_one_grad = nt_dot(hold_dp[0], w_qkv[0]) + nt_dot(hold_dp[1], w_qkv[1])
    keep_one = {}
    for kx, ky in ((1, 1), (1, 0), (0, 1), (0, 0)):
        rows = slice(ky * quarter, (ky + 1) * quarter)
        keep_one[kx, ky] = (one_piece(rows, kx) + got_one[kx][rows].astype(f32)).astype(bf16)
    (hold_grad,) = after(keep_one, norm_one_grad)
    in_grad = mid_grad + norm_back(hold_grad, unit_one, inv_one, gains[0])
    g_one = scatter_keep(links, keep_one)

    (hold_mid,) = after(keep_one, mid_rows)
    mlp_sum = nt_dot(hidden[0], w_fc2[0]) + nt_dot(hidden[1], w_fc2[1])
    block_out = (live * (hold_mid + mlp_sum + outs[1])).astype(bf16)
    sums = jnp.stack(
        [
            jnp.sum(hold_grad * unit_one, axis=0),
            jnp.sum(norm_two_grad * unit_two, axis=0),
            jnp.sum(hold_grad, axis=0),
            jnp.sum(norm_two_grad, axis=0),
            jnp.sum(mid_grad, axis=0),
            jnp.sum(out_grad, axis=0),
        ]
    )
    sums = lax.dot_general(
        sums, order_f, (((1,), (1,)), ((), ())), precision=lax.Precision.HIGHEST
    )
    placed = lambda near, far: jnp.where(
        t == 0, jnp.concatenate([near, far]), jnp.concatenate([far, near])
    )
    small = [
        sums.reshape(-1),
        placed(q_sums[0, :heads_cols], q_sums[0, heads_cols:]),
        placed(v_sums[0, :heads_cols], v_sums[0, heads_cols:]),
        placed(*g_fc1b),
    ]
    small = total_over_all(links, jnp.concatenate(small).reshape(-1, 128)).reshape(-1) * grad_scale
    sums = small[: 6 * width].reshape(6, width)
    own = lambda first, size: lax.dynamic_slice_in_dim(small, first + t * size, size, 0)

    def back_home(rows_rel):
        rows = lax.dot_general(
            rows_rel.astype(bf16), order_b, (((1,), (1,)), ((), ())), preferred_element_type=f32
        ).astype(bf16)
        got = links.x(rows[shard_rows:])
        near = rows[:shard_rows]
        return jnp.where(t == 0, jnp.stack([near, got]), jnp.stack([got, near]))

    return (
        back_home(block_out),
        back_home(in_grad).astype(f32),
        g_one[:, :qkv_cols].reshape(block, 3, heads_cols) * grad_scale,
        own(6 * width, heads_cols),
        own(6 * width + 2 * heads_cols, heads_cols),
        g_one[:, qkv_cols:].T * grad_scale,
        g_fc1 * grad_scale,
        own(6 * width + 4 * heads_cols, hidden_here),
        g_fc2.T * grad_scale,
        sums[0:2],
        sums[2:4],
        sums[4:6],
    )


def solution(mesh):
    body = own_slot if fits_own_slot(mesh) else shared_slots
    return jax.shard_map(
        body,
        mesh=mesh,
        in_specs=(
            P("wide", "tp", None),
            P("wide", "tp", None),
            P("wide"),
            P("wide", None, "tp"),
            P("tp"),
            P("tp"),
            P("tp", "wide"),
            P("wide", "tp"),
            P("tp"),
            P("tp", "wide"),
            P(),
            P(),
            P(),
        ),
        out_specs=(
            P("wide", "tp", None),
            P("wide", "tp", None),
            P("wide", None, "tp"),
            P("tp"),
            P("tp"),
            P("tp", "wide"),
            P("wide", "tp"),
            P("tp"),
            P("tp", "wide"),
            P(),
            P(),
            P(),
        ),
        check_vma=False,
    )
```

```python
from functools import partial
import math

import jax
import jax.numpy as jnp
from jax import lax
from jax.experimental import pallas as pl
from jax.experimental.pallas import tpu as pltpu
from jax.sharding import PartitionSpec as P

HEAD_DIM = 64


norm_eps = 1e-06
root_half = 1.0 / math.sqrt(2.0)
inv_root_two_pi = 1.0 / math.sqrt(2.0 * math.pi)


def layer_norm(in_rows, gain_row, shift_row):
    row_mean = jnp.mean(in_rows, axis=-1, keepdims=True)
    centred = in_rows - row_mean
    spread = jnp.mean(centred * centred, axis=-1, keepdims=True)
    inverse = lax.rsqrt(spread + norm_eps)
    unit_rows = centred * inverse
    return (unit_rows * gain_row + shift_row, unit_rows, inverse)


def norm_back(grad_rows, unit_rows, inverse, gain_row):
    scaled = grad_rows * gain_row
    mean_one = jnp.mean(scaled, axis=-1, keepdims=True)
    second = jnp.mean(scaled * unit_rows, axis=-1, keepdims=True)
    return inverse * (scaled - mean_one - unit_rows * second)


def contract_last(left_op, right_op):
    return lax.dot_general(
        left_op, right_op, (((1,), (1,)), ((), ())), preferred_element_type=jnp.float32
    )


def contract_first(left_op, right_op):
    return lax.dot_general(
        left_op, right_op, (((0,), (0,)), ((), ())), preferred_element_type=jnp.float32
    )


def attend_block(query, key_rows, value_rows):
    scores = jnp.einsum("qhd,khd->hqk", query, key_rows, preferred_element_type=jnp.float32)
    row_max = jnp.max(scores, axis=-1, keepdims=True)
    weights = jnp.exp(scores - row_max)
    row_sum = jnp.sum(weights, axis=-1, keepdims=True)
    prob_rows = (weights / row_sum).astype(jnp.bfloat16)
    mixed_rows = jnp.einsum(
        "hqk,khd->qhd", prob_rows, value_rows, preferred_element_type=jnp.float32
    )
    return (mixed_rows, row_max[..., 0] + jnp.log(row_sum[..., 0]))


def attend_back(query, grad_rows, log_total, key_rows, value_rows):
    scores = jnp.einsum("qhd,khd->hqk", query, key_rows, preferred_element_type=jnp.float32)
    prob_rows = jnp.exp(scores - log_total[..., None])
    dprobs = jnp.einsum("qhd,khd->hqk", grad_rows, value_rows, preferred_element_type=jnp.float32)
    row_delta = jnp.sum(prob_rows * dprobs, axis=-1, keepdims=True)
    dscores = (prob_rows * (dprobs - row_delta)).astype(jnp.bfloat16)
    dquery = jnp.einsum("hqk,khd->qhd", dscores, key_rows, preferred_element_type=jnp.float32)
    d_keys = jnp.einsum("hqk,qhd->khd", dscores, query, preferred_element_type=jnp.float32)
    dvalues = jnp.einsum(
        "hqk,qhd->khd",
        prob_rows.astype(jnp.bfloat16),
        grad_rows,
        preferred_element_type=jnp.float32,
    )
    return (dquery, d_keys, dvalues)


def shared_slots(
    clips,
    cotangent,
    clip_live,
    qkv_weight,
    q_bias,
    v_bias,
    proj_weight,
    fc1_weight,
    fc1_bias,
    fc2_weight,
    ln_gains,
    ln_biases,
    out_bias,
):
    tp_count = lax.axis_size("tp")
    wide_count = lax.axis_size("wide")
    slot_count, shard_rows, width = clips.shape
    length = shard_rows * tp_count
    local_cols = qkv_weight.shape[2]
    heads_here = local_cols // HEAD_DIM
    hidden_here = fc1_weight.shape[1]
    q_scale = 1.0 / math.sqrt(HEAD_DIM)
    grad_scale = 1.0 / math.sqrt(wide_count * slot_count * length)
    block_rows = 512
    blocks = length // block_rows
    tp_place = lax.axis_index("tp")
    live_slots = clip_live.astype(jnp.float32)
    qv_bias = jnp.stack([q_bias, v_bias])
    own_weights = (qkv_weight, proj_weight, fc1_weight, fc2_weight)

    def one_slot(state_in, inputs):
        rows_in, cot_in, live_one = inputs
        tied_weights = lax.optimization_barrier((own_weights, rows_in))[0]
        w_qkv, w_proj, w_fc1, w_fc2 = (
            lax.all_gather(tied_weights[0], "wide", axis=0, tiled=True),
            lax.all_gather(tied_weights[1], "wide", axis=1, tiled=True),
            lax.all_gather(tied_weights[2], "wide", axis=0, tiled=True),
            lax.all_gather(tied_weights[3], "wide", axis=1, tiled=True),
        )
        x_rows = rows_in.astype(jnp.float32)
        norm_one, unit_one, inv_one = layer_norm(x_rows, ln_gains[0], ln_biases[0])
        h1_full = lax.all_gather(norm_one.astype(jnp.bfloat16), "tp", axis=0, tiled=True)
        qkv_flat = w_qkv.reshape(width, 3 * local_cols)
        projected = jnp.dot(h1_full, qkv_flat, preferred_element_type=jnp.float32).reshape(
            length, 3, local_cols
        )
        query = (
            ((projected[:, 0] + qv_bias[0]) * q_scale)
            .astype(jnp.bfloat16)
            .reshape(length, heads_here, HEAD_DIM)
        )
        key_rows = projected[:, 1].astype(jnp.bfloat16).reshape(length, heads_here, HEAD_DIM)
        value_rows = (
            (projected[:, 2] + qv_bias[1])
            .astype(jnp.bfloat16)
            .reshape(length, heads_here, HEAD_DIM)
        )
        query_blocks = query.reshape(blocks, block_rows, heads_here, HEAD_DIM)
        mixed_blocks, log_totals = lax.map(
            partial(attend_block, key_rows=key_rows, value_rows=value_rows), query_blocks
        )
        attn_out = mixed_blocks.reshape(length, local_cols).astype(jnp.bfloat16)
        attn_sum = lax.psum_scatter(
            jnp.dot(attn_out, w_proj, preferred_element_type=jnp.float32),
            "tp",
            scatter_dimension=0,
            tiled=True,
        )
        mid_rows = x_rows + attn_sum + out_bias[0]
        norm_two, unit_two, inv_two = layer_norm(mid_rows, ln_gains[1], ln_biases[1])
        h2_full = lax.all_gather(norm_two.astype(jnp.bfloat16), "tp", axis=0, tiled=True)
        pre_act = jnp.dot(h2_full, w_fc1, preferred_element_type=jnp.float32) + fc1_bias
        cdf_part = 0.5 * (1.0 + lax.erf(pre_act * root_half))
        hidden = (pre_act * cdf_part).astype(jnp.bfloat16)
        mlp_sum = lax.psum_scatter(
            jnp.dot(hidden, w_fc2, preferred_element_type=jnp.float32).astype(jnp.bfloat16),
            "tp",
            scatter_dimension=0,
            tiled=True,
        ).astype(jnp.float32)
        block_out = (live_one * (mid_rows + mlp_sum + out_bias[1])).astype(jnp.bfloat16)
        out_grad = live_one * cot_in.astype(jnp.float32)
        out_full = lax.all_gather(out_grad.astype(jnp.bfloat16), "tp", axis=0, tiled=True)
        g_fc2 = contract_first(hidden, out_full)
        act_grad = contract_last(out_full, w_fc2)
        slope = cdf_part + pre_act * jnp.exp(-0.5 * pre_act * pre_act) * inv_root_two_pi
        pre_grad = act_grad * slope
        pre_grad_b = pre_grad.astype(jnp.bfloat16)
        g_fc1 = contract_first(h2_full, pre_grad_b)
        g_fc1b = jnp.sum(pre_grad, axis=0)
        norm_two_grad = lax.psum_scatter(
            contract_last(pre_grad_b, w_fc1), "tp", scatter_dimension=0, tiled=True
        )
        mid_grad = out_grad + norm_back(norm_two_grad, unit_two, inv_two, ln_gains[1])
        attn_full = lax.all_gather(mid_grad.astype(jnp.bfloat16), "tp", axis=0, tiled=True)
        g_proj = contract_first(attn_out, attn_full)
        mixed_grad = (
            contract_last(attn_full, w_proj)
            .astype(jnp.bfloat16)
            .reshape(blocks, block_rows, heads_here, HEAD_DIM)
        )

        def back_block(block_state, pieces):
            query_b, grad_b, lse_b = pieces
            d_query, d_keys, d_values = attend_back(query_b, grad_b, lse_b, key_rows, value_rows)
            return ((block_state[0] + d_keys, block_state[1] + d_values), d_query)

        empty_kv = jnp.zeros((length, heads_here, HEAD_DIM), jnp.float32)
        (key_grad, value_grad), query_grad = lax.scan(
            back_block, (empty_kv, empty_kv), (query_blocks, mixed_grad, log_totals)
        )
        query_grad = query_grad.reshape(length, local_cols) * q_scale
        key_grad = key_grad.reshape(length, local_cols)
        value_grad = value_grad.reshape(length, local_cols)
        g_qvb = jnp.stack([jnp.sum(query_grad, axis=0), jnp.sum(value_grad, axis=0)])
        proj_grads = (
            jnp.stack([query_grad, key_grad, value_grad], axis=1)
            .astype(jnp.bfloat16)
            .reshape(length, 3 * local_cols)
        )
        g_qkv = contract_first(h1_full, proj_grads).reshape(width, 3, local_cols)
        norm_one_grad = lax.psum_scatter(
            contract_last(proj_grads, qkv_flat).astype(jnp.bfloat16),
            "tp",
            scatter_dimension=0,
            tiled=True,
        ).astype(jnp.float32)
        in_grad = mid_grad + norm_back(norm_one_grad, unit_one, inv_one, ln_gains[0])
        gain_part = jnp.stack(
            [jnp.sum(norm_one_grad * unit_one, axis=0), jnp.sum(norm_two_grad * unit_two, axis=0)]
        )
        shift_part = jnp.stack([jnp.sum(norm_one_grad, axis=0), jnp.sum(norm_two_grad, axis=0)])
        bias_part = jnp.stack([jnp.sum(mid_grad, axis=0), jnp.sum(out_grad, axis=0)])
        summed = (
            lax.psum_scatter(
                g_qkv.astype(jnp.bfloat16), "wide", scatter_dimension=0, tiled=True
            ).astype(jnp.float32),
            lax.psum_scatter(
                g_proj.astype(jnp.bfloat16), "wide", scatter_dimension=1, tiled=True
            ).astype(jnp.float32),
            lax.psum_scatter(
                g_fc1.astype(jnp.bfloat16), "wide", scatter_dimension=0, tiled=True
            ).astype(jnp.float32),
            lax.psum_scatter(
                g_fc2.astype(jnp.bfloat16), "wide", scatter_dimension=1, tiled=True
            ).astype(jnp.float32),
        )
        weight_acc = jax.tree.map(jnp.add, state_in[0], summed)
        vector_acc = jax.tree.map(
            jnp.add, state_in[1], (gain_part, shift_part, bias_part, g_qvb, g_fc1b)
        )
        return ((weight_acc, vector_acc), (block_out, in_grad))

    weight_zero = tuple((jnp.zeros(shard_in.shape, jnp.float32) for shard_in in own_weights))
    vector_zero = (
        jnp.zeros((2, width), jnp.float32),
        jnp.zeros((2, width), jnp.float32),
        jnp.zeros((2, width), jnp.float32),
        jnp.zeros((2, local_cols), jnp.float32),
        jnp.zeros((hidden_here,), jnp.float32),
    )
    (weight_sums, vector_acc), (block_out, clips_grad) = lax.scan(
        one_slot, (weight_zero, vector_zero), (clips, cotangent, live_slots)
    )
    gain_acc, shift_acc, bias_acc, qvb_acc, fc1b_acc = vector_acc
    qvb_pad = lax.dynamic_update_slice(
        jnp.zeros((2, width), jnp.float32), qvb_acc, (0, tp_place * local_cols)
    )
    fc1b_pad = lax.dynamic_update_slice(
        jnp.zeros((hidden_here * tp_count,), jnp.float32), fc1b_acc, (tp_place * hidden_here,)
    )
    gain_sum, shift_sum, bias_sum, qvb_sum, fc1b_sum = lax.psum(
        (gain_acc, shift_acc, bias_acc, qvb_pad, fc1b_pad), ("wide", "tp")
    )
    qvb_own = lax.dynamic_slice_in_dim(qvb_sum, tp_place * local_cols, local_cols, 1)
    fc1b_own = lax.dynamic_slice_in_dim(fc1b_sum, tp_place * hidden_here, hidden_here, 0)
    return (
        block_out,
        clips_grad,
        weight_sums[0] * grad_scale,
        qvb_own[0] * grad_scale,
        qvb_own[1] * grad_scale,
        weight_sums[1] * grad_scale,
        weight_sums[2] * grad_scale,
        fc1b_own * grad_scale,
        weight_sums[3] * grad_scale,
        gain_sum * grad_scale,
        shift_sum * grad_scale,
        bias_sum * grad_scale,
    )


AXES = ("wide", "tp")
PAIR = 128
TILE = 512
VMEM_MIB = 60
WIDE = 1024
bf16 = jnp.bfloat16
f32 = jnp.float32


def fits_own_slot(mesh):
    return mesh.shape["tp"] == 2 and mesh.shape["wide"] % 4 == 0


def nt_dot(left_op, right_op):
    return lax.dot_general(
        left_op, right_op, (((1,), (1,)), ((), ())), preferred_element_type=f32
    )


def nn_dot(left_op, right_op):
    return lax.dot_general(
        left_op, right_op, (((1,), (0,)), ((), ())), preferred_element_type=f32
    )


def kernel_call(body, name, grid, in_specs, out_specs, out_shape, scratch=(), scalars=0, vmem=VMEM_MIB):
    return pl.pallas_call(
        body,
        grid_spec=pltpu.PrefetchScalarGridSpec(
            num_scalar_prefetch=scalars,
            grid=grid,
            in_specs=in_specs,
            out_specs=out_specs,
            scratch_shapes=list(scratch),
        ),
        out_shape=out_shape,
        compiler_params=pltpu.CompilerParams(vmem_limit_bytes=vmem * 1024 * 1024),
        cost_estimate=pl.CostEstimate(flops=1, bytes_accessed=1, transcendentals=0),
        name=name,
    )


def whole(shape):
    return pl.BlockSpec(shape, lambda *at: (0,) * len(shape))


def array(*shape, dtype=bf16):
    return jax.ShapeDtypeStruct(shape, dtype)


def norm_stats(rows):
    row_mean = jnp.mean(rows, axis=-1, keepdims=True)
    centred = rows - row_mean
    spread = jnp.mean(centred * centred, axis=-1, keepdims=True)
    inverse = lax.rsqrt(spread + norm_eps)
    return centred * inverse, inverse


NEAR = (0, 2, 5, 7)
FAR = (1, 3, 4, 6, 8, 9)


class Pieces:
    def __init__(self, pieces, columns, first=0):
        self.pieces, self.columns, self.first = pieces, columns, first
        self.args = list(pieces)
        self.specs = [pl.BlockSpec(memory_space=pl.ANY)] * len(pieces)
        rows = sum(pieces[i].shape[0] for i in NEAR)
        self.scratch = [
            pltpu.VMEM((2, rows, columns), bf16),
            pltpu.SemaphoreType.DMA((len(pieces),)),
        ]

    def copies(self, refs, side, w_ref, sems):
        at, found = 0, []
        for index in FAR if side else NEAR:
            rows = self.pieces[index].shape[0]
            found.append(
                pltpu.make_async_copy(
                    refs[index].at[:, pl.ds(self.first, self.columns)],
                    w_ref.at[side, pl.ds(at, rows)],
                    sems.at[index],
                )
            )
            at += rows
        return found

    def start(self, refs, w_ref, sems):
        for side in range(2):
            for copy in self.copies(refs, side, w_ref, sems):
                copy.start()

    def wait(self, refs, side, w_ref, sems):
        for copy in self.copies(refs, side, w_ref, sems):
            copy.wait()


class Gathered:
    def __init__(self, weights):
        self.wide, _, self.rows, self.columns = weights.shape
        self.args = [weights]
        self.specs = [pl.BlockSpec(memory_space=pl.ANY)]
        self.scratch = [
            pltpu.VMEM((2, self.wide * self.rows, self.columns), bf16),
            pltpu.SemaphoreType.DMA((2, self.wide)),
        ]

    def copies(self, refs, side, w_ref, sems):
        place_ref, all_ref = refs
        return [
            pltpu.make_async_copy(
                all_ref.at[place_ref[1 + j], place_ref[0] ^ side],
                w_ref.at[side, pl.ds(j * self.rows, self.rows)],
                sems.at[side, j],
            )
            for j in range(self.wide)
        ]

    start = Pieces.start
    wait = Pieces.wait


def enter_kernel(own_ref, got_ref, order_ref, gain_ref, shift_ref, x_ref, h_ref, ht_ref):
    half = own_ref.shape[0]
    for part, ref in enumerate((own_ref, got_ref)):
        rows = nn_dot(ref[...], order_ref[...])
        here = pl.ds(part * half, half)
        x_ref[here, :] = rows.astype(bf16)
        unit, _ = norm_stats(rows)
        normed = (unit * gain_ref[...] + shift_ref[...]).astype(bf16)
        h_ref[here, :] = normed
        ht_ref[:, here] = normed.T


def enter(own, got, order_b, gain, shift):
    half, width = own.shape
    length = 2 * half
    return kernel_call(
        enter_kernel,
        "enter",
        (1,),
        [whole((half, width))] * 2 + [whole((width, width))] + [whole((1, width))] * 2,
        [whole((length, width))] * 2 + [whole((width, length))],
        [array(length, width)] * 2 + [array(width, length)],
    )(own, got, order_b, gain, shift)


def cot_kernel(own_ref, got_ref, order_ref, live_ref, e_ref, et_ref):
    half = own_ref.shape[0]
    for part, ref in enumerate((own_ref, got_ref)):
        rows = (live_ref[...] * nn_dot(ref[...], order_ref[...])).astype(bf16)
        here = pl.ds(part * half, half)
        e_ref[here, :] = rows
        et_ref[:, here] = rows.T


def enter_cot(own, got, order_b, live):
    half, width = own.shape
    length = 2 * half
    return kernel_call(
        cot_kernel,
        "enter_cot",
        (1,),
        [whole((half, width))] * 2 + [whole((width, width)), whole((1, width))],
        [whole((length, width)), whole((width, length))],
        [array(length, width), array(width, length)],
    )(own, got, order_b, live)


def project(h, pieces, biases):
    length, width = h.shape
    cols = pieces[0].shape[1]
    each = cols // 3
    q_scale = 1.0 / math.sqrt(HEAD_DIM)
    load = Pieces(pieces, cols)

    def body(h_ref, bias_ref, *refs):
        refs, out_ref, w_ref, sems = refs[:-3], *refs[-3:]
        pl.when(pl.program_id(0) == 0)(lambda: load.start(refs, w_ref, sems))
        for side in range(2):

            @pl.when(pl.program_id(0) == side)
            def _():
                load.wait(refs, side, w_ref, sems)
                acc = nn_dot(h_ref[...], w_ref[side]) + bias_ref[0]
                out_ref[0] = (acc[:, :each] * q_scale).astype(bf16)
                out_ref[1] = acc[:, each : 2 * each].astype(bf16)
                out_ref[2] = acc[:, 2 * each :].astype(bf16)

    return kernel_call(
        body,
        "project",
        (2,),
        [whole((length, width)), pl.BlockSpec((1, 1, cols), lambda s: (s, 0, 0))] + load.specs,
        pl.BlockSpec((3, length, each), lambda s: (0, 0, s)),
        array(3, length, width),
        load.scratch,
        vmem=VMEM_MIB,
    )(h, biases, *load.args)


def attend_kernel(q_ref, k_ref, v_ref, o_ref, lse_ref):
    pair = pl.program_id(0)
    rows = q_ref.shape[1]
    lanes = lax.broadcasted_iota(jnp.int32, (rows, PAIR), 1)
    keys = k_ref[0]
    values = v_ref[0]
    total = jnp.zeros((rows, PAIR), f32)
    for half in range(2):
        mask = (lanes // HEAD_DIM) == half
        query = jnp.where(mask, q_ref[0], jnp.zeros_like(keys))
        scores = nt_dot(query, keys)
        row_max = jnp.max(scores, axis=-1, keepdims=True)
        weights = jnp.exp(scores - row_max)
        row_sum = jnp.sum(weights, axis=-1, keepdims=True)
        probs = (weights * (1.0 / row_sum)).astype(bf16)
        mixed = nn_dot(probs, values)
        total = jnp.where(mask, mixed, total)
        lse = row_max + jnp.log(row_sum)
        lse_ref[...] = jnp.where(lanes == 2 * pair + half, lse, lse_ref[...])
    o_ref[...] = total.astype(bf16)


def head_spec(length, index):
    return pl.BlockSpec((1, length, PAIR), lambda i: (index, 0, i))


def attend_fwd(qkv):
    _, length, width = qkv.shape
    return kernel_call(
        attend_kernel,
        "attend_fwd",
        (width // PAIR,),
        [head_spec(length, j) for j in range(3)],
        [pl.BlockSpec((length, PAIR), lambda i: (0, i)), whole((length, PAIR))],
        [array(length, width), array(length, PAIR, dtype=f32)],
    )(qkv, qkv, qkv)


def join_heads(attn, x, pieces, first, bias, gain, shift):
    length, width = x.shape
    load = Pieces(pieces, TILE, first)

    def body(attn_ref, x_ref, bias_ref, gain_ref, shift_ref, *refs):
        refs, (y_ref, h_ref, ht_ref, w_ref, sems) = refs[:-5], refs[-5:]
        load.start(refs, w_ref, sems)
        load.wait(refs, 0, w_ref, sems)
        load.wait(refs, 1, w_ref, sems)
        half = length // 2
        for part in range(2):
            here = pl.ds(part * half, half)
            rows = nt_dot(attn_ref[here, :TILE], w_ref[0]) + nt_dot(attn_ref[here, TILE:], w_ref[1])
            rows = x_ref[here, :].astype(f32) + rows + bias_ref[...]
            y_ref[here, :] = rows
            unit, _ = norm_stats(rows)
            normed = (unit * gain_ref[...] + shift_ref[...]).astype(bf16)
            h_ref[here, :] = normed
            ht_ref[:, here] = normed.T

    return kernel_call(
        body,
        "join_heads",
        (1,),
        [whole((length, width))] * 2 + [whole((1, width))] * 3 + load.specs,
        [whole((length, width))] * 2 + [whole((width, length))],
        [array(length, width, dtype=f32), array(length, width), array(width, length)],
        load.scratch,
    )(attn, x, bias, gain, shift, *load.args)


def expand(h, pieces, bias, hidden):
    length, width = h.shape
    per = hidden // WIDE
    load = Pieces(pieces, hidden)

    def body(h_ref, bias_ref, *refs):
        refs, (g_ref, slope_ref, w_ref, sems) = refs[:-4], refs[-4:]
        step = pl.program_id(0)
        pl.when(step == 0)(lambda: load.start(refs, w_ref, sems))
        for side in range(2):
            pl.when(step == side * per)(partial(load.wait, refs, side, w_ref, sems))
        at = pl.ds(pl.multiple_of(step % per * WIDE, WIDE), WIDE)
        pre = nn_dot(h_ref[...], w_ref[step // per, :, at]) + bias_ref[...]
        cdf = 0.5 * (1.0 + lax.erf(pre * root_half))
        g_ref[...] = (pre * cdf).astype(bf16)
        density = jnp.exp(-0.5 * pre * pre) * inv_root_two_pi
        slope_ref[...] = (cdf + pre * density).astype(bf16)

    block = pl.BlockSpec((length, WIDE), lambda s: (0, s))
    return kernel_call(
        body,
        "expand",
        (2 * per,),
        [whole((length, width)), pl.BlockSpec((1, WIDE), lambda s: (0, s))] + load.specs,
        [block] * 2,
        [array(length, 2 * hidden)] * 2,
        load.scratch,
        vmem=VMEM_MIB,
    )(h, bias, *load.args)


def hidden_back(e, slope, weights, place):
    length, width = e.shape
    hidden = weights.shape[3]
    per = hidden // WIDE
    load = Gathered(weights)

    def body(place_ref, e_ref, slope_ref, all_ref, du_ref, sum_ref, w_ref, sems):
        refs = (place_ref, all_ref)
        step = pl.program_id(0)
        pl.when(step == 0)(lambda: load.start(refs, w_ref, sems))
        for side in range(2):
            pl.when(step == side * per)(partial(load.wait, refs, side, w_ref, sems))
        at = pl.ds(pl.multiple_of(step % per * WIDE, WIDE), WIDE)
        du = nn_dot(e_ref[...], w_ref[step // per, :, at]) * slope_ref[...].astype(f32)
        du_ref[...] = du.astype(bf16)
        sum_ref[...] = jnp.sum(du, axis=0, keepdims=True)

    block = pl.BlockSpec((length, WIDE), lambda s, *_: (0, s))
    row = pl.BlockSpec((1, WIDE), lambda s, *_: (0, s))
    return kernel_call(
        body,
        "hidden_back",
        (2 * per,),
        [whole((length, width)), block] + load.specs,
        [block, row],
        [array(length, 2 * hidden), array(1, 2 * hidden, dtype=f32)],
        load.scratch,
        scalars=1,
        vmem=VMEM_MIB,
    )(place, e, slope, weights)


def heads_back(da, pieces, first):
    length, width = da.shape
    load = Pieces(pieces, TILE, first)

    def body(da_ref, *refs):
        refs, (out_ref, w_ref, sems) = refs[:-3], refs[-3:]
        load.start(refs, w_ref, sems)
        for side in range(2):
            load.wait(refs, side, w_ref, sems)
            out_ref[:, pl.ds(side * TILE, TILE)] = nn_dot(da_ref[...], w_ref[side]).astype(bf16)

    return kernel_call(
        body,
        "heads_back",
        (1,),
        [whole((length, width))] + load.specs,
        whole((length, 2 * TILE)),
        array(length, 2 * TILE),
        load.scratch,
        vmem=VMEM_MIB,
    )(da, *load.args)


def contract_back(rows, rows_specs, left_of, load, extras, extra_specs, finish, name, outs, place=()):
    count = len(extras)
    length, width = extras[0].shape

    def body(*refs):
        place_refs, refs = refs[: len(place)], refs[len(place) :]
        rows_refs, refs = refs[: len(rows)], refs[len(rows) :]
        extra_refs, refs = refs[:count], refs[count:]
        w_refs, refs = place_refs + refs[: len(load.args)], refs[len(load.args) :]
        out_refs, (w_ref, sems, acc_ref) = refs[:-3], refs[-3:]

        @pl.when(pl.program_id(0) == 0)
        def _():
            load.start(w_refs, w_ref, sems)
            load.wait(w_refs, 0, w_ref, sems)
            acc_ref[...] = nt_dot(left_of(rows_refs, 0), w_ref[0])

        @pl.when(pl.program_id(0) == 1)
        def _():
            load.wait(w_refs, 1, w_ref, sems)
            acc_ref[...] += nt_dot(left_of(rows_refs, 1), w_ref[1])
            finish(acc_ref, extra_refs, out_refs)

    return kernel_call(
        body,
        name,
        (2,),
        rows_specs + extra_specs + load.specs,
        [whole(o.shape) for o in outs],
        outs,
        load.scratch + [pltpu.VMEM((length, width), f32)],
        scalars=len(place),
        vmem=VMEM_MIB,
    )(*place, *rows, *extras, *load.args)


def to_home(rows, order_ref):
    return nt_dot(rows.astype(bf16), order_ref[...]).astype(bf16)


def layer_out(hidden, weights, place, y, bias, live, order_b):
    length, width = y.shape
    half = length // 2
    columns = weights.shape[3]

    def finish(acc_ref, ins, outs):
        y_ref, bias_ref, live_ref, order_ref = ins
        for part in range(2):
            here = pl.ds(part * half, half)
            rows = live_ref[...] * (y_ref[here, :] + acc_ref[here, :] + bias_ref[...])
            outs[part][...] = to_home(rows, order_ref)

    return contract_back(
        [hidden],
        [pl.BlockSpec((length, columns), lambda s, *_: (0, s))],
        lambda refs, side: refs[0][...],
        Gathered(weights),
        (y, bias, live, order_b),
        [whole((length, width)), whole((1, width)), whole((1, width)), whole((width, width))],
        finish,
        "layer_out",
        [array(half, width)] * 2,
        (place,),
    )


def second_back(du, pieces, hidden, y, e, gain):
    length, width = y.shape
    half = length // 2

    def finish(acc_ref, ins, outs):
        y_ref, e_ref, gain_ref = ins
        mid_ref, da_ref, dat_ref, sum_ref = outs
        sums = [jnp.zeros((1, width), f32)] * 4
        for part in range(2):
            here = pl.ds(part * half, half)
            unit, inverse = norm_stats(y_ref[here, :])
            grad = acc_ref[here, :]
            e_rows = e_ref[here, :].astype(f32)
            mid = e_rows + norm_back(grad, unit, inverse, gain_ref[...])
            mid_ref[here, :] = mid
            mid_b = mid.astype(bf16)
            da_ref[here, :] = mid_b
            dat_ref[:, here] = mid_b.T
            terms = (grad * unit, grad, mid, e_rows)
            sums = [s + jnp.sum(term, axis=0, keepdims=True) for s, term in zip(sums, terms)]
        sum_ref[...] = jnp.concatenate(sums, axis=0)

    return contract_back(
        [du],
        [pl.BlockSpec((length, hidden), lambda s: (0, s))],
        lambda refs, side: refs[0][...],
        Pieces(pieces, hidden),
        (y, e, gain),
        [whole((length, width)), whole((length, width)), whole((1, width))],
        finish,
        "second_back",
        [
            array(length, width, dtype=f32),
            array(length, width),
            array(width, length),
            array(4, width, dtype=f32),
        ],
    )


def first_back(dps, pieces, x, mid, gain, order_b):
    length, width = x.shape
    half = length // 2

    def finish(acc_ref, ins, outs):
        x_ref, mid_ref, gain_ref, order_ref = ins
        sum_ref = outs[2]
        sums = [jnp.zeros((1, width), f32)] * 2
        for part in range(2):
            here = pl.ds(part * half, half)
            unit, inverse = norm_stats(x_ref[here, :].astype(f32))
            grad = acc_ref[here, :]
            rows = mid_ref[here, :] + norm_back(grad, unit, inverse, gain_ref[...])
            outs[part][...] = to_home(rows, order_ref)
            terms = (grad * unit, grad)
            sums = [s + jnp.sum(term, axis=0, keepdims=True) for s, term in zip(sums, terms)]
        sum_ref[...] = jnp.concatenate(sums, axis=0)

    return contract_back(
        dps,
        [whole(dps[0].shape)] * 2,
        lambda refs, side: jnp.concatenate([refs[side][j] for j in range(3)], axis=1),
        Pieces(pieces, pieces[0].shape[1]),
        (x, mid, gain, order_b),
        [whole((length, width)), whole((length, width)), whole((1, width)), whole((width, width))],
        finish,
        "first_back",
        [array(half, width)] * 2 + [array(2, width, dtype=f32)],
    )


def attend_back_kernel(first, q_ref, k_ref, v_ref, g_ref, lse_ref, dp_ref, qs_ref, vs_ref):
    pair = first + pl.program_id(0)
    rows = q_ref.shape[1]
    lanes = lax.broadcasted_iota(jnp.int32, (rows, PAIR), 1)
    sub = lax.broadcasted_iota(jnp.int32, (PAIR, rows), 0)
    query = q_ref[0]
    keys = k_ref[0]
    values = v_ref[0]
    grads = g_ref[...]
    blank = jnp.zeros_like(keys)
    keys_t = keys.T
    dq_t = jnp.zeros((PAIR, rows), f32)
    dk = jnp.zeros((rows, PAIR), f32)
    dv = jnp.zeros((rows, PAIR), f32)
    for half in range(2):
        mask = (lanes // HEAD_DIM) == half
        scores_t = nt_dot(jnp.where(mask, keys, blank), query)
        lse = lse_ref[pl.ds(2 * pair + half, 1), :]
        probs_t = jnp.exp(scores_t - lse)
        dprobs_t = nt_dot(jnp.where(mask, values, blank), grads)
        delta = jnp.sum(probs_t * dprobs_t, axis=0, keepdims=True)
        ds_t = (probs_t * (dprobs_t - delta)).astype(bf16)
        dv = jnp.where(mask, nn_dot(probs_t.astype(bf16), grads), dv)
        dk = jnp.where(mask, nn_dot(ds_t, query), dk)
        dq_t = jnp.where((sub // HEAD_DIM) == half, nn_dot(keys_t, ds_t), dq_t)
    dq = dq_t.T * (1.0 / math.sqrt(HEAD_DIM))
    dp_ref[0] = dq.astype(bf16)
    dp_ref[1] = dk.astype(bf16)
    dp_ref[2] = dv.astype(bf16)
    qs_ref[...] = jnp.sum(dq, axis=0, keepdims=True)
    vs_ref[...] = jnp.sum(dv, axis=0, keepdims=True)


def attend_bwd(qkv, grads, lse_rows, side):
    _, length, width = qkv.shape
    count = width // PAIR // 2
    first = side * count
    head = lambda j: pl.BlockSpec((1, length, PAIR), lambda i: (j, 0, first + i))
    row = pl.BlockSpec((1, PAIR), lambda i: (0, i))
    sums = array(1, width // 2, dtype=f32)
    return kernel_call(
        partial(attend_back_kernel, first),
        "attend_bwd",
        (count,),
        [head(j) for j in range(3)]
        + [pl.BlockSpec((length, PAIR), lambda i: (0, first + i)), whole((PAIR, length))],
        [pl.BlockSpec((3, length, PAIR), lambda i: (0, 0, i)), row, row],
        [array(3, length, width // 2), sums, sums],
    )(qkv, qkv, qkv, grads, lse_rows)


def grad_call(args, specs, terms, cuts, name, steps):
    count = len(args)
    kinds, choose, terms = terms

    def body(*refs):
        def run(kind):
            left, right = terms(refs[:count], kind)
            acc = nn_dot(left, right).astype(bf16)
            for ref, ranges in zip(refs[count:], cuts):
                at = 0
                for start, stop in ranges:
                    ref[pl.ds(at, stop - start), :] = acc[start:stop]
                    at += stop - start

        for kind in range(kinds):
            if kinds == 1:
                run(kind)
            else:
                pl.when(choose(pl.program_id(0)) == kind)(partial(run, kind))

    sizes = [sum(b - a for a, b in ranges) for ranges in cuts]
    return kernel_call(
        body,
        name,
        (steps,),
        specs,
        [pl.BlockSpec((size, TILE), lambda s: (0, s)) for size in sizes],
        [array(size, steps * TILE) for size in sizes],
    )(*args)


def add_mid_kernel(k01_ref, rx_ref, k10_ref, ry_ref, y_ref, x_ref):
    half = k01_ref.shape[0]
    y_ref[...] = (k01_ref[...].astype(f32) + rx_ref[pl.ds(half, half), :].astype(f32)).astype(bf16)
    x_ref[...] = (k10_ref[...].astype(f32) + ry_ref[pl.ds(0, half), :].astype(f32)).astype(bf16)


def add_last_kernel(k00_ref, rx_ref, ry_ref, y2_ref, x2_ref, out_ref):
    half = y2_ref.shape[0]
    top, low = pl.ds(0, half), pl.ds(half, half)
    near = (rx_ref[top, :], y2_ref[...]), (ry_ref[low, :], x2_ref[...])
    for here, (one, two) in zip((top, low), near):
        total = k00_ref[here, :].astype(f32) + one.astype(f32) + two.astype(f32)
        out_ref[here, :] = total.astype(bf16)


def small_call(body, name, args, shapes):
    out_specs = [whole(s.shape) for s in shapes]
    return kernel_call(body, name, (1,), [whole(a.shape) for a in args], out_specs, shapes)(*args)


class Links:
    def __init__(self):
        self.nz = lax.axis_size("wide") // 4
        self.across = self.table(lambda z, y, c, x: (z, y, c, 1 - x))
        self.beside = self.table(lambda z, y, c, x: (z, 1 - y, c, x))
        self.twin = self.table(lambda z, y, c, x: (z, y, 1 - c, x))

    def table(self, source):
        pairs = []
        for z in range(self.nz):
            for y in range(2):
                for c in range(2):
                    for x in range(2):
                        zs, ys, cs, xs = source(z, y, c, x)
                        pairs.append(
                            (((zs * 2 + ys) * 2 + cs) * 2 + xs, ((z * 2 + y) * 2 + c) * 2 + x)
                        )
        return pairs

    def from_z(self, rows, step):
        shift = self.table(lambda z, y, c, x: ((z + step) % self.nz, y, c, x))
        return lax.ppermute(rows, AXES, shift)

    def z_groups(self):
        rest = [(y, c, x) for y in range(2) for c in range(2) for x in range(2)]
        return [
            [((z * 2 + y) * 2 + c) * 2 + x for z in range(self.nz)] for y, c, x in rest
        ]

    def z_sum_apart(self, rows):
        return lax.psum_scatter(
            rows, AXES, scatter_dimension=0, tiled=True, axis_index_groups=self.z_groups()
        )

    def z_sum(self, rows):
        got = lax.all_to_all(rows, AXES, 0, 0, tiled=True, axis_index_groups=self.z_groups())
        return got.reshape(self.nz, -1, rows.shape[1])

    def z_all(self, rows):
        return lax.all_gather(
            rows, AXES, axis=0, tiled=True, axis_index_groups=self.z_groups()
        )

    def x(self, rows):
        return lax.ppermute(rows, AXES, self.across)

    def y(self, rows):
        return lax.ppermute(rows, AXES, self.beside)

    def c(self, rows):
        return lax.ppermute(rows, AXES, self.twin)

    def flip(self, rows, bit):
        swap = self.table(lambda z, y, c, x: (z ^ bit, y, c, x))
        return lax.ppermute(rows, AXES, swap)


def after(done, *values):
    out = lax.optimization_barrier((values, done))[0]
    return out if len(values) > 1 else out[0]


def total_over_all(links, rows):
    for move in (links.c, links.x, links.y):
        rows = rows + move(rows)
    bit = 1
    while bit < links.nz:
        rows = rows + links.flip(rows, bit)
        bit *= 2
    return rows


def start_far(links, near):
    by_x, by_y = near
    half = by_x.shape[0] // 2
    return links.x(by_y[:half]), links.y(by_x[half:])


class Home:
    def __init__(self, links):
        self.links = links

    def first(self, far, near):
        x_first, y_low_far, self.k10_low = far
        self.k00, self.k01_top, y_low_near = near
        self.x_got = self.links.x(x_first)
        self.y_got = self.links.y(jnp.concatenate([y_low_far, y_low_near], axis=0))

    def middle(self):
        half = self.k01_top.shape[0]
        args = (self.k01_top, self.x_got, self.k10_low, self.y_got)
        shape = array(*self.k01_top.shape)
        out_y, out_x = small_call(add_mid_kernel, "add_mid", args, [shape, shape])
        return out_y, out_x

    def second(self, out_y, out_x):
        self.y_last, self.x_last = self.links.y(out_y), self.links.x(out_x)

    def last(self, done, apart):
        y_last, x_last = after(done, self.y_last, self.x_last)
        args = (self.k00, self.x_got, self.y_got, y_last, x_last)
        (total,) = small_call(add_last_kernel, "add_last", args, [array(*self.k00.shape)])
        self.home = self.links.z_sum_apart(total)[None] if apart else self.links.z_sum(total)
        return total

    def value(self, done, scale):
        return jnp.sum(after(done, self.home).astype(f32), axis=0) * scale


def own_slot(
    clips,
    cotangent,
    clip_live,
    qkv_weight,
    q_bias,
    v_bias,
    proj_weight,
    fc1_weight,
    fc1_bias,
    fc2_weight,
    ln_gains,
    ln_biases,
    out_bias,
):
    links = Links()
    slot_count, shard_rows, width = clips.shape
    wide_count = lax.axis_size("wide")
    length = 2 * shard_rows
    block = qkv_weight.shape[0]
    heads_cols = qkv_weight.shape[2]
    hidden_here = fc1_weight.shape[1]
    grad_scale = 1.0 / math.sqrt(wide_count * slot_count * length)
    wide_at = lax.axis_index("wide")
    t = lax.axis_index("tp")
    z_at, y_at, c_at = wide_at // 4, (wide_at // 2) % 2, wide_at % 2
    qkv_cols = 3 * heads_cols
    pick = lambda both, at: lax.dynamic_index_in_dim(both, at, 0, keepdims=False)
    row = lambda vector: vector.reshape(1, -1)

    two_shard = jnp.concatenate([fc1_weight, proj_weight.T], axis=1)
    along_two = links.z_all(two_shard)
    q_shard = qkv_weight.reshape(block, qkv_cols)
    steps_one = [links.from_z(q_shard, k) for k in range(1, links.nz)]
    got_rows = links.x(jnp.concatenate([pick(clips, 1 - t), pick(cotangent, 1 - t)], axis=0))
    far_small = jnp.concatenate([q_bias, v_bias, fc1_bias]).reshape(-1, 128)
    far_small = links.x(far_small).reshape(-1)

    spot = jnp.arange(width)
    rel = spot // block
    kc, ky, kz = rel // (2 * links.nz), (rel // links.nz) % 2, rel % links.nz
    home = (kz * 2 + (y_at ^ ky)) * 2 + (c_at ^ kc)
    order = spot[:, None] == (home * block + spot % block)[None, :]
    place = jnp.concatenate([t.reshape(1), home[::block]]).astype(jnp.int32)
    order_b = order.astype(bf16)
    order_f = order.astype(f32)
    vectors = jnp.dot(
        jnp.concatenate([ln_gains, ln_biases, out_bias], axis=0),
        order_f,
        precision=lax.Precision.HIGHEST,
    )
    gains, shifts, outs = (
        (vectors[2 * i : 2 * i + 1], vectors[2 * i + 1 : 2 * i + 2]) for i in range(3)
    )
    live = jnp.full((1, width), pick(clip_live, t).astype(f32))
    along_one = jnp.zeros((links.nz * block, qkv_cols), bf16)
    for step, piece in enumerate([q_shard] + steps_one):
        at = (z_at + step) % links.nz * block
        along_one = lax.dynamic_update_slice(along_one, piece, (at, 0))
    got_rows, far_small = after(along_one, got_rows, far_small)
    near_one = links.x(along_one), links.y(along_one)
    x, h1, h1_t = enter(pick(clips, t), got_rows[:shard_rows], order_b, gains[0], shifts[0])
    e, e_t = enter_cot(pick(cotangent, t), got_rows[shard_rows:], order_b, live)
    half = width // 2
    twin_rows = jnp.concatenate([e_t[half:], h1_t[half:]], axis=0)
    near_one, along_two, twin_rows, fc2_turned = after(
        (twin_rows, h1, e), near_one, along_two, twin_rows, fc2_weight.T
    )
    w_fc2 = lax.all_gather(after(along_two, fc2_turned), AXES, axis=0, tiled=True)
    w_fc2 = w_fc2.reshape(wide_count, 2, block, hidden_here)
    far_one = start_far(links, near_one)
    other_one = [links.c(piece) for piece in (after(near_one, along_one), *near_one)]
    far_one, other_one, along_two, twin_rows = after((), far_one, other_one, along_two, twin_rows)
    near_two = links.x(along_two), links.y(along_two)
    other_one += [links.c(piece) for piece in far_one]
    twin_rows = links.c(twin_rows)
    twin_rows, other_one = after((), twin_rows, other_one)
    twin_e, twin_h1 = twin_rows[:half], twin_rows[half:]
    w_one = [along_one, *near_one, *far_one, *other_one]
    zero_row = jnp.zeros((heads_cols,), f32)
    biases = jnp.stack(
        [
            jnp.concatenate([q_bias, zero_row, v_bias]),
            jnp.concatenate(
                [far_small[:heads_cols], zero_row, far_small[heads_cols : 2 * heads_cols]]
            ),
        ]
    )[:, None]
    fc1_biases = row(jnp.concatenate([fc1_bias, far_small[2 * heads_cols :]]))
    qkv = project(h1, w_one, biases)
    attn, lse = attend_fwd(qkv)
    lse_rows = lse.T

    near_two = after(attn, near_two)
    far_two = start_far(links, near_two)
    other_two = [links.c(piece) for piece in (after(near_two, along_two), *near_two)]
    far_two, other_two = after((), far_two, other_two)
    other_two += [links.c(piece) for piece in far_two]
    twin_attn = links.c(after(far_two, attn))
    other_two, twin_attn = after((), other_two, twin_attn)
    w_two = [along_two, *near_two, *far_two, *other_two]
    y, h2, h2_t = join_heads(attn, x, w_two, hidden_here, outs[0], gains[1], shifts[1])
    twin_h2 = links.c(h2_t[half:])
    hidden, slope = expand(h2, w_two, fc1_biases, hidden_here)
    twin_hidden = links.c(hidden)

    quarter, mid_row = width // 4, width // 8
    top, low = (0, mid_row), (mid_row, quarter)
    top_y, low_y = (quarter, quarter + mid_row), (quarter + mid_row, half)
    far_cuts = [[top, top_y], [low_y], [low]]
    near_cuts = [[(0, quarter)], [top_y], [low_y]]

    cuts = (near_cuts, far_cuts)
    stack = lambda one, two: jnp.concatenate([one[...], two[...]], axis=0)
    join = lambda one, two: jnp.concatenate([one[...], two[...]], axis=1)
    left_spec = pl.BlockSpec((half, length), lambda *_: (0, 0))

    def grad_of(lefts, rights, side, name, done):
        steps = hidden_here // TILE
        cols = pl.BlockSpec((length, TILE), lambda s: (0, side * steps + s))
        terms = lambda refs, kind: (join(*refs[:2]), stack(*refs[2:4]))
        args = [*lefts, *after(done, *rights)]
        specs = [left_spec] * 2 + [cols] * 2
        return grad_call(args, specs, (1, None, terms), cuts[side], name, steps)

    def grad_one(lefts, dps, attns, side, name, done):
        cols = pl.BlockSpec((length, heads_cols), lambda *_: (0, side))
        one_dp = pl.BlockSpec((1, length, heads_cols), lambda s: (jnp.minimum(s, 2), 0, 0))

        def terms(refs, kind):
            if kind == 0:
                return join(*refs[:2]), jnp.concatenate([refs[4][0], refs[5][0]], axis=0)
            return join(*refs[2:4]), stack(*refs[6:8])

        args = [*lefts, *after(done, *dps), *attns]
        specs = [left_spec] * 4 + [one_dp] * 2 + [cols] * 2
        return grad_call(args, specs, (2, lambda s: s // 3, terms), cuts[side], name, 4)

    w_fc2 = after(hidden, w_fc2)
    home_fc2, home_fc1, home_one = Home(links), Home(links), Home(links)

    du, fc1b_sum = hidden_back(e, slope, w_fc2, place)
    du, twin_hidden, twin_h2 = after((), du, twin_hidden, twin_h2)

    twin_du = links.c(du)
    fc2_args = (e_t, twin_e), (hidden, twin_hidden)
    far = grad_of(*fc2_args, 1, "fc2_far", ())
    near = grad_of(*fc2_args, 0, "fc2_near", far)
    far, near, twin_du = after((), far, near, twin_du)

    home_fc2.first(far, near)
    mid, da, da_t, second_sums = second_back(
        after(near, du), w_two, hidden_here, y, e, gains[1]
    )
    fc1_args = (h2_t, twin_h2), (du, twin_du)
    far = grad_of(*fc1_args, 1, "fc1_far", da)
    near = grad_of(*fc1_args, 0, "fc1_near", far)
    far, near, home_fc2.x_got, home_fc2.y_got = after(
        (), far, near, home_fc2.x_got, home_fc2.y_got
    )

    home_fc1.first(far, near)
    moved_fc2 = home_fc2.middle()
    d_heads = heads_back(after((near, moved_fc2), da), w_two, hidden_here)
    dp_far, q_far, v_far = attend_bwd(qkv, d_heads, lse_rows, 1)
    dp_near, q_near, v_near = attend_bwd(after(dp_far, qkv), d_heads, lse_rows, 0)
    dp_far, dp_near, home_fc1.x_got, home_fc1.y_got = after(
        (), dp_far, dp_near, home_fc1.x_got, home_fc1.y_got
    )

    moved_fc1 = home_fc1.middle()
    dp_far, dp_near, moved_fc2, moved_fc1, da_t_far = after(
        (), dp_far, dp_near, moved_fc2, moved_fc1, da_t[half:]
    )
    twin_dp = links.c(jnp.concatenate([dp_far, dp_near], axis=0))
    twin_da = links.c(da_t_far)
    home_fc2.second(*moved_fc2)
    home_fc1.second(*moved_fc1)
    grad_near, grad_sent_rows, first_sums = first_back(
        [dp_near, dp_far], w_one, x, mid, gains[0], order_b
    )
    twin_dp, twin_da, grad_sent_rows = after(
        grad_near, twin_dp, twin_da, grad_sent_rows
    )
    twin_far, twin_near = twin_dp[:3], twin_dp[3:]
    lefts, attns = (h1_t, twin_h1, da_t, twin_da), (attn, twin_attn)
    far = grad_one(lefts, (dp_far, twin_far), attns, 1, "one_far", ())
    near = grad_one(lefts, (dp_near, twin_near), attns, 0, "one_near", far)
    lasts = [home_fc2.y_last, home_fc2.x_last, home_fc1.y_last, home_fc1.x_last]
    far, near, lasts = after((), far, near, lasts)
    home_fc2.y_last, home_fc2.x_last, home_fc1.y_last, home_fc1.x_last = lasts

    home_one.first(far, near)
    moved = home_fc2.last(near, True)
    moved = home_fc1.last(moved, True)
    out_near, out_sent = layer_out(
        after(moved, hidden), w_fc2, place, y, outs[1], live, order_b
    )
    home_one.x_got, home_one.y_got = after(out_near, home_one.x_got, home_one.y_got)
    moved_one = home_one.middle()
    moved_one, grad_sent_rows = after((), moved_one, grad_sent_rows)
    home_one.second(*moved_one)
    grad_got = links.x(grad_sent_rows)
    moved = home_one.last((), False)
    out_got = links.x(after(moved, out_sent))

    sums = jnp.concatenate(
        [first_sums[:1], second_sums[:1], first_sums[1:], second_sums[1:]], axis=0
    )
    sums = lax.dot_general(
        sums, order_f, (((1,), (1,)), ((), ())), precision=lax.Precision.HIGHEST
    )

    def placed(near, far):
        return jnp.where(t == 0, jnp.concatenate([near, far]), jnp.concatenate([far, near]))

    small = [
        sums.reshape(-1),
        placed(q_near[0], q_far[0]),
        placed(v_near[0], v_far[0]),
        placed(fc1b_sum[0, :hidden_here], fc1b_sum[0, hidden_here:]),
    ]
    small = total_over_all(links, jnp.concatenate(small).reshape(-1, 128)).reshape(-1) * grad_scale
    sums = small[: 6 * width].reshape(6, width)
    own = lambda first, size: lax.dynamic_slice_in_dim(small, first + t * size, size, 0)

    g_one = home_one.value((), grad_scale)
    g_fc2 = home_fc2.value(moved, grad_scale)
    g_fc1 = home_fc1.value(moved, grad_scale)

    def both_slots(near, got):
        return jnp.where(t == 0, jnp.stack([near, got]), jnp.stack([got, near]))

    return (
        both_slots(out_near, out_got),
        both_slots(grad_near, grad_got).astype(f32),
        g_one[:, :qkv_cols].reshape(block, 3, heads_cols),
        own(6 * width, heads_cols),
        own(6 * width + 2 * heads_cols, heads_cols),
        g_one[:, qkv_cols:].T,
        g_fc1,
        own(6 * width + 4 * heads_cols, hidden_here),
        g_fc2.T,
        sums[0:2],
        sums[2:4],
        sums[4:6],
    )


def solution(mesh):
    body = own_slot if fits_own_slot(mesh) else shared_slots
    return jax.shard_map(
        body,
        mesh=mesh,
        in_specs=(
            P("wide", "tp", None),
            P("wide", "tp", None),
            P("wide"),
            P("wide", None, "tp"),
            P("tp"),
            P("tp"),
            P("tp", "wide"),
            P("wide", "tp"),
            P("tp"),
            P("tp", "wide"),
            P(),
            P(),
            P(),
        ),
        out_specs=(
            P("wide", "tp", None),
            P("wide", "tp", None),
            P("wide", None, "tp"),
            P("tp"),
            P("tp"),
            P("tp", "wide"),
            P("wide", "tp"),
            P("tp"),
            P("tp", "wide"),
            P(),
            P(),
            P(),
        ),
        check_vma=False,
    )
```

```python
from functools import partial
import math

import jax
import jax.numpy as jnp
from jax import lax
from jax.experimental import pallas as pl
from jax.experimental.pallas import tpu as pltpu
from jax.sharding import PartitionSpec as P

HEAD_DIM = 64


norm_eps = 1e-06
root_half = 1.0 / math.sqrt(2.0)
inv_root_two_pi = 1.0 / math.sqrt(2.0 * math.pi)


def layer_norm(in_rows, gain_row, shift_row):
    row_mean = jnp.mean(in_rows, axis=-1, keepdims=True)
    centred = in_rows - row_mean
    spread = jnp.mean(centred * centred, axis=-1, keepdims=True)
    inverse = lax.rsqrt(spread + norm_eps)
    unit_rows = centred * inverse
    return (unit_rows * gain_row + shift_row, unit_rows, inverse)


def norm_back(grad_rows, unit_rows, inverse, gain_row):
    scaled = grad_rows * gain_row
    mean_one = jnp.mean(scaled, axis=-1, keepdims=True)
    second = jnp.mean(scaled * unit_rows, axis=-1, keepdims=True)
    return inverse * (scaled - mean_one - unit_rows * second)


def contract_last(left_op, right_op):
    return lax.dot_general(
        left_op, right_op, (((1,), (1,)), ((), ())), preferred_element_type=jnp.float32
    )


def contract_first(left_op, right_op):
    return lax.dot_general(
        left_op, right_op, (((0,), (0,)), ((), ())), preferred_element_type=jnp.float32
    )


def attend_block(query, key_rows, value_rows):
    scores = jnp.einsum("qhd,khd->hqk", query, key_rows, preferred_element_type=jnp.float32)
    row_max = jnp.max(scores, axis=-1, keepdims=True)
    weights = jnp.exp(scores - row_max)
    row_sum = jnp.sum(weights, axis=-1, keepdims=True)
    prob_rows = (weights / row_sum).astype(jnp.bfloat16)
    mixed_rows = jnp.einsum(
        "hqk,khd->qhd", prob_rows, value_rows, preferred_element_type=jnp.float32
    )
    return (mixed_rows, row_max[..., 0] + jnp.log(row_sum[..., 0]))


def attend_back(query, grad_rows, log_total, key_rows, value_rows):
    scores = jnp.einsum("qhd,khd->hqk", query, key_rows, preferred_element_type=jnp.float32)
    prob_rows = jnp.exp(scores - log_total[..., None])
    dprobs = jnp.einsum("qhd,khd->hqk", grad_rows, value_rows, preferred_element_type=jnp.float32)
    row_delta = jnp.sum(prob_rows * dprobs, axis=-1, keepdims=True)
    dscores = (prob_rows * (dprobs - row_delta)).astype(jnp.bfloat16)
    dquery = jnp.einsum("hqk,khd->qhd", dscores, key_rows, preferred_element_type=jnp.float32)
    d_keys = jnp.einsum("hqk,qhd->khd", dscores, query, preferred_element_type=jnp.float32)
    dvalues = jnp.einsum(
        "hqk,qhd->khd",
        prob_rows.astype(jnp.bfloat16),
        grad_rows,
        preferred_element_type=jnp.float32,
    )
    return (dquery, d_keys, dvalues)


def shared_slots(
    clips,
    cotangent,
    clip_live,
    qkv_weight,
    q_bias,
    v_bias,
    proj_weight,
    fc1_weight,
    fc1_bias,
    fc2_weight,
    ln_gains,
    ln_biases,
    out_bias,
):
    tp_count = lax.axis_size("tp")
    wide_count = lax.axis_size("wide")
    slot_count, shard_rows, width = clips.shape
    length = shard_rows * tp_count
    local_cols = qkv_weight.shape[2]
    heads_here = local_cols // HEAD_DIM
    hidden_here = fc1_weight.shape[1]
    q_scale = 1.0 / math.sqrt(HEAD_DIM)
    grad_scale = 1.0 / math.sqrt(wide_count * slot_count * length)
    block_rows = 512
    blocks = length // block_rows
    tp_place = lax.axis_index("tp")
    live_slots = clip_live.astype(jnp.float32)
    qv_bias = jnp.stack([q_bias, v_bias])
    own_weights = (qkv_weight, proj_weight, fc1_weight, fc2_weight)

    def one_slot(state_in, inputs):
        rows_in, cot_in, live_one = inputs
        tied_weights = lax.optimization_barrier((own_weights, rows_in))[0]
        w_qkv, w_proj, w_fc1, w_fc2 = (
            lax.all_gather(tied_weights[0], "wide", axis=0, tiled=True),
            lax.all_gather(tied_weights[1], "wide", axis=1, tiled=True),
            lax.all_gather(tied_weights[2], "wide", axis=0, tiled=True),
            lax.all_gather(tied_weights[3], "wide", axis=1, tiled=True),
        )
        x_rows = rows_in.astype(jnp.float32)
        norm_one, unit_one, inv_one = layer_norm(x_rows, ln_gains[0], ln_biases[0])
        h1_full = lax.all_gather(norm_one.astype(jnp.bfloat16), "tp", axis=0, tiled=True)
        qkv_flat = w_qkv.reshape(width, 3 * local_cols)
        projected = jnp.dot(h1_full, qkv_flat, preferred_element_type=jnp.float32).reshape(
            length, 3, local_cols
        )
        query = (
            ((projected[:, 0] + qv_bias[0]) * q_scale)
            .astype(jnp.bfloat16)
            .reshape(length, heads_here, HEAD_DIM)
        )
        key_rows = projected[:, 1].astype(jnp.bfloat16).reshape(length, heads_here, HEAD_DIM)
        value_rows = (
            (projected[:, 2] + qv_bias[1])
            .astype(jnp.bfloat16)
            .reshape(length, heads_here, HEAD_DIM)
        )
        query_blocks = query.reshape(blocks, block_rows, heads_here, HEAD_DIM)
        mixed_blocks, log_totals = lax.map(
            partial(attend_block, key_rows=key_rows, value_rows=value_rows), query_blocks
        )
        attn_out = mixed_blocks.reshape(length, local_cols).astype(jnp.bfloat16)
        attn_sum = lax.psum_scatter(
            jnp.dot(attn_out, w_proj, preferred_element_type=jnp.float32),
            "tp",
            scatter_dimension=0,
            tiled=True,
        )
        mid_rows = x_rows + attn_sum + out_bias[0]
        norm_two, unit_two, inv_two = layer_norm(mid_rows, ln_gains[1], ln_biases[1])
        h2_full = lax.all_gather(norm_two.astype(jnp.bfloat16), "tp", axis=0, tiled=True)
        pre_act = jnp.dot(h2_full, w_fc1, preferred_element_type=jnp.float32) + fc1_bias
        cdf_part = 0.5 * (1.0 + lax.erf(pre_act * root_half))
        hidden = (pre_act * cdf_part).astype(jnp.bfloat16)
        mlp_sum = lax.psum_scatter(
            jnp.dot(hidden, w_fc2, preferred_element_type=jnp.float32).astype(jnp.bfloat16),
            "tp",
            scatter_dimension=0,
            tiled=True,
        ).astype(jnp.float32)
        block_out = (live_one * (mid_rows + mlp_sum + out_bias[1])).astype(jnp.bfloat16)
        out_grad = live_one * cot_in.astype(jnp.float32)
        out_full = lax.all_gather(out_grad.astype(jnp.bfloat16), "tp", axis=0, tiled=True)
        g_fc2 = contract_first(hidden, out_full)
        act_grad = contract_last(out_full, w_fc2)
        slope = cdf_part + pre_act * jnp.exp(-0.5 * pre_act * pre_act) * inv_root_two_pi
        pre_grad = act_grad * slope
        pre_grad_b = pre_grad.astype(jnp.bfloat16)
        g_fc1 = contract_first(h2_full, pre_grad_b)
        g_fc1b = jnp.sum(pre_grad, axis=0)
        norm_two_grad = lax.psum_scatter(
            contract_last(pre_grad_b, w_fc1), "tp", scatter_dimension=0, tiled=True
        )
        mid_grad = out_grad + norm_back(norm_two_grad, unit_two, inv_two, ln_gains[1])
        attn_full = lax.all_gather(mid_grad.astype(jnp.bfloat16), "tp", axis=0, tiled=True)
        g_proj = contract_first(attn_out, attn_full)
        mixed_grad = (
            contract_last(attn_full, w_proj)
            .astype(jnp.bfloat16)
            .reshape(blocks, block_rows, heads_here, HEAD_DIM)
        )

        def back_block(block_state, pieces):
            query_b, grad_b, lse_b = pieces
            d_query, d_keys, d_values = attend_back(query_b, grad_b, lse_b, key_rows, value_rows)
            return ((block_state[0] + d_keys, block_state[1] + d_values), d_query)

        empty_kv = jnp.zeros((length, heads_here, HEAD_DIM), jnp.float32)
        (key_grad, value_grad), query_grad = lax.scan(
            back_block, (empty_kv, empty_kv), (query_blocks, mixed_grad, log_totals)
        )
        query_grad = query_grad.reshape(length, local_cols) * q_scale
        key_grad = key_grad.reshape(length, local_cols)
        value_grad = value_grad.reshape(length, local_cols)
        g_qvb = jnp.stack([jnp.sum(query_grad, axis=0), jnp.sum(value_grad, axis=0)])
        proj_grads = (
            jnp.stack([query_grad, key_grad, value_grad], axis=1)
            .astype(jnp.bfloat16)
            .reshape(length, 3 * local_cols)
        )
        g_qkv = contract_first(h1_full, proj_grads).reshape(width, 3, local_cols)
        norm_one_grad = lax.psum_scatter(
            contract_last(proj_grads, qkv_flat).astype(jnp.bfloat16),
            "tp",
            scatter_dimension=0,
            tiled=True,
        ).astype(jnp.float32)
        in_grad = mid_grad + norm_back(norm_one_grad, unit_one, inv_one, ln_gains[0])
        gain_part = jnp.stack(
            [jnp.sum(norm_one_grad * unit_one, axis=0), jnp.sum(norm_two_grad * unit_two, axis=0)]
        )
        shift_part = jnp.stack([jnp.sum(norm_one_grad, axis=0), jnp.sum(norm_two_grad, axis=0)])
        bias_part = jnp.stack([jnp.sum(mid_grad, axis=0), jnp.sum(out_grad, axis=0)])
        summed = (
            lax.psum_scatter(
                g_qkv.astype(jnp.bfloat16), "wide", scatter_dimension=0, tiled=True
            ).astype(jnp.float32),
            lax.psum_scatter(
                g_proj.astype(jnp.bfloat16), "wide", scatter_dimension=1, tiled=True
            ).astype(jnp.float32),
            lax.psum_scatter(
                g_fc1.astype(jnp.bfloat16), "wide", scatter_dimension=0, tiled=True
            ).astype(jnp.float32),
            lax.psum_scatter(
                g_fc2.astype(jnp.bfloat16), "wide", scatter_dimension=1, tiled=True
            ).astype(jnp.float32),
        )
        weight_acc = jax.tree.map(jnp.add, state_in[0], summed)
        vector_acc = jax.tree.map(
            jnp.add, state_in[1], (gain_part, shift_part, bias_part, g_qvb, g_fc1b)
        )
        return ((weight_acc, vector_acc), (block_out, in_grad))

    weight_zero = tuple((jnp.zeros(shard_in.shape, jnp.float32) for shard_in in own_weights))
    vector_zero = (
        jnp.zeros((2, width), jnp.float32),
        jnp.zeros((2, width), jnp.float32),
        jnp.zeros((2, width), jnp.float32),
        jnp.zeros((2, local_cols), jnp.float32),
        jnp.zeros((hidden_here,), jnp.float32),
    )
    (weight_sums, vector_acc), (block_out, clips_grad) = lax.scan(
        one_slot, (weight_zero, vector_zero), (clips, cotangent, live_slots)
    )
    gain_acc, shift_acc, bias_acc, qvb_acc, fc1b_acc = vector_acc
    qvb_pad = lax.dynamic_update_slice(
        jnp.zeros((2, width), jnp.float32), qvb_acc, (0, tp_place * local_cols)
    )
    fc1b_pad = lax.dynamic_update_slice(
        jnp.zeros((hidden_here * tp_count,), jnp.float32), fc1b_acc, (tp_place * hidden_here,)
    )
    gain_sum, shift_sum, bias_sum, qvb_sum, fc1b_sum = lax.psum(
        (gain_acc, shift_acc, bias_acc, qvb_pad, fc1b_pad), ("wide", "tp")
    )
    qvb_own = lax.dynamic_slice_in_dim(qvb_sum, tp_place * local_cols, local_cols, 1)
    fc1b_own = lax.dynamic_slice_in_dim(fc1b_sum, tp_place * hidden_here, hidden_here, 0)
    return (
        block_out,
        clips_grad,
        weight_sums[0] * grad_scale,
        qvb_own[0] * grad_scale,
        qvb_own[1] * grad_scale,
        weight_sums[1] * grad_scale,
        weight_sums[2] * grad_scale,
        fc1b_own * grad_scale,
        weight_sums[3] * grad_scale,
        gain_sum * grad_scale,
        shift_sum * grad_scale,
        bias_sum * grad_scale,
    )


AXES = ("wide", "tp")
PAIR = 128
TILE = 512
MIB = 1024 * 1024
GRANT = {"project": 60, "hidden_back": 60, "heads_back": 60, "layer_out": 60}
WIDE = 1024
bf16 = jnp.bfloat16
f32 = jnp.float32


def fits_own_slot(mesh):
    return mesh.shape["tp"] == 2 and mesh.shape["wide"] % 4 == 0


def nt_dot(left_op, right_op):
    return lax.dot_general(
        left_op, right_op, (((1,), (1,)), ((), ())), preferred_element_type=f32
    )


def nn_dot(left_op, right_op):
    return lax.dot_general(
        left_op, right_op, (((1,), (0,)), ((), ())), preferred_element_type=f32
    )


def kernel_call(body, name, grid, in_specs, out_specs, out_shape, scratch=(), scalars=0):
    return pl.pallas_call(
        body,
        grid_spec=pltpu.PrefetchScalarGridSpec(
            num_scalar_prefetch=scalars,
            grid=grid,
            in_specs=in_specs,
            out_specs=out_specs,
            scratch_shapes=list(scratch),
        ),
        out_shape=out_shape,
        compiler_params=pltpu.CompilerParams(vmem_limit_bytes=GRANT.get(name, 60) * MIB),
        cost_estimate=pl.CostEstimate(flops=1, bytes_accessed=1, transcendentals=0),
        name=name,
    )


def whole(shape):
    return pl.BlockSpec(shape, lambda *at: (0,) * len(shape))


def array(*shape, dtype=bf16):
    return jax.ShapeDtypeStruct(shape, dtype)


def norm_stats(rows):
    row_mean = jnp.mean(rows, axis=-1, keepdims=True)
    centred = rows - row_mean
    spread = jnp.mean(centred * centred, axis=-1, keepdims=True)
    inverse = lax.rsqrt(spread + norm_eps)
    return centred * inverse, inverse


NEAR = (0, 2, 5, 7)
FAR = (1, 3, 4, 6, 8, 9)


class Pieces:
    def __init__(self, pieces, columns, first=0, tile=WIDE):
        self.pieces, self.columns, self.first = pieces, columns, first
        self.tile = min(tile, columns)
        self.tiles = columns // self.tile
        self.args = list(pieces)
        self.specs = [pl.BlockSpec(memory_space=pl.ANY)] * len(pieces)
        rows = sum(pieces[i].shape[0] for i in NEAR)
        self.scratch = [
            pltpu.VMEM((2, rows, columns), bf16),
            pltpu.SemaphoreType.DMA((self.tiles, len(pieces))),
        ]

    def copies(self, refs, side, tile, w_ref, sems):
        at, found = 0, []
        for index in FAR if side else NEAR:
            rows = self.pieces[index].shape[0]
            found.append(
                pltpu.make_async_copy(
                    refs[index].at[:, pl.ds(self.first + tile * self.tile, self.tile)],
                    w_ref.at[side, pl.ds(at, rows), pl.ds(tile * self.tile, self.tile)],
                    sems.at[tile, index],
                )
            )
            at += rows
        return found

    def start(self, refs, w_ref, sems):
        for side in range(2):
            for tile in range(self.tiles):
                for copy in self.copies(refs, side, tile, w_ref, sems):
                    copy.start()

    def wait(self, refs, side, tile, w_ref, sems):
        for copy in self.copies(refs, side, tile, w_ref, sems):
            copy.wait()

    def get(self, refs, side, tile, w_ref, sems):
        self.wait(refs, side, tile, w_ref, sems)
        return w_ref[side, :, pl.ds(tile * self.tile, self.tile)]

    def each_step(self, step, refs, w_ref, sems, work):
        pl.when(step == 0)(lambda: self.start(refs, w_ref, sems))
        for side in range(2):
            for tile in range(self.tiles):

                @pl.when(step == side * self.tiles + tile)
                def _():
                    work(side, tile, self.get(refs, side, tile, w_ref, sems))


def enter_kernel(own_ref, got_ref, order_ref, gain_ref, shift_ref, x_ref, h_ref, ht_ref):
    half = own_ref.shape[0]
    for part, ref in enumerate((own_ref, got_ref)):
        rows = nn_dot(ref[...], order_ref[...])
        here = pl.ds(part * half, half)
        x_ref[here, :] = rows.astype(bf16)
        unit, _ = norm_stats(rows)
        normed = (unit * gain_ref[...] + shift_ref[...]).astype(bf16)
        h_ref[here, :] = normed
        ht_ref[:, here] = normed.T


def enter(own, got, order_b, gain, shift):
    half, width = own.shape
    length = 2 * half
    return kernel_call(
        enter_kernel,
        "enter",
        (1,),
        [whole((half, width))] * 2 + [whole((width, width))] + [whole((1, width))] * 2,
        [whole((length, width))] * 2 + [whole((width, length))],
        [array(length, width)] * 2 + [array(width, length)],
    )(own, got, order_b, gain, shift)


def cot_kernel(own_ref, got_ref, order_ref, live_ref, e_ref, et_ref):
    half = own_ref.shape[0]
    for part, ref in enumerate((own_ref, got_ref)):
        rows = (live_ref[...] * nn_dot(ref[...], order_ref[...])).astype(bf16)
        here = pl.ds(part * half, half)
        e_ref[here, :] = rows
        et_ref[:, here] = rows.T


def enter_cot(own, got, order_b, live):
    half, width = own.shape
    length = 2 * half
    return kernel_call(
        cot_kernel,
        "enter_cot",
        (1,),
        [whole((half, width))] * 2 + [whole((width, width)), whole((1, width))],
        [whole((length, width)), whole((width, length))],
        [array(length, width), array(width, length)],
    )(own, got, order_b, live)


def project(h, pieces, biases):
    length, width = h.shape
    each = pieces[0].shape[1] // 3
    load = Pieces(pieces, 3 * each, 0, each)
    scales = (1.0 / math.sqrt(HEAD_DIM), None, None)

    def body(h_ref, bias_ref, *refs):
        refs, (out_ref, w_ref, sems) = refs[:-3], refs[-3:]

        def work(side, tile, weight):
            acc = nn_dot(h_ref[...], weight) + bias_ref[0]
            out_ref[0] = (acc if scales[tile] is None else acc * scales[tile]).astype(bf16)

        load.each_step(pl.program_id(0), refs, w_ref, sems, work)

    return kernel_call(
        body,
        "project",
        (6,),
        [whole((length, width)), pl.BlockSpec((1, 1, each), lambda s: (s // 3, 0, s % 3))]
        + load.specs,
        pl.BlockSpec((1, length, each), lambda s: (s % 3, 0, s // 3)),
        array(3, length, width),
        load.scratch,
    )(h, biases, *load.args)


def attend_kernel(q_ref, k_ref, v_ref, o_ref, lse_ref):
    pair = pl.program_id(0)
    rows = q_ref.shape[1]
    lanes = lax.broadcasted_iota(jnp.int32, (rows, PAIR), 1)
    keys = k_ref[0]
    values = v_ref[0]
    total = jnp.zeros((rows, PAIR), f32)
    for half in range(2):
        mask = (lanes // HEAD_DIM) == half
        query = jnp.where(mask, q_ref[0], jnp.zeros_like(keys))
        scores = nt_dot(query, keys)
        row_max = jnp.max(scores, axis=-1, keepdims=True)
        weights = jnp.exp(scores - row_max)
        row_sum = jnp.sum(weights, axis=-1, keepdims=True)
        probs = (weights * (1.0 / row_sum)).astype(bf16)
        mixed = nn_dot(probs, values)
        total = jnp.where(mask, mixed, total)
        lse = row_max + jnp.log(row_sum)
        lse_ref[...] = jnp.where(lanes == 2 * pair + half, lse, lse_ref[...])
    o_ref[...] = total.astype(bf16)


def head_spec(length, index):
    return pl.BlockSpec((1, length, PAIR), lambda i: (index, 0, i))


def attend_fwd(qkv):
    _, length, width = qkv.shape
    return kernel_call(
        attend_kernel,
        "attend_fwd",
        (width // PAIR,),
        [head_spec(length, j) for j in range(3)],
        [pl.BlockSpec((length, PAIR), lambda i: (0, i)), whole((length, PAIR))],
        [array(length, width), array(length, PAIR, dtype=f32)],
    )(qkv, qkv, qkv)


def join_heads(attn, x, pieces, first, bias, gain, shift):
    length, width = x.shape
    load = Pieces(pieces, TILE, first)

    def body(attn_ref, x_ref, bias_ref, gain_ref, shift_ref, *refs):
        refs, (y_ref, h_ref, ht_ref, w_ref, sems) = refs[:-5], refs[-5:]
        load.start(refs, w_ref, sems)
        load.wait(refs, 0, 0, w_ref, sems)
        load.wait(refs, 1, 0, w_ref, sems)
        half = length // 2
        for part in range(2):
            here = pl.ds(part * half, half)
            rows = nt_dot(attn_ref[here, :TILE], w_ref[0]) + nt_dot(attn_ref[here, TILE:], w_ref[1])
            rows = x_ref[here, :].astype(f32) + rows + bias_ref[...]
            y_ref[here, :] = rows
            unit, _ = norm_stats(rows)
            normed = (unit * gain_ref[...] + shift_ref[...]).astype(bf16)
            h_ref[here, :] = normed
            ht_ref[:, here] = normed.T

    return kernel_call(
        body,
        "join_heads",
        (1,),
        [whole((length, width))] * 2 + [whole((1, width))] * 3 + load.specs,
        [whole((length, width))] * 2 + [whole((width, length))],
        [array(length, width, dtype=f32), array(length, width), array(width, length)],
        load.scratch,
    )(attn, x, bias, gain, shift, *load.args)


def expand(h, pieces, bias, hidden):
    length, width = h.shape
    load = Pieces(pieces, hidden)

    def body(h_ref, bias_ref, *refs):
        refs, (g_ref, slope_ref, w_ref, sems) = refs[:-4], refs[-4:]

        def work(side, tile, weight):
            pre = nn_dot(h_ref[...], weight) + bias_ref[...]
            cdf = 0.5 * (1.0 + lax.erf(pre * root_half))
            g_ref[...] = (pre * cdf).astype(bf16)
            density = jnp.exp(-0.5 * pre * pre) * inv_root_two_pi
            slope_ref[...] = (cdf + pre * density).astype(bf16)

        load.each_step(pl.program_id(0), refs, w_ref, sems, work)

    block = pl.BlockSpec((length, WIDE), lambda s: (0, s))
    return kernel_call(
        body,
        "expand",
        (2 * load.tiles,),
        [whole((length, width)), pl.BlockSpec((1, WIDE), lambda s: (0, s))] + load.specs,
        [block] * 2,
        [array(length, 2 * hidden)] * 2,
        load.scratch,
    )(h, bias, *load.args)


def hidden_back(e, slope, pieces):
    length, width = e.shape
    hidden = pieces[0].shape[1]
    load = Pieces(pieces, hidden)

    def body(e_ref, slope_ref, *refs):
        refs, (du_ref, sum_ref, w_ref, sems) = refs[:-4], refs[-4:]

        def work(side, tile, weight):
            du = nn_dot(e_ref[...], weight) * slope_ref[...].astype(f32)
            du_ref[...] = du.astype(bf16)
            sum_ref[...] = jnp.sum(du, axis=0, keepdims=True)

        load.each_step(pl.program_id(0), refs, w_ref, sems, work)

    block = pl.BlockSpec((length, WIDE), lambda s: (0, s))
    row = pl.BlockSpec((1, WIDE), lambda s: (0, s))
    return kernel_call(
        body,
        "hidden_back",
        (2 * load.tiles,),
        [whole((length, width)), block] + load.specs,
        [block, row],
        [array(length, 2 * hidden), array(1, 2 * hidden, dtype=f32)],
        load.scratch,
    )(e, slope, *load.args)


def heads_back(da, pieces, first):
    length, width = da.shape
    load = Pieces(pieces, TILE, first)

    def body(da_ref, *refs):
        refs, (out_ref, w_ref, sems) = refs[:-3], refs[-3:]
        load.start(refs, w_ref, sems)
        for side in range(2):
            load.wait(refs, side, 0, w_ref, sems)
            out_ref[:, pl.ds(side * TILE, TILE)] = nn_dot(da_ref[...], w_ref[side]).astype(bf16)

    return kernel_call(
        body,
        "heads_back",
        (1,),
        [whole((length, width))] + load.specs,
        whole((length, 2 * TILE)),
        array(length, 2 * TILE),
        load.scratch,
    )(da, *load.args)


def contract_back(rows, rows_specs, left_of, load, extras, finish, name, outs):
    count = len(extras)
    length, width = extras[0].shape

    def body(*refs):
        rows_refs, refs = refs[: len(rows)], refs[len(rows) :]
        extra_refs, refs = refs[:count], refs[count:]
        w_refs, refs = refs[: len(load.args)], refs[len(load.args) :]
        out_refs, refs = refs[: len(outs)], refs[len(outs) :]
        w_ref, sems, acc_ref, extra_sems = refs[:4]
        held = refs[4:]
        copies = [
            pltpu.make_async_copy(source, target, extra_sems.at[i])
            for i, (source, target) in enumerate(zip(extra_refs, held))
        ]

        def work(side, tile, weight):
            term = nt_dot(left_of(rows_refs), weight)
            if side == 0 and tile == 0:
                for copy in copies:
                    copy.start()
                acc_ref[...] = term
            else:
                acc_ref[...] += term
            if side == 1 and tile == load.tiles - 1:
                for copy in copies:
                    copy.wait()
                finish(acc_ref, held, out_refs)

        load.each_step(pl.program_id(0), w_refs, w_ref, sems, work)

    return kernel_call(
        body,
        name,
        (2 * load.tiles,),
        rows_specs + [pl.BlockSpec(memory_space=pl.ANY)] * count + load.specs,
        [whole(o.shape) for o in outs],
        outs,
        load.scratch
        + [pltpu.VMEM((length, width), f32), pltpu.SemaphoreType.DMA((count,))]
        + [pltpu.VMEM(extra.shape, extra.dtype) for extra in extras],
    )(*rows, *extras, *load.args)


def to_home(rows, order_ref):
    return nt_dot(rows.astype(bf16), order_ref[...]).astype(bf16)


def layer_out(hidden, pieces, y, bias, live, order_b):
    length, width = y.shape
    half = length // 2

    def finish(acc_ref, ins, outs):
        y_ref, bias_ref, live_ref, order_ref = ins
        for part in range(2):
            here = pl.ds(part * half, half)
            rows = live_ref[...] * (y_ref[here, :] + acc_ref[here, :] + bias_ref[...])
            outs[part][...] = to_home(rows, order_ref)

    return contract_back(
        [hidden],
        [pl.BlockSpec((length, WIDE), lambda s, *_: (0, s))],
        lambda refs: refs[0][...],
        Pieces(pieces, pieces[0].shape[1]),
        (y, bias, live, order_b),
        finish,
        "layer_out",
        [array(half, width)] * 2,
    )


def second_back(du, pieces, hidden, y, e, gain):
    length, width = y.shape
    half = length // 2

    def finish(acc_ref, ins, outs):
        y_ref, e_ref, gain_ref = ins
        mid_ref, da_ref, dat_ref, sum_ref = outs
        sums = [jnp.zeros((1, width), f32)] * 4
        for part in range(2):
            here = pl.ds(part * half, half)
            unit, inverse = norm_stats(y_ref[here, :])
            grad = acc_ref[here, :]
            e_rows = e_ref[here, :].astype(f32)
            mid = e_rows + norm_back(grad, unit, inverse, gain_ref[...])
            mid_ref[here, :] = mid
            mid_b = mid.astype(bf16)
            da_ref[here, :] = mid_b
            dat_ref[:, here] = mid_b.T
            terms = (grad * unit, grad, mid, e_rows)
            sums = [s + jnp.sum(term, axis=0, keepdims=True) for s, term in zip(sums, terms)]
        sum_ref[...] = jnp.concatenate(sums, axis=0)

    return contract_back(
        [du],
        [pl.BlockSpec((length, WIDE), lambda s: (0, s))],
        lambda refs: refs[0][...],
        Pieces(pieces, hidden),
        (y, e, gain),
        finish,
        "second_back",
        [
            array(length, width, dtype=f32),
            array(length, width),
            array(width, length),
            array(4, width, dtype=f32),
        ],
    )


def first_back(dp, pieces, x, mid, gain, order_b):
    length, width = x.shape
    half = length // 2

    def finish(acc_ref, ins, outs):
        x_ref, mid_ref, gain_ref, order_ref = ins
        sum_ref = outs[2]
        sums = [jnp.zeros((1, width), f32)] * 2
        for part in range(2):
            here = pl.ds(part * half, half)
            unit, inverse = norm_stats(x_ref[here, :].astype(f32))
            grad = acc_ref[here, :]
            rows = mid_ref[here, :] + norm_back(grad, unit, inverse, gain_ref[...])
            outs[part][...] = to_home(rows, order_ref)
            terms = (grad * unit, grad)
            sums = [s + jnp.sum(term, axis=0, keepdims=True) for s, term in zip(sums, terms)]
        sum_ref[...] = jnp.concatenate(sums, axis=0)

    return contract_back(
        [dp],
        [pl.BlockSpec((3, length, width // 2), lambda s: (0, 0, s))],
        lambda refs: jnp.concatenate([refs[0][j] for j in range(3)], axis=1),
        Pieces(pieces, pieces[0].shape[1], 0, pieces[0].shape[1]),
        (x, mid, gain, order_b),
        finish,
        "first_back",
        [array(half, width)] * 2 + [array(2, width, dtype=f32)],
    )


def attend_back_kernel(q_ref, k_ref, v_ref, g_ref, lse_ref, dp_ref, qs_ref, vs_ref):
    pair = pl.program_id(0)
    rows = q_ref.shape[1]
    lanes = lax.broadcasted_iota(jnp.int32, (rows, PAIR), 1)
    sub = lax.broadcasted_iota(jnp.int32, (PAIR, rows), 0)
    query = q_ref[0]
    keys = k_ref[0]
    values = v_ref[0]
    grads = g_ref[...]
    blank = jnp.zeros_like(keys)
    keys_t = keys.T
    dq_t = jnp.zeros((PAIR, rows), f32)
    dk = jnp.zeros((rows, PAIR), f32)
    dv = jnp.zeros((rows, PAIR), f32)
    for half in range(2):
        mask = (lanes // HEAD_DIM) == half
        scores_t = nt_dot(jnp.where(mask, keys, blank), query)
        lse = lse_ref[pl.ds(2 * pair + half, 1), :]
        probs_t = jnp.exp(scores_t - lse)
        dprobs_t = nt_dot(jnp.where(mask, values, blank), grads)
        delta = jnp.sum(probs_t * dprobs_t, axis=0, keepdims=True)
        ds_t = (probs_t * (dprobs_t - delta)).astype(bf16)
        dv = jnp.where(mask, nn_dot(probs_t.astype(bf16), grads), dv)
        dk = jnp.where(mask, nn_dot(ds_t, query), dk)
        dq_t = jnp.where((sub // HEAD_DIM) == half, nn_dot(keys_t, ds_t), dq_t)
    dq = dq_t.T * (1.0 / math.sqrt(HEAD_DIM))
    dp_ref[0] = dq.astype(bf16)
    dp_ref[1] = dk.astype(bf16)
    dp_ref[2] = dv.astype(bf16)
    qs_ref[...] = jnp.sum(dq, axis=0, keepdims=True)
    vs_ref[...] = jnp.sum(dv, axis=0, keepdims=True)


def attend_bwd(qkv, grads, lse_rows):
    _, length, width = qkv.shape
    row = pl.BlockSpec((1, PAIR), lambda i: (0, i))
    sums = array(1, width, dtype=f32)
    return kernel_call(
        attend_back_kernel,
        "attend_bwd",
        (width // PAIR,),
        [head_spec(length, j) for j in range(3)]
        + [pl.BlockSpec((length, PAIR), lambda i: (0, i)), whole((PAIR, length))],
        [pl.BlockSpec((3, length, PAIR), lambda i: (0, 0, i)), row, row],
        [array(3, length, width), sums, sums],
    )(qkv, qkv, qkv, grads, lse_rows)


def both_sides(args, specs, kinds, terms, name, tiles):
    count = len(args)
    half = args[0].shape[0] // 2
    mid = half // 4

    def body(*refs):
        x_ref, y_ref, k10_ref, k00_ref, k01_ref = refs[count:]
        step = pl.program_id(0)

        def run(kind, side):
            left, right = terms(refs[:count], kind)
            acc = nn_dot(left, right).astype(bf16)
            y_ref[...] = acc[3 * mid :]
            if side:
                x_ref[pl.ds(0, mid), :] = acc[:mid]
                x_ref[pl.ds(mid, mid), :] = acc[2 * mid : 3 * mid]
                k10_ref[...] = acc[mid : 2 * mid]
            else:
                k00_ref[...] = acc[: 2 * mid]
                k01_ref[...] = acc[2 * mid : 3 * mid]

        for side in range(2):
            for kind, first in enumerate(kinds):
                last = kinds[kind + 1] if kind + 1 < len(kinds) else tiles
                base = 0 if side else tiles
                here = (step >= base + first) & (step < base + last)
                pl.when(here)(partial(run, kind, side))

    far = lambda size: pl.BlockSpec((size, TILE), lambda s: (0, jnp.minimum(s, tiles - 1)))
    near = lambda size: pl.BlockSpec((size, TILE), lambda s: (0, jnp.maximum(s - tiles, 0)))
    both = pl.BlockSpec((mid, TILE), lambda s: (s // tiles, s % tiles))
    sizes = (2 * mid, 2 * mid, mid, 2 * mid, mid)
    return kernel_call(
        body,
        name,
        (2 * tiles,),
        specs,
        [far(2 * mid), both, far(mid), near(2 * mid), near(mid)],
        [array(size, tiles * TILE) for size in sizes],
    )(*args)


def add_mid_kernel(k01_ref, rx_ref, k10_ref, ry_ref, y_ref, x_ref):
    half = k01_ref.shape[0]
    y_ref[...] = (k01_ref[...].astype(f32) + rx_ref[pl.ds(half, half), :].astype(f32)).astype(bf16)
    x_ref[...] = (k10_ref[...].astype(f32) + ry_ref[pl.ds(0, half), :].astype(f32)).astype(bf16)


def add_last_kernel(k00_ref, rx_ref, ry_ref, y2_ref, x2_ref, out_ref):
    half = y2_ref.shape[0]
    top, low = pl.ds(0, half), pl.ds(half, half)
    near = (rx_ref[top, :], y2_ref[...]), (ry_ref[low, :], x2_ref[...])
    for here, (one, two) in zip((top, low), near):
        total = k00_ref[here, :].astype(f32) + one.astype(f32) + two.astype(f32)
        out_ref[here, :] = total.astype(bf16)


def small_call(body, name, args, shapes):
    out_specs = [whole(s.shape) for s in shapes]
    return kernel_call(body, name, (1,), [whole(a.shape) for a in args], out_specs, shapes)(*args)


class Links:
    def __init__(self):
        self.nz = lax.axis_size("wide") // 4
        self.across = self.table(lambda z, y, c, x: (z, y, c, 1 - x))
        self.beside = self.table(lambda z, y, c, x: (z, 1 - y, c, x))
        self.twin = self.table(lambda z, y, c, x: (z, y, 1 - c, x))

    def table(self, source):
        pairs = []
        for z in range(self.nz):
            for y in range(2):
                for c in range(2):
                    for x in range(2):
                        zs, ys, cs, xs = source(z, y, c, x)
                        pairs.append(
                            (((zs * 2 + ys) * 2 + cs) * 2 + xs, ((z * 2 + y) * 2 + c) * 2 + x)
                        )
        return pairs

    def from_z(self, rows, step):
        shift = self.table(lambda z, y, c, x: ((z + step) % self.nz, y, c, x))
        return lax.ppermute(rows, AXES, shift)

    def z_groups(self):
        rest = [(y, c, x) for y in range(2) for c in range(2) for x in range(2)]
        return [
            [((z * 2 + y) * 2 + c) * 2 + x for z in range(self.nz)] for y, c, x in rest
        ]

    def z_sum_apart(self, rows):
        return lax.psum_scatter(
            rows, AXES, scatter_dimension=0, tiled=True, axis_index_groups=self.z_groups()
        )

    def z_sum(self, rows):
        got = lax.all_to_all(rows, AXES, 0, 0, tiled=True, axis_index_groups=self.z_groups())
        return got.reshape(self.nz, -1, rows.shape[1])

    def z_all(self, rows):
        return lax.all_gather(
            rows, AXES, axis=0, tiled=True, axis_index_groups=self.z_groups()
        )

    def x(self, rows):
        return lax.ppermute(rows, AXES, self.across)

    def y(self, rows):
        return lax.ppermute(rows, AXES, self.beside)

    def c(self, rows):
        return lax.ppermute(rows, AXES, self.twin)

    def flip(self, rows, bit):
        swap = self.table(lambda z, y, c, x: (z ^ bit, y, c, x))
        return lax.ppermute(rows, AXES, swap)


def after(done, *values):
    out = lax.optimization_barrier((values, done))[0]
    return out if len(values) > 1 else out[0]


def total_over_all(links, rows):
    for move in (links.c, links.x, links.y):
        rows = rows + move(rows)
    bit = 1
    while bit < links.nz:
        rows = rows + links.flip(rows, bit)
        bit *= 2
    return rows


def start_far(links, near):
    by_x, by_y = near
    half = by_x.shape[0] // 2
    return links.x(by_y[:half]), links.y(by_x[half:])


class Home:
    def __init__(self, links):
        self.links = links

    def first(self, pieces):
        x_first, y_first, self.k10_low, self.k00, self.k01_top = pieces
        self.x_got, self.y_got = self.links.x(x_first), self.links.y(y_first)

    def middle(self):
        half = self.k01_top.shape[0]
        args = (self.k01_top, self.x_got, self.k10_low, self.y_got)
        shape = array(*self.k01_top.shape)
        out_y, out_x = small_call(add_mid_kernel, "add_mid", args, [shape, shape])
        return out_y, out_x

    def second(self, out_y, out_x):
        self.y_last, self.x_last = self.links.y(out_y), self.links.x(out_x)

    def last(self, done, apart):
        y_last, x_last = after(done, self.y_last, self.x_last)
        args = (self.k00, self.x_got, self.y_got, y_last, x_last)
        (total,) = small_call(add_last_kernel, "add_last", args, [array(*self.k00.shape)])
        self.home = self.links.z_sum_apart(total)[None] if apart else self.links.z_sum(total)
        return total

    def value(self, done, scale):
        return jnp.sum(after(done, self.home).astype(f32), axis=0) * scale


def own_slot(
    clips,
    cotangent,
    clip_live,
    qkv_weight,
    q_bias,
    v_bias,
    proj_weight,
    fc1_weight,
    fc1_bias,
    fc2_weight,
    ln_gains,
    ln_biases,
    out_bias,
):
    links = Links()
    slot_count, shard_rows, width = clips.shape
    wide_count = lax.axis_size("wide")
    length = 2 * shard_rows
    block = qkv_weight.shape[0]
    heads_cols = qkv_weight.shape[2]
    hidden_here = fc1_weight.shape[1]
    grad_scale = 1.0 / math.sqrt(wide_count * slot_count * length)
    wide_at = lax.axis_index("wide")
    t = lax.axis_index("tp")
    z_at, y_at, c_at = wide_at // 4, (wide_at // 2) % 2, wide_at % 2
    qkv_cols = 3 * heads_cols
    pick = lambda both, at: lax.dynamic_index_in_dim(both, at, 0, keepdims=False)
    row = lambda vector: vector.reshape(1, -1)

    two_shard = jnp.concatenate([fc1_weight, proj_weight.T], axis=1)
    along_two = links.z_all(two_shard)
    q_shard = qkv_weight.reshape(block, qkv_cols)
    steps_one = [links.from_z(q_shard, k) for k in range(1, links.nz)]
    got_rows = links.x(jnp.concatenate([pick(clips, 1 - t), pick(cotangent, 1 - t)], axis=0))
    far_small = jnp.concatenate([q_bias, v_bias, fc1_bias]).reshape(-1, 128)
    far_small = links.x(far_small).reshape(-1)

    spot = jnp.arange(width)
    rel = spot // block
    kc, ky, kz = rel // (2 * links.nz), (rel // links.nz) % 2, rel % links.nz
    home = (kz * 2 + (y_at ^ ky)) * 2 + (c_at ^ kc)
    order = spot[:, None] == (home * block + spot % block)[None, :]
    order_b = order.astype(bf16)
    order_f = order.astype(f32)
    vectors = jnp.dot(
        jnp.concatenate([ln_gains, ln_biases, out_bias], axis=0),
        order_f,
        precision=lax.Precision.HIGHEST,
    )
    gains, shifts, outs = (
        (vectors[2 * i : 2 * i + 1], vectors[2 * i + 1 : 2 * i + 2]) for i in range(3)
    )
    live = jnp.full((1, width), pick(clip_live, t).astype(f32))
    along_one = jnp.zeros((links.nz * block, qkv_cols), bf16)
    for step, piece in enumerate([q_shard] + steps_one):
        at = (z_at + step) % links.nz * block
        along_one = lax.dynamic_update_slice(along_one, piece, (at, 0))
    got_rows, far_small = after(along_one, got_rows, far_small)
    near_one = links.x(along_one), links.y(along_one)
    x, h1, h1_t = enter(pick(clips, t), got_rows[:shard_rows], order_b, gains[0], shifts[0])
    e, e_t = enter_cot(pick(cotangent, t), got_rows[shard_rows:], order_b, live)
    half = width // 2
    twin_rows = jnp.concatenate([e_t[half:], h1_t[half:]], axis=0)
    near_one, along_two, twin_rows, fc2_turned = after(
        (twin_rows, h1, e), near_one, along_two, twin_rows, fc2_weight.T
    )
    along_three = links.z_all(after(along_two, fc2_turned))
    far_one = start_far(links, near_one)
    other_one = [links.c(piece) for piece in (after(near_one, along_one), *near_one)]
    far_one, other_one, along_two, twin_rows = after((), far_one, other_one, along_two, twin_rows)
    near_two = links.x(along_two), links.y(along_two)
    other_one += [links.c(piece) for piece in far_one]
    twin_rows = links.c(twin_rows)
    twin_rows, other_one = after((), twin_rows, other_one)
    w_one = [along_one, *near_one, *far_one, *other_one]
    zero_row = jnp.zeros((heads_cols,), f32)
    biases = jnp.stack(
        [
            jnp.concatenate([q_bias, zero_row, v_bias]),
            jnp.concatenate(
                [far_small[:heads_cols], zero_row, far_small[heads_cols : 2 * heads_cols]]
            ),
        ]
    )[:, None]
    fc1_biases = row(jnp.concatenate([fc1_bias, far_small[2 * heads_cols :]]))
    qkv = project(h1, w_one, biases)
    attn, lse = attend_fwd(qkv)

    near_two, lse_rows = after(attn, near_two, lse.T)
    far_two = start_far(links, near_two)
    other_two = [links.c(piece) for piece in (after(near_two, along_two), *near_two)]
    far_two, other_two, along_three, attn_sent = after((), far_two, other_two, along_three, attn)

    near_three = links.x(along_three), links.y(along_three)
    other_two += [links.c(piece) for piece in far_two]
    twin_attn = links.c(attn_sent)
    other_two, twin_attn = after((), other_two, twin_attn)
    w_two = [along_two, *near_two, *far_two, *other_two]
    y, h2, h2_t = join_heads(attn, x, w_two, hidden_here, outs[0], gains[1], shifts[1])
    hidden, slope = expand(h2, w_two, fc1_biases, hidden_here)
    near_three, hidden, slope, h2_t, along_three = after(
        (), near_three, hidden, slope, h2_t, along_three
    )

    far_three = start_far(links, near_three)
    twin_hidden = links.c(hidden)
    other_three = [links.c(piece) for piece in (along_three, near_three[0])]
    far_three, twin_hidden, other_three, near_three, h2_sent = after(
        (), far_three, twin_hidden, other_three, near_three, h2_t[half:]
    )

    stack = lambda one, two: jnp.concatenate([one[...], two[...]], axis=0)
    join = lambda one, two: jnp.concatenate([one[...], two[...]], axis=1)
    tiles = hidden_here // TILE
    left_at = lambda at: pl.BlockSpec((half, length), lambda s: (at, 0))

    def tile_spec(count):
        def at(s):
            tile = jnp.minimum(s % count, tiles - 1)
            return (0, jnp.where(s < count, tiles, 0) + tile)

        return pl.BlockSpec((length, TILE), at)

    attn_spec = lambda count: pl.BlockSpec((length, TILE), lambda s: (0, 1 - s // count))

    def grad_fc2():
        terms = lambda refs, kind: (join(*refs[:2]), stack(*refs[2:]))
        args = [e_t, twin_rows, hidden, twin_hidden]
        specs = [left_at(0), left_at(0)] + [tile_spec(tiles)] * 2
        return both_sides(args, specs, (0,), terms, "grad_fc2", tiles)

    def grad_two():
        count = tiles + 1

        def terms(refs, kind):
            return join(*refs[4 * kind :][:2]), stack(*refs[4 * kind + 2 :][:2])

        args = [h2_t, twin_h2, du, twin_du, da_t, twin_da, attn, twin_attn]
        specs = [left_at(0)] * 2 + [tile_spec(count)] * 2
        specs += [left_at(0)] * 2 + [attn_spec(count)] * 2
        return both_sides(args, specs, (0, tiles), terms, "grad_two", count)

    def grad_qkv():
        def terms(refs, kind):
            return join(*refs[:2]), jnp.concatenate([refs[2][0], refs[3][0]], axis=0)

        args = [h1_t, twin_rows, dp, twin_dp]
        dp_spec = pl.BlockSpec((1, length, TILE), lambda s: (s % 3, 0, 1 - s // 3))
        specs = [left_at(0), left_at(1)] + [dp_spec] * 2
        return both_sides(args, specs, (0,), terms, "grad_qkv", 3)

    def enter_window(done, *homes):
        for home in homes:
            home.x_got, home.y_got = after(done, home.x_got, home.y_got)

    home_fc2, home_two, home_qkv = Home(links), Home(links), Home(links)

    other_three += [links.c(piece) for piece in (near_three[1], *far_three)]
    twin_h2 = links.c(h2_sent)
    pieces = grad_fc2()
    pieces, other_three, twin_h2 = after((), pieces, other_three, twin_h2)
    w_fc2 = [along_three, *near_three, *far_three, *other_three]

    home_fc2.first(pieces)
    du, fc1b_sum = hidden_back(e, slope, w_fc2)
    mid, da, da_t, second_sums = second_back(du, w_two, hidden_here, y, e, gains[1])
    enter_window(da, home_fc2)
    du, da, da_t, da_t_far = after(home_fc2.x_got, du, da, da_t, da_t[half:])

    twin_du = links.c(du)
    twin_da = links.c(da_t_far)
    home_fc2.second(*home_fc2.middle())
    d_heads = heads_back(da, w_two, hidden_here)
    twin_du, twin_da = after(d_heads, twin_du, twin_da)
    pieces = grad_two()
    pieces, d_heads, home_fc2.y_last, home_fc2.x_last = after(
        (), pieces, d_heads, home_fc2.y_last, home_fc2.x_last
    )

    home_two.first(pieces)
    moved = home_fc2.last(pieces, True)
    dp, q_sums, v_sums = attend_bwd(qkv, after(moved, d_heads), lse_rows)
    grad_near, grad_sent_rows, first_sums = first_back(
        dp, w_one, x, mid, gains[0], order_b
    )
    enter_window(grad_near, home_two)
    dp = after(home_two.x_got, dp)

    twin_dp = links.c(dp)
    home_two.second(*home_two.middle())
    out_near, out_sent = layer_out(after(dp, hidden), w_fc2, y, outs[1], live, order_b)
    twin_dp = after(out_near, twin_dp)
    pieces = grad_qkv()
    pieces, home_two.y_last, home_two.x_last = after(
        (), pieces, home_two.y_last, home_two.x_last
    )

    home_qkv.first(pieces)
    moved = home_two.last(pieces, True)
    enter_window(moved, home_qkv)
    moved, grad_sent_rows = after((), home_qkv.middle(), grad_sent_rows)
    home_qkv.second(*moved)
    grad_got = links.x(grad_sent_rows)
    moved = home_qkv.last((), False)
    out_got = links.x(after(moved, out_sent))

    sums = jnp.concatenate(
        [first_sums[:1], second_sums[:1], first_sums[1:], second_sums[1:]], axis=0
    )
    sums = lax.dot_general(
        sums, order_f, (((1,), (1,)), ((), ())), precision=lax.Precision.HIGHEST
    )

    def placed(both):
        size = both.shape[1] // 2
        return jnp.where(t == 0, both[0], jnp.concatenate([both[0, size:], both[0, :size]]))

    small = [sums.reshape(-1), placed(q_sums), placed(v_sums), placed(fc1b_sum)]
    small = total_over_all(links, jnp.concatenate(small).reshape(-1, 128)).reshape(-1) * grad_scale
    sums = small[: 6 * width].reshape(6, width)
    own = lambda first, size: lax.dynamic_slice_in_dim(small, first + t * size, size, 0)

    g_qkv = home_qkv.value((), grad_scale)
    g_fc2 = home_fc2.value(moved, grad_scale)
    g_two = home_two.value(moved, grad_scale)

    def both_slots(near, got):
        return jnp.where(t == 0, jnp.stack([near, got]), jnp.stack([got, near]))

    return (
        both_slots(out_near, out_got),
        both_slots(grad_near, grad_got).astype(f32),
        g_qkv.reshape(block, 3, heads_cols),
        own(6 * width, heads_cols),
        own(6 * width + 2 * heads_cols, heads_cols),
        g_two[:, hidden_here:].T,
        g_two[:, :hidden_here],
        own(6 * width + 4 * heads_cols, hidden_here),
        g_fc2.T,
        sums[0:2],
        sums[2:4],
        sums[4:6],
    )


def solution(mesh):
    body = own_slot if fits_own_slot(mesh) else shared_slots
    return jax.shard_map(
        body,
        mesh=mesh,
        in_specs=(
            P("wide", "tp", None),
            P("wide", "tp", None),
            P("wide"),
            P("wide", None, "tp"),
            P("tp"),
            P("tp"),
            P("tp", "wide"),
            P("wide", "tp"),
            P("tp"),
            P("tp", "wide"),
            P(),
            P(),
            P(),
        ),
        out_specs=(
            P("wide", "tp", None),
            P("wide", "tp", None),
            P("wide", None, "tp"),
            P("tp"),
            P("tp"),
            P("tp", "wide"),
            P("wide", "tp"),
            P("tp"),
            P("tp", "wide"),
            P(),
            P(),
            P(),
        ),
        check_vma=False,
    )
```

```python
from functools import partial
import math

import jax
import jax.numpy as jnp
from jax import lax
from jax.experimental import pallas as pl
from jax.experimental.pallas import tpu as pltpu
from jax.sharding import PartitionSpec as P

HEAD_DIM = 64


norm_eps = 1e-06
root_half = 1.0 / math.sqrt(2.0)
inv_root_two_pi = 1.0 / math.sqrt(2.0 * math.pi)


def layer_norm(in_rows, gain_row, shift_row):
    row_mean = jnp.mean(in_rows, axis=-1, keepdims=True)
    centred = in_rows - row_mean
    spread = jnp.mean(centred * centred, axis=-1, keepdims=True)
    inverse = lax.rsqrt(spread + norm_eps)
    unit_rows = centred * inverse
    return (unit_rows * gain_row + shift_row, unit_rows, inverse)


def norm_back(grad_rows, unit_rows, inverse, gain_row):
    scaled = grad_rows * gain_row
    mean_one = jnp.mean(scaled, axis=-1, keepdims=True)
    second = jnp.mean(scaled * unit_rows, axis=-1, keepdims=True)
    return inverse * (scaled - mean_one - unit_rows * second)


def contract_last(left_op, right_op):
    return lax.dot_general(
        left_op, right_op, (((1,), (1,)), ((), ())), preferred_element_type=jnp.float32
    )


def contract_first(left_op, right_op):
    return lax.dot_general(
        left_op, right_op, (((0,), (0,)), ((), ())), preferred_element_type=jnp.float32
    )


def attend_block(query, key_rows, value_rows):
    scores = jnp.einsum("qhd,khd->hqk", query, key_rows, preferred_element_type=jnp.float32)
    row_max = jnp.max(scores, axis=-1, keepdims=True)
    weights = jnp.exp(scores - row_max)
    row_sum = jnp.sum(weights, axis=-1, keepdims=True)
    prob_rows = (weights / row_sum).astype(jnp.bfloat16)
    mixed_rows = jnp.einsum(
        "hqk,khd->qhd", prob_rows, value_rows, preferred_element_type=jnp.float32
    )
    return (mixed_rows, row_max[..., 0] + jnp.log(row_sum[..., 0]))


def attend_back(query, grad_rows, log_total, key_rows, value_rows):
    scores = jnp.einsum("qhd,khd->hqk", query, key_rows, preferred_element_type=jnp.float32)
    prob_rows = jnp.exp(scores - log_total[..., None])
    dprobs = jnp.einsum("qhd,khd->hqk", grad_rows, value_rows, preferred_element_type=jnp.float32)
    row_delta = jnp.sum(prob_rows * dprobs, axis=-1, keepdims=True)
    dscores = (prob_rows * (dprobs - row_delta)).astype(jnp.bfloat16)
    dquery = jnp.einsum("hqk,khd->qhd", dscores, key_rows, preferred_element_type=jnp.float32)
    d_keys = jnp.einsum("hqk,qhd->khd", dscores, query, preferred_element_type=jnp.float32)
    dvalues = jnp.einsum(
        "hqk,qhd->khd",
        prob_rows.astype(jnp.bfloat16),
        grad_rows,
        preferred_element_type=jnp.float32,
    )
    return (dquery, d_keys, dvalues)


def shared_slots(
    clips,
    cotangent,
    clip_live,
    qkv_weight,
    q_bias,
    v_bias,
    proj_weight,
    fc1_weight,
    fc1_bias,
    fc2_weight,
    ln_gains,
    ln_biases,
    out_bias,
):
    tp_count = lax.axis_size("tp")
    wide_count = lax.axis_size("wide")
    slot_count, shard_rows, width = clips.shape
    length = shard_rows * tp_count
    local_cols = qkv_weight.shape[2]
    heads_here = local_cols // HEAD_DIM
    hidden_here = fc1_weight.shape[1]
    q_scale = 1.0 / math.sqrt(HEAD_DIM)
    grad_scale = 1.0 / math.sqrt(wide_count * slot_count * length)
    block_rows = 512
    blocks = length // block_rows
    tp_place = lax.axis_index("tp")
    live_slots = clip_live.astype(jnp.float32)
    qv_bias = jnp.stack([q_bias, v_bias])
    own_weights = (qkv_weight, proj_weight, fc1_weight, fc2_weight)

    def one_slot(state_in, inputs):
        rows_in, cot_in, live_one = inputs
        tied_weights = lax.optimization_barrier((own_weights, rows_in))[0]
        w_qkv, w_proj, w_fc1, w_fc2 = (
            lax.all_gather(tied_weights[0], "wide", axis=0, tiled=True),
            lax.all_gather(tied_weights[1], "wide", axis=1, tiled=True),
            lax.all_gather(tied_weights[2], "wide", axis=0, tiled=True),
            lax.all_gather(tied_weights[3], "wide", axis=1, tiled=True),
        )
        x_rows = rows_in.astype(jnp.float32)
        norm_one, unit_one, inv_one = layer_norm(x_rows, ln_gains[0], ln_biases[0])
        h1_full = lax.all_gather(norm_one.astype(jnp.bfloat16), "tp", axis=0, tiled=True)
        qkv_flat = w_qkv.reshape(width, 3 * local_cols)
        projected = jnp.dot(h1_full, qkv_flat, preferred_element_type=jnp.float32).reshape(
            length, 3, local_cols
        )
        query = (
            ((projected[:, 0] + qv_bias[0]) * q_scale)
            .astype(jnp.bfloat16)
            .reshape(length, heads_here, HEAD_DIM)
        )
        key_rows = projected[:, 1].astype(jnp.bfloat16).reshape(length, heads_here, HEAD_DIM)
        value_rows = (
            (projected[:, 2] + qv_bias[1])
            .astype(jnp.bfloat16)
            .reshape(length, heads_here, HEAD_DIM)
        )
        query_blocks = query.reshape(blocks, block_rows, heads_here, HEAD_DIM)
        mixed_blocks, log_totals = lax.map(
            partial(attend_block, key_rows=key_rows, value_rows=value_rows), query_blocks
        )
        attn_out = mixed_blocks.reshape(length, local_cols).astype(jnp.bfloat16)
        attn_sum = lax.psum_scatter(
            jnp.dot(attn_out, w_proj, preferred_element_type=jnp.float32),
            "tp",
            scatter_dimension=0,
            tiled=True,
        )
        mid_rows = x_rows + attn_sum + out_bias[0]
        norm_two, unit_two, inv_two = layer_norm(mid_rows, ln_gains[1], ln_biases[1])
        h2_full = lax.all_gather(norm_two.astype(jnp.bfloat16), "tp", axis=0, tiled=True)
        pre_act = jnp.dot(h2_full, w_fc1, preferred_element_type=jnp.float32) + fc1_bias
        cdf_part = 0.5 * (1.0 + lax.erf(pre_act * root_half))
        hidden = (pre_act * cdf_part).astype(jnp.bfloat16)
        mlp_sum = lax.psum_scatter(
            jnp.dot(hidden, w_fc2, preferred_element_type=jnp.float32).astype(jnp.bfloat16),
            "tp",
            scatter_dimension=0,
            tiled=True,
        ).astype(jnp.float32)
        block_out = (live_one * (mid_rows + mlp_sum + out_bias[1])).astype(jnp.bfloat16)
        out_grad = live_one * cot_in.astype(jnp.float32)
        out_full = lax.all_gather(out_grad.astype(jnp.bfloat16), "tp", axis=0, tiled=True)
        g_fc2 = contract_first(hidden, out_full)
        act_grad = contract_last(out_full, w_fc2)
        slope = cdf_part + pre_act * jnp.exp(-0.5 * pre_act * pre_act) * inv_root_two_pi
        pre_grad = act_grad * slope
        pre_grad_b = pre_grad.astype(jnp.bfloat16)
        g_fc1 = contract_first(h2_full, pre_grad_b)
        g_fc1b = jnp.sum(pre_grad, axis=0)
        norm_two_grad = lax.psum_scatter(
            contract_last(pre_grad_b, w_fc1), "tp", scatter_dimension=0, tiled=True
        )
        mid_grad = out_grad + norm_back(norm_two_grad, unit_two, inv_two, ln_gains[1])
        attn_full = lax.all_gather(mid_grad.astype(jnp.bfloat16), "tp", axis=0, tiled=True)
        g_proj = contract_first(attn_out, attn_full)
        mixed_grad = (
            contract_last(attn_full, w_proj)
            .astype(jnp.bfloat16)
            .reshape(blocks, block_rows, heads_here, HEAD_DIM)
        )

        def back_block(block_state, pieces):
            query_b, grad_b, lse_b = pieces
            d_query, d_keys, d_values = attend_back(query_b, grad_b, lse_b, key_rows, value_rows)
            return ((block_state[0] + d_keys, block_state[1] + d_values), d_query)

        empty_kv = jnp.zeros((length, heads_here, HEAD_DIM), jnp.float32)
        (key_grad, value_grad), query_grad = lax.scan(
            back_block, (empty_kv, empty_kv), (query_blocks, mixed_grad, log_totals)
        )
        query_grad = query_grad.reshape(length, local_cols) * q_scale
        key_grad = key_grad.reshape(length, local_cols)
        value_grad = value_grad.reshape(length, local_cols)
        g_qvb = jnp.stack([jnp.sum(query_grad, axis=0), jnp.sum(value_grad, axis=0)])
        proj_grads = (
            jnp.stack([query_grad, key_grad, value_grad], axis=1)
            .astype(jnp.bfloat16)
            .reshape(length, 3 * local_cols)
        )
        g_qkv = contract_first(h1_full, proj_grads).reshape(width, 3, local_cols)
        norm_one_grad = lax.psum_scatter(
            contract_last(proj_grads, qkv_flat).astype(jnp.bfloat16),
            "tp",
            scatter_dimension=0,
            tiled=True,
        ).astype(jnp.float32)
        in_grad = mid_grad + norm_back(norm_one_grad, unit_one, inv_one, ln_gains[0])
        gain_part = jnp.stack(
            [jnp.sum(norm_one_grad * unit_one, axis=0), jnp.sum(norm_two_grad * unit_two, axis=0)]
        )
        shift_part = jnp.stack([jnp.sum(norm_one_grad, axis=0), jnp.sum(norm_two_grad, axis=0)])
        bias_part = jnp.stack([jnp.sum(mid_grad, axis=0), jnp.sum(out_grad, axis=0)])
        summed = (
            lax.psum_scatter(
                g_qkv.astype(jnp.bfloat16), "wide", scatter_dimension=0, tiled=True
            ).astype(jnp.float32),
            lax.psum_scatter(
                g_proj.astype(jnp.bfloat16), "wide", scatter_dimension=1, tiled=True
            ).astype(jnp.float32),
            lax.psum_scatter(
                g_fc1.astype(jnp.bfloat16), "wide", scatter_dimension=0, tiled=True
            ).astype(jnp.float32),
            lax.psum_scatter(
                g_fc2.astype(jnp.bfloat16), "wide", scatter_dimension=1, tiled=True
            ).astype(jnp.float32),
        )
        weight_acc = jax.tree.map(jnp.add, state_in[0], summed)
        vector_acc = jax.tree.map(
            jnp.add, state_in[1], (gain_part, shift_part, bias_part, g_qvb, g_fc1b)
        )
        return ((weight_acc, vector_acc), (block_out, in_grad))

    weight_zero = tuple((jnp.zeros(shard_in.shape, jnp.float32) for shard_in in own_weights))
    vector_zero = (
        jnp.zeros((2, width), jnp.float32),
        jnp.zeros((2, width), jnp.float32),
        jnp.zeros((2, width), jnp.float32),
        jnp.zeros((2, local_cols), jnp.float32),
        jnp.zeros((hidden_here,), jnp.float32),
    )
    (weight_sums, vector_acc), (block_out, clips_grad) = lax.scan(
        one_slot, (weight_zero, vector_zero), (clips, cotangent, live_slots)
    )
    gain_acc, shift_acc, bias_acc, qvb_acc, fc1b_acc = vector_acc
    qvb_pad = lax.dynamic_update_slice(
        jnp.zeros((2, width), jnp.float32), qvb_acc, (0, tp_place * local_cols)
    )
    fc1b_pad = lax.dynamic_update_slice(
        jnp.zeros((hidden_here * tp_count,), jnp.float32), fc1b_acc, (tp_place * hidden_here,)
    )
    gain_sum, shift_sum, bias_sum, qvb_sum, fc1b_sum = lax.psum(
        (gain_acc, shift_acc, bias_acc, qvb_pad, fc1b_pad), ("wide", "tp")
    )
    qvb_own = lax.dynamic_slice_in_dim(qvb_sum, tp_place * local_cols, local_cols, 1)
    fc1b_own = lax.dynamic_slice_in_dim(fc1b_sum, tp_place * hidden_here, hidden_here, 0)
    return (
        block_out,
        clips_grad,
        weight_sums[0] * grad_scale,
        qvb_own[0] * grad_scale,
        qvb_own[1] * grad_scale,
        weight_sums[1] * grad_scale,
        weight_sums[2] * grad_scale,
        fc1b_own * grad_scale,
        weight_sums[3] * grad_scale,
        gain_sum * grad_scale,
        shift_sum * grad_scale,
        bias_sum * grad_scale,
    )


AXES = ("wide", "tp")
PAIR = 128
TILE = 512
MIB = 1024 * 1024
GRANT = {"project": 60, "hidden_back": 60, "heads_back": 60, "layer_out": 60}
WIDE = 1024
bf16 = jnp.bfloat16
f32 = jnp.float32


def fits_own_slot(mesh):
    return mesh.shape["tp"] == 2 and mesh.shape["wide"] % 4 == 0


def nt_dot(left_op, right_op):
    return lax.dot_general(
        left_op, right_op, (((1,), (1,)), ((), ())), preferred_element_type=f32
    )


def nn_dot(left_op, right_op):
    return lax.dot_general(
        left_op, right_op, (((1,), (0,)), ((), ())), preferred_element_type=f32
    )


def kernel_call(body, name, grid, in_specs, out_specs, out_shape, scratch=(), scalars=0):
    return pl.pallas_call(
        body,
        grid_spec=pltpu.PrefetchScalarGridSpec(
            num_scalar_prefetch=scalars,
            grid=grid,
            in_specs=in_specs,
            out_specs=out_specs,
            scratch_shapes=list(scratch),
        ),
        out_shape=out_shape,
        compiler_params=pltpu.CompilerParams(vmem_limit_bytes=GRANT.get(name, 60) * MIB),
        cost_estimate=pl.CostEstimate(flops=1, bytes_accessed=1, transcendentals=0),
        name=name,
    )


def whole(shape):
    return pl.BlockSpec(shape, lambda *at: (0,) * len(shape))


def array(*shape, dtype=bf16):
    return jax.ShapeDtypeStruct(shape, dtype)


def norm_stats(rows):
    row_mean = jnp.mean(rows, axis=-1, keepdims=True)
    centred = rows - row_mean
    spread = jnp.mean(centred * centred, axis=-1, keepdims=True)
    inverse = lax.rsqrt(spread + norm_eps)
    return centred * inverse, inverse


NEAR = (0, 2, 5, 7)
FAR = (1, 3, 4, 6, 8, 9)


class Pieces:
    def __init__(self, pieces, columns, first=0, tile=WIDE):
        self.pieces, self.columns, self.first = pieces, columns, first
        self.tile = min(tile, columns)
        self.tiles = columns // self.tile
        self.args = list(pieces)
        self.specs = [pl.BlockSpec(memory_space=pl.ANY)] * len(pieces)
        rows = sum(pieces[i].shape[0] for i in NEAR)
        self.scratch = [
            pltpu.VMEM((2, rows, columns), bf16),
            pltpu.SemaphoreType.DMA((self.tiles, len(pieces))),
        ]

    def copies(self, refs, side, tile, w_ref, sems):
        at, found = 0, []
        for index in FAR if side else NEAR:
            rows = self.pieces[index].shape[0]
            found.append(
                pltpu.make_async_copy(
                    refs[index].at[:, pl.ds(self.first + tile * self.tile, self.tile)],
                    w_ref.at[side, pl.ds(at, rows), pl.ds(tile * self.tile, self.tile)],
                    sems.at[tile, index],
                )
            )
            at += rows
        return found

    def start(self, refs, w_ref, sems):
        for side in range(2):
            for tile in range(self.tiles):
                for copy in self.copies(refs, side, tile, w_ref, sems):
                    copy.start()

    def wait(self, refs, side, tile, w_ref, sems):
        for copy in self.copies(refs, side, tile, w_ref, sems):
            copy.wait()

    def get(self, refs, side, tile, w_ref, sems):
        self.wait(refs, side, tile, w_ref, sems)
        return w_ref[side, :, pl.ds(tile * self.tile, self.tile)]

    def each_step(self, step, refs, w_ref, sems, work):
        pl.when(step == 0)(lambda: self.start(refs, w_ref, sems))
        for side in range(2):
            for tile in range(self.tiles):

                @pl.when(step == side * self.tiles + tile)
                def _():
                    work(side, tile, self.get(refs, side, tile, w_ref, sems))


def enter_kernel(own_ref, got_ref, order_ref, gain_ref, shift_ref, x_ref, h_ref, ht_ref):
    half = own_ref.shape[0]
    for part, ref in enumerate((own_ref, got_ref)):
        rows = nn_dot(ref[...], order_ref[...])
        here = pl.ds(part * half, half)
        x_ref[here, :] = rows.astype(bf16)
        unit, _ = norm_stats(rows)
        normed = (unit * gain_ref[...] + shift_ref[...]).astype(bf16)
        h_ref[here, :] = normed
        ht_ref[:, here] = normed.T


def enter(own, got, order_b, gain, shift):
    half, width = own.shape
    length = 2 * half
    return kernel_call(
        enter_kernel,
        "enter",
        (1,),
        [whole((half, width))] * 2 + [whole((width, width))] + [whole((1, width))] * 2,
        [whole((length, width))] * 2 + [whole((width, length))],
        [array(length, width)] * 2 + [array(width, length)],
    )(own, got, order_b, gain, shift)


def cot_kernel(own_ref, got_ref, order_ref, live_ref, e_ref, et_ref):
    half = own_ref.shape[0]
    for part, ref in enumerate((own_ref, got_ref)):
        rows = (live_ref[...] * nn_dot(ref[...], order_ref[...])).astype(bf16)
        here = pl.ds(part * half, half)
        e_ref[here, :] = rows
        et_ref[:, here] = rows.T


def enter_cot(own, got, order_b, live):
    half, width = own.shape
    length = 2 * half
    return kernel_call(
        cot_kernel,
        "enter_cot",
        (1,),
        [whole((half, width))] * 2 + [whole((width, width)), whole((1, width))],
        [whole((length, width)), whole((width, length))],
        [array(length, width), array(width, length)],
    )(own, got, order_b, live)


def project(h, pieces, biases):
    length, width = h.shape
    each = pieces[0].shape[1] // 3
    load = Pieces(pieces, 3 * each, 0, each)
    scales = (1.0 / math.sqrt(HEAD_DIM), None, None)

    def body(h_ref, bias_ref, *refs):
        refs, (out_ref, w_ref, sems) = refs[:-3], refs[-3:]

        def work(side, tile, weight):
            acc = nn_dot(h_ref[...], weight) + bias_ref[0]
            out_ref[0] = (acc if scales[tile] is None else acc * scales[tile]).astype(bf16)

        load.each_step(pl.program_id(0), refs, w_ref, sems, work)

    return kernel_call(
        body,
        "project",
        (6,),
        [whole((length, width)), pl.BlockSpec((1, 1, each), lambda s: (s // 3, 0, s % 3))]
        + load.specs,
        pl.BlockSpec((1, length, each), lambda s: (s % 3, 0, s // 3)),
        array(3, length, width),
        load.scratch,
    )(h, biases, *load.args)


def attend_kernel(q_ref, k_ref, v_ref, o_ref, lse_ref):
    pair = pl.program_id(0)
    rows = q_ref.shape[1]
    lanes = lax.broadcasted_iota(jnp.int32, (rows, PAIR), 1)
    keys = k_ref[0]
    values = v_ref[0]
    total = jnp.zeros((rows, PAIR), f32)
    for half in range(2):
        mask = (lanes // HEAD_DIM) == half
        query = jnp.where(mask, q_ref[0], jnp.zeros_like(keys))
        scores = nt_dot(query, keys)
        row_max = jnp.max(scores, axis=-1, keepdims=True)
        weights = jnp.exp(scores - row_max)
        row_sum = jnp.sum(weights, axis=-1, keepdims=True)
        probs = (weights * (1.0 / row_sum)).astype(bf16)
        mixed = nn_dot(probs, values)
        total = jnp.where(mask, mixed, total)
        lse = row_max + jnp.log(row_sum)
        lse_ref[...] = jnp.where(lanes == 2 * pair + half, lse, lse_ref[...])
    o_ref[...] = total.astype(bf16)


def head_spec(length, index):
    return pl.BlockSpec((1, length, PAIR), lambda i: (index, 0, i))


def attend_fwd(qkv):
    _, length, width = qkv.shape
    return kernel_call(
        attend_kernel,
        "attend_fwd",
        (width // PAIR,),
        [head_spec(length, j) for j in range(3)],
        [pl.BlockSpec((length, PAIR), lambda i: (0, i)), whole((length, PAIR))],
        [array(length, width), array(length, PAIR, dtype=f32)],
    )(qkv, qkv, qkv)


def join_heads(attn, x, pieces, first, bias, gain, shift):
    length, width = x.shape
    load = Pieces(pieces, TILE, first)

    def body(attn_ref, x_ref, bias_ref, gain_ref, shift_ref, *refs):
        refs, (y_ref, h_ref, ht_ref, w_ref, sems) = refs[:-5], refs[-5:]
        load.start(refs, w_ref, sems)
        load.wait(refs, 0, 0, w_ref, sems)
        load.wait(refs, 1, 0, w_ref, sems)
        half = length // 2
        for part in range(2):
            here = pl.ds(part * half, half)
            rows = nt_dot(attn_ref[here, :TILE], w_ref[0]) + nt_dot(attn_ref[here, TILE:], w_ref[1])
            rows = x_ref[here, :].astype(f32) + rows + bias_ref[...]
            y_ref[here, :] = rows
            unit, _ = norm_stats(rows)
            normed = (unit * gain_ref[...] + shift_ref[...]).astype(bf16)
            h_ref[here, :] = normed
            ht_ref[:, here] = normed.T

    return kernel_call(
        body,
        "join_heads",
        (1,),
        [whole((length, width))] * 2 + [whole((1, width))] * 3 + load.specs,
        [whole((length, width))] * 2 + [whole((width, length))],
        [array(length, width, dtype=f32), array(length, width), array(width, length)],
        load.scratch,
    )(attn, x, bias, gain, shift, *load.args)


def expand(h, pieces, bias, hidden):
    length, width = h.shape
    load = Pieces(pieces, hidden)

    def body(h_ref, bias_ref, *refs):
        refs, (g_ref, slope_ref, w_ref, sems) = refs[:-4], refs[-4:]

        def work(side, tile, weight):
            pre = nn_dot(h_ref[...], weight) + bias_ref[...]
            cdf = 0.5 * (1.0 + lax.erf(pre * root_half))
            g_ref[...] = (pre * cdf).astype(bf16)
            density = jnp.exp(-0.5 * pre * pre) * inv_root_two_pi
            slope_ref[...] = (cdf + pre * density).astype(bf16)

        load.each_step(pl.program_id(0), refs, w_ref, sems, work)

    block = pl.BlockSpec((length, WIDE), lambda s: (0, s))
    return kernel_call(
        body,
        "expand",
        (2 * load.tiles,),
        [whole((length, width)), pl.BlockSpec((1, WIDE), lambda s: (0, s))] + load.specs,
        [block] * 2,
        [array(length, 2 * hidden)] * 2,
        load.scratch,
    )(h, bias, *load.args)


def hidden_back(e, slope, pieces):
    length, width = e.shape
    hidden = pieces[0].shape[1]
    load = Pieces(pieces, hidden)

    def body(e_ref, slope_ref, *refs):
        refs, (du_ref, sum_ref, w_ref, sems) = refs[:-4], refs[-4:]

        def work(side, tile, weight):
            du = nn_dot(e_ref[...], weight) * slope_ref[...].astype(f32)
            du_ref[...] = du.astype(bf16)
            sum_ref[...] = jnp.sum(du, axis=0, keepdims=True)

        load.each_step(pl.program_id(0), refs, w_ref, sems, work)

    block = pl.BlockSpec((length, WIDE), lambda s: (0, s))
    row = pl.BlockSpec((1, WIDE), lambda s: (0, s))
    return kernel_call(
        body,
        "hidden_back",
        (2 * load.tiles,),
        [whole((length, width)), block] + load.specs,
        [block, row],
        [array(length, 2 * hidden), array(1, 2 * hidden, dtype=f32)],
        load.scratch,
    )(e, slope, *load.args)


def heads_back(da, pieces, first):
    length, width = da.shape
    load = Pieces(pieces, TILE, first)

    def body(da_ref, *refs):
        refs, (out_ref, w_ref, sems) = refs[:-3], refs[-3:]
        load.start(refs, w_ref, sems)
        for side in range(2):
            load.wait(refs, side, 0, w_ref, sems)
            out_ref[:, pl.ds(side * TILE, TILE)] = nn_dot(da_ref[...], w_ref[side]).astype(bf16)

    return kernel_call(
        body,
        "heads_back",
        (1,),
        [whole((length, width))] + load.specs,
        whole((length, 2 * TILE)),
        array(length, 2 * TILE),
        load.scratch,
    )(da, *load.args)


def contract_back(rows, rows_specs, left_of, load, extras, finish, name, outs):
    count = len(extras)
    length, width = extras[0].shape

    def body(*refs):
        rows_refs, refs = refs[: len(rows)], refs[len(rows) :]
        extra_refs, refs = refs[:count], refs[count:]
        w_refs, refs = refs[: len(load.args)], refs[len(load.args) :]
        out_refs, refs = refs[: len(outs)], refs[len(outs) :]
        w_ref, sems, acc_ref, extra_sems = refs[:4]
        held = refs[4:]
        copies = [
            pltpu.make_async_copy(source, target, extra_sems.at[i])
            for i, (source, target) in enumerate(zip(extra_refs, held))
        ]

        def work(side, tile, weight):
            term = nt_dot(left_of(rows_refs), weight)
            if side == 0 and tile == 0:
                for copy in copies:
                    copy.start()
                acc_ref[...] = term
            else:
                acc_ref[...] += term
            if side == 1 and tile == load.tiles - 1:
                for copy in copies:
                    copy.wait()
                finish(acc_ref, held, out_refs)

        load.each_step(pl.program_id(0), w_refs, w_ref, sems, work)

    return kernel_call(
        body,
        name,
        (2 * load.tiles,),
        rows_specs + [pl.BlockSpec(memory_space=pl.ANY)] * count + load.specs,
        [whole(o.shape) for o in outs],
        outs,
        load.scratch
        + [pltpu.VMEM((length, width), f32), pltpu.SemaphoreType.DMA((count,))]
        + [pltpu.VMEM(extra.shape, extra.dtype) for extra in extras],
    )(*rows, *extras, *load.args)


def to_home(rows, order_ref):
    return nt_dot(rows.astype(bf16), order_ref[...]).astype(bf16)


def layer_out(hidden, pieces, y, bias, live, order_b):
    length, width = y.shape
    half = length // 2

    def finish(acc_ref, ins, outs):
        y_ref, bias_ref, live_ref, order_ref = ins
        for part in range(2):
            here = pl.ds(part * half, half)
            rows = live_ref[...] * (y_ref[here, :] + acc_ref[here, :] + bias_ref[...])
            outs[part][...] = to_home(rows, order_ref)

    return contract_back(
        [hidden],
        [pl.BlockSpec((length, WIDE), lambda s, *_: (0, s))],
        lambda refs: refs[0][...],
        Pieces(pieces, pieces[0].shape[1]),
        (y, bias, live, order_b),
        finish,
        "layer_out",
        [array(half, width)] * 2,
    )


def second_back(du, pieces, hidden, y, e, gain):
    length, width = y.shape
    half = length // 2

    def finish(acc_ref, ins, outs):
        y_ref, e_ref, gain_ref = ins
        mid_ref, da_ref, dat_ref, dat_far_ref, sum_ref = outs
        sums = [jnp.zeros((1, width), f32)] * 4
        for part in range(2):
            here = pl.ds(part * half, half)
            unit, inverse = norm_stats(y_ref[here, :])
            grad = acc_ref[here, :]
            e_rows = e_ref[here, :].astype(f32)
            mid = e_rows + norm_back(grad, unit, inverse, gain_ref[...])
            mid_ref[here, :] = mid
            mid_b = mid.astype(bf16)
            da_ref[here, :] = mid_b
            dat_ref[:, here] = mid_b[:, : width // 2].T
            dat_far_ref[:, here] = mid_b[:, width // 2 :].T
            terms = (grad * unit, grad, mid, e_rows)
            sums = [s + jnp.sum(term, axis=0, keepdims=True) for s, term in zip(sums, terms)]
        sum_ref[...] = jnp.concatenate(sums, axis=0)

    return contract_back(
        [du],
        [pl.BlockSpec((length, WIDE), lambda s: (0, s))],
        lambda refs: refs[0][...],
        Pieces(pieces, hidden),
        (y, e, gain),
        finish,
        "second_back",
        [
            array(length, width, dtype=f32),
            array(length, width),
            array(width // 2, length),
            array(width // 2, length),
            array(4, width, dtype=f32),
        ],
    )


def first_back(dp, pieces, x, mid, gain, order_b):
    length, width = x.shape
    half = length // 2

    def finish(acc_ref, ins, outs):
        x_ref, mid_ref, gain_ref, order_ref = ins
        sum_ref = outs[2]
        sums = [jnp.zeros((1, width), f32)] * 2
        for part in range(2):
            here = pl.ds(part * half, half)
            unit, inverse = norm_stats(x_ref[here, :].astype(f32))
            grad = acc_ref[here, :]
            rows = mid_ref[here, :] + norm_back(grad, unit, inverse, gain_ref[...])
            outs[part][...] = to_home(rows, order_ref)
            terms = (grad * unit, grad)
            sums = [s + jnp.sum(term, axis=0, keepdims=True) for s, term in zip(sums, terms)]
        sum_ref[...] = jnp.concatenate(sums, axis=0)

    return contract_back(
        [dp],
        [pl.BlockSpec((3, length, width // 2), lambda s: (0, 0, s))],
        lambda refs: jnp.concatenate([refs[0][j] for j in range(3)], axis=1),
        Pieces(pieces, pieces[0].shape[1], 0, pieces[0].shape[1]),
        (x, mid, gain, order_b),
        finish,
        "first_back",
        [array(half, width)] * 2 + [array(2, width, dtype=f32)],
    )


def attend_back_kernel(q_ref, k_ref, v_ref, g_ref, lse_ref, dp_ref, qs_ref, vs_ref):
    pair = pl.program_id(0)
    rows = q_ref.shape[1]
    lanes = lax.broadcasted_iota(jnp.int32, (rows, PAIR), 1)
    sub = lax.broadcasted_iota(jnp.int32, (PAIR, rows), 0)
    query = q_ref[0]
    keys = k_ref[0]
    values = v_ref[0]
    grads = g_ref[...]
    blank = jnp.zeros_like(keys)
    keys_t = keys.T
    dq_t = jnp.zeros((PAIR, rows), f32)
    dk = jnp.zeros((rows, PAIR), f32)
    dv = jnp.zeros((rows, PAIR), f32)
    for half in range(2):
        mask = (lanes // HEAD_DIM) == half
        scores_t = nt_dot(jnp.where(mask, keys, blank), query)
        lse = lse_ref[pl.ds(2 * pair + half, 1), :]
        probs_t = jnp.exp(scores_t - lse)
        dprobs_t = nt_dot(jnp.where(mask, values, blank), grads)
        delta = jnp.sum(probs_t * dprobs_t, axis=0, keepdims=True)
        ds_t = (probs_t * (dprobs_t - delta)).astype(bf16)
        dv = jnp.where(mask, nn_dot(probs_t.astype(bf16), grads), dv)
        dk = jnp.where(mask, nn_dot(ds_t, query), dk)
        dq_t = jnp.where((sub // HEAD_DIM) == half, nn_dot(keys_t, ds_t), dq_t)
    dq = dq_t.T * (1.0 / math.sqrt(HEAD_DIM))
    dp_ref[0] = dq.astype(bf16)
    dp_ref[1] = dk.astype(bf16)
    dp_ref[2] = dv.astype(bf16)
    qs_ref[...] = jnp.sum(dq, axis=0, keepdims=True)
    vs_ref[...] = jnp.sum(dv, axis=0, keepdims=True)


def attend_bwd(qkv, grads, lse_rows):
    _, length, width = qkv.shape
    row = pl.BlockSpec((1, PAIR), lambda i: (0, i))
    sums = array(1, width, dtype=f32)
    return kernel_call(
        attend_back_kernel,
        "attend_bwd",
        (width // PAIR,),
        [head_spec(length, j) for j in range(3)]
        + [pl.BlockSpec((length, PAIR), lambda i: (0, i)), whole((PAIR, length))],
        [pl.BlockSpec((3, length, PAIR), lambda i: (0, 0, i)), row, row],
        [array(3, length, width), sums, sums],
    )(qkv, qkv, qkv, grads, lse_rows)


def both_sides(args, specs, kinds, terms, name, tiles, z_first=0):
    count = len(args)
    half = args[0].shape[0] // 2
    mid = half // 4
    kept = tiles - 1 if z_first else tiles

    def body(*refs):
        x_ref, y_ref, k10_ref, k00_ref, k01_ref = refs[count : count + 5]
        step = pl.program_id(0)

        def apart(kind):
            left, right = terms(refs[:count], kind)
            acc = nn_dot(left, right).astype(bf16)
            size = acc.shape[0] // 2 // z_first
            for z in range(z_first):
                for ky in range(2):
                    first = (ky * z_first + z) * size
                    refs[-1][z, 0, pl.ds(ky * size, size), :] = acc[first : first + size]

        def run(kind, side):
            left, right = terms(refs[:count], kind)
            acc = nn_dot(left, right).astype(bf16)
            y_ref[...] = acc[3 * mid :]
            if side:
                x_ref[pl.ds(0, mid), :] = acc[:mid]
                x_ref[pl.ds(mid, mid), :] = acc[2 * mid : 3 * mid]
                k10_ref[...] = acc[mid : 2 * mid]
            else:
                k00_ref[...] = acc[: 2 * mid]
                k01_ref[...] = acc[2 * mid : 3 * mid]

        for side in range(2):
            for kind, first in enumerate(kinds):
                last = kinds[kind + 1] if kind + 1 < len(kinds) else tiles
                base = 0 if side else tiles
                here = (step >= base + first) & (step < base + min(last, kept))
                pl.when(here)(partial(run, kind, side))
        if z_first:
            pl.when(step % tiles == tiles - 1)(partial(apart, len(kinds) - 1))

    most = kept - 1
    far = lambda size: pl.BlockSpec((size, TILE), lambda s: (0, jnp.minimum(s, most)))
    near = lambda size: pl.BlockSpec(
        (size, TILE), lambda s: (0, jnp.minimum(jnp.maximum(s - tiles, 0), most))
    )
    both = pl.BlockSpec((mid, TILE), lambda s: (s // tiles, jnp.minimum(s % tiles, most)))
    sizes = (2 * mid, 2 * mid, mid, 2 * mid, mid)
    out_specs = [far(2 * mid), both, far(mid), near(2 * mid), near(mid)]
    shapes = [array(size, kept * TILE) for size in sizes]
    if z_first:
        each = half // z_first
        out_specs.append(
            pl.BlockSpec((z_first, 1, each, TILE), lambda s: (0, 1 - s // tiles, 0, 0))
        )
        shapes.append(array(z_first, 2, each, TILE))
    return kernel_call(body, name, (2 * tiles,), specs, out_specs, shapes)(*args)


def add_mid_kernel(k01_ref, rx_ref, k10_ref, ry_ref, y_ref, x_ref):
    half = k01_ref.shape[0]
    y_ref[...] = (k01_ref[...].astype(f32) + rx_ref[pl.ds(half, half), :].astype(f32)).astype(bf16)
    x_ref[...] = (k10_ref[...].astype(f32) + ry_ref[pl.ds(0, half), :].astype(f32)).astype(bf16)


def add_last_kernel(k00_ref, rx_ref, ry_ref, y2_ref, x2_ref, out_ref):
    half = y2_ref.shape[0]
    top, low = pl.ds(0, half), pl.ds(half, half)
    near = (rx_ref[top, :], y2_ref[...]), (ry_ref[low, :], x2_ref[...])
    for here, (one, two) in zip((top, low), near):
        total = k00_ref[here, :].astype(f32) + one.astype(f32) + two.astype(f32)
        out_ref[here, :] = total.astype(bf16)


def small_call(body, name, args, shapes):
    out_specs = [whole(s.shape) for s in shapes]
    return kernel_call(body, name, (1,), [whole(a.shape) for a in args], out_specs, shapes)(*args)


class Links:
    def __init__(self):
        self.nz = lax.axis_size("wide") // 4
        self.across = self.table(lambda z, y, c, x: (z, y, c, 1 - x))
        self.beside = self.table(lambda z, y, c, x: (z, 1 - y, c, x))
        self.twin = self.table(lambda z, y, c, x: (z, y, 1 - c, x))

    def table(self, source):
        pairs = []
        for z in range(self.nz):
            for y in range(2):
                for c in range(2):
                    for x in range(2):
                        zs, ys, cs, xs = source(z, y, c, x)
                        pairs.append(
                            (((zs * 2 + ys) * 2 + cs) * 2 + xs, ((z * 2 + y) * 2 + c) * 2 + x)
                        )
        return pairs

    def from_z(self, rows, step):
        shift = self.table(lambda z, y, c, x: ((z + step) % self.nz, y, c, x))
        return lax.ppermute(rows, AXES, shift)

    def z_groups(self):
        rest = [(y, c, x) for y in range(2) for c in range(2) for x in range(2)]
        return [
            [((z * 2 + y) * 2 + c) * 2 + x for z in range(self.nz)] for y, c, x in rest
        ]

    def z_sum_apart(self, rows):
        return lax.psum_scatter(
            rows, AXES, scatter_dimension=0, tiled=True, axis_index_groups=self.z_groups()
        )

    def z_sum(self, rows):
        got = lax.all_to_all(rows, AXES, 0, 0, tiled=True, axis_index_groups=self.z_groups())
        return got.reshape(self.nz, -1, rows.shape[1])

    def z_all(self, rows):
        return lax.all_gather(
            rows, AXES, axis=0, tiled=True, axis_index_groups=self.z_groups()
        )

    def x(self, rows):
        return lax.ppermute(rows, AXES, self.across)

    def y(self, rows):
        return lax.ppermute(rows, AXES, self.beside)

    def c(self, rows):
        return lax.ppermute(rows, AXES, self.twin)

    def flip(self, rows, bit):
        swap = self.table(lambda z, y, c, x: (z ^ bit, y, c, x))
        return lax.ppermute(rows, AXES, swap)


def after(done, *values):
    out = lax.optimization_barrier((values, done))[0]
    return out if len(values) > 1 else out[0]


def start_far(links, near):
    by_x, by_y = near
    cut = by_x.shape[0] // 2
    return links.x(by_y[:cut]), links.y(by_x[cut:])


class Home:
    def __init__(self, links):
        self.links = links

    def first(self, pieces):
        x_first, y_first, self.k10_low, self.k00, self.k01_top = pieces
        self.x_got, self.y_got = self.links.x(x_first), self.links.y(y_first)

    def middle(self):
        half = self.k01_top.shape[0]
        args = (self.k01_top, self.x_got, self.k10_low, self.y_got)
        shape = array(*self.k01_top.shape)
        out_y, out_x = small_call(add_mid_kernel, "add_mid", args, [shape, shape])
        return out_y, out_x

    def second(self, out_y, out_x):
        self.y_last, self.x_last = self.links.y(out_y), self.links.x(out_x)

    def last(self, done, apart):
        y_last, x_last = after(done, self.y_last, self.x_last)
        args = (self.k00, self.x_got, self.y_got, y_last, x_last)
        (total,) = small_call(add_last_kernel, "add_last", args, [array(*self.k00.shape)])
        self.home = self.links.z_sum_apart(total)[None] if apart else self.links.z_sum(total)
        return total

    def value(self, done, scale):
        return jnp.sum(after(done, self.home).astype(f32), axis=0) * scale


def own_slot(
    clips,
    cotangent,
    clip_live,
    qkv_weight,
    q_bias,
    v_bias,
    proj_weight,
    fc1_weight,
    fc1_bias,
    fc2_weight,
    ln_gains,
    ln_biases,
    out_bias,
):
    links = Links()
    slot_count, shard_rows, width = clips.shape
    wide_count = lax.axis_size("wide")
    length = 2 * shard_rows
    block = qkv_weight.shape[0]
    heads_cols = qkv_weight.shape[2]
    hidden_here = fc1_weight.shape[1]
    grad_scale = 1.0 / math.sqrt(wide_count * slot_count * length)
    wide_at = lax.axis_index("wide")
    t = lax.axis_index("tp")
    z_at, y_at, c_at = wide_at // 4, (wide_at // 2) % 2, wide_at % 2
    qkv_cols = 3 * heads_cols
    pick = lambda both, at: lax.dynamic_index_in_dim(both, at, 0, keepdims=False)
    row = lambda vector: vector.reshape(1, -1)

    sent_rows = jnp.concatenate([pick(clips, 1 - t), pick(cotangent, 1 - t)], axis=0)
    q_shard, sent_rows = after((), qkv_weight.reshape(block, qkv_cols), sent_rows)
    two_shard = jnp.concatenate([fc1_weight, proj_weight.T], axis=1)
    along_two = links.z_all(two_shard)
    steps_one = [links.from_z(q_shard, k) for k in range(1, links.nz)]
    got_rows = links.x(sent_rows)
    far_small = jnp.concatenate([q_bias, v_bias, fc1_bias]).reshape(-1, 128)
    far_small = links.x(far_small).reshape(-1)

    spot = jnp.arange(width)
    rel = spot // block
    kc, ky, kz = rel // (2 * links.nz), (rel // links.nz) % 2, rel % links.nz
    home = (kz * 2 + (y_at ^ ky)) * 2 + (c_at ^ kc)
    order = spot[:, None] == (home * block + spot % block)[None, :]
    order_b = order.astype(bf16)
    order_f = order.astype(f32)
    vectors = jnp.dot(
        jnp.concatenate([ln_gains, ln_biases, out_bias], axis=0),
        order_f,
        precision=lax.Precision.HIGHEST,
    )
    gains, shifts, outs = (
        (vectors[2 * i : 2 * i + 1], vectors[2 * i + 1 : 2 * i + 2]) for i in range(3)
    )
    live = jnp.full((1, width), pick(clip_live, t).astype(f32))
    along_one = jnp.zeros((links.nz * block, qkv_cols), bf16)
    for step, piece in enumerate([q_shard] + steps_one):
        at = (z_at + step) % links.nz * block
        along_one = lax.dynamic_update_slice(along_one, piece, (at, 0))
    got_rows, far_small = after(along_one, got_rows, far_small)
    near_one = links.x(along_one), links.y(along_one)
    x, h1, h1_t = enter(pick(clips, t), got_rows[:shard_rows], order_b, gains[0], shifts[0])
    e, e_t = enter_cot(pick(cotangent, t), got_rows[shard_rows:], order_b, live)
    half = width // 2
    twin_rows = jnp.concatenate([e_t[half:], h1_t[half:]], axis=0)
    near_one, along_two, twin_rows, fc2_turned = after(
        (twin_rows, h1, e), near_one, along_two, twin_rows, fc2_weight.T
    )
    along_three = links.z_all(after(along_two, fc2_turned))
    far_one = start_far(links, near_one)
    other_one = [links.c(piece) for piece in (after(near_one, along_one), *near_one)]
    other_one, along_two = after((), other_one, along_two)
    near_two = links.x(along_two), links.y(along_two)
    far_one, twin_rows = after(other_one, far_one, twin_rows)
    other_one += [links.c(piece) for piece in far_one]
    twin_rows = links.c(twin_rows)
    twin_rows, other_one = after((), twin_rows, other_one)
    w_one = [along_one, *near_one, *far_one, *other_one]
    zero_row = jnp.zeros((heads_cols,), f32)
    biases = jnp.stack(
        [
            jnp.concatenate([q_bias, zero_row, v_bias]),
            jnp.concatenate(
                [far_small[:heads_cols], zero_row, far_small[heads_cols : 2 * heads_cols]]
            ),
        ]
    )[:, None]
    fc1_biases = row(jnp.concatenate([fc1_bias, far_small[2 * heads_cols :]]))
    qkv = project(h1, w_one, biases)
    attn, lse = attend_fwd(qkv)

    near_two, lse_rows = after(attn, near_two, lse.T)
    far_two = start_far(links, near_two)
    other_two = [links.c(piece) for piece in (after(near_two, along_two), *near_two)]
    other_two, along_three = after((), other_two, along_three)

    near_three = links.x(along_three), links.y(along_three)
    far_two = after(other_two, far_two)
    other_two += [links.c(piece) for piece in far_two]
    w_two = [along_two, *near_two, *far_two, *other_two]
    y, h2, h2_t = join_heads(attn, x, w_two, hidden_here, outs[0], gains[1], shifts[1])
    hidden, slope = expand(h2, w_two, fc1_biases, hidden_here)
    near_three, hidden, slope, h2_t, along_three = after(
        (), near_three, hidden, slope, h2_t, along_three
    )

    far_three = start_far(links, near_three)
    twin_hidden = links.c(hidden)
    other_three = [links.c(piece) for piece in (along_three, near_three[0])]
    far_three, twin_hidden, other_three, near_three, h2_sent, attn_sent = after(
        (), far_three, twin_hidden, other_three, near_three, h2_t[half:], attn
    )

    quarter = width // 8
    stack = lambda one, two: jnp.concatenate([one[...], two[...]], axis=0)
    join = lambda one, two: jnp.concatenate([one[...], two[...]], axis=1)
    tiles = hidden_here // TILE
    left_at = lambda at: pl.BlockSpec((half, length), lambda s: (at, 0))

    def tile_spec(count):
        def at(s):
            tile = jnp.minimum(s % count, tiles - 1)
            return (0, jnp.where(s < count, tiles, 0) + tile)

        return pl.BlockSpec((length, TILE), at)

    attn_spec = lambda count: pl.BlockSpec((length, TILE), lambda s: (0, 1 - s // count))

    def grad_fc2():
        terms = lambda refs, kind: (join(*refs[:2]), stack(*refs[2:]))
        args = [e_t, twin_rows, hidden, twin_hidden]
        specs = [left_at(0), left_at(0)] + [tile_spec(tiles)] * 2
        return both_sides(args, specs, (0,), terms, "grad_fc2", tiles)

    def grad_two():
        count = tiles + 1

        def terms(refs, kind):
            return join(*refs[4 * kind :][:2]), stack(*refs[4 * kind + 2 :][:2])

        args = [h2_t, twin_h2, du, twin_du, da_t, twin_da, attn, twin_attn]
        specs = [left_at(0)] * 2 + [tile_spec(count)] * 2
        specs += [left_at(0)] * 2 + [attn_spec(count)] * 2
        return both_sides(args, specs, (0, tiles), terms, "grad_two", count)

    def grad_qkv():
        def terms(refs, kind):
            return join(*refs[:2]), jnp.concatenate([refs[2][0], refs[3][0]], axis=0)

        args = [h1_t, twin_rows, dp, twin_dp]
        dp_spec = pl.BlockSpec((1, length, TILE), lambda s: (s % 3, 0, 1 - s // 3))
        specs = [left_at(0), left_at(1)] + [dp_spec] * 2
        return both_sides(args, specs, (0,), terms, "grad_qkv", 3, links.nz)

    def enter_window(done, *homes):
        for home in homes:
            home.x_got, home.y_got = after(done, home.x_got, home.y_got)

    home_fc2, home_two, home_qkv = Home(links), Home(links), Home(links)

    other_three += [links.c(piece) for piece in (near_three[1], *far_three)]
    twin_h2 = links.c(h2_sent)
    pieces = grad_fc2()
    pieces, other_three, twin_h2, attn_sent = after(
        (), pieces, other_three, twin_h2, attn_sent
    )
    w_fc2 = [along_three, *near_three, *far_three, *other_three]

    home_fc2.first(pieces)
    twin_attn = links.c(attn_sent)
    du, fc1b_sum = hidden_back(e, slope, w_fc2)
    mid, da, da_t, da_t_far, second_sums = second_back(du, w_two, hidden_here, y, e, gains[1])
    enter_window(da, home_fc2)
    du, da, da_t, da_t_far, twin_attn = after(
        home_fc2.x_got, du, da, da_t, da_t_far, twin_attn
    )

    twin_du = links.c(du)
    twin_da = links.c(da_t_far)
    home_fc2.second(*home_fc2.middle())
    d_heads = heads_back(da, w_two, hidden_here)
    twin_du, twin_da = after(d_heads, twin_du, twin_da)
    pieces = grad_two()
    pieces, d_heads, home_fc2.y_last, home_fc2.x_last = after(
        (), pieces, d_heads, home_fc2.y_last, home_fc2.x_last
    )

    home_two.first(pieces)
    moved = home_fc2.last(pieces, True)
    dp, q_sums, v_sums = attend_bwd(qkv, after(moved, d_heads), lse_rows)
    grad_near, grad_sent_rows, first_sums = first_back(
        dp, w_one, x, mid, gains[0], order_b
    )
    enter_window(grad_near, home_two)
    dp, first_sums = after(home_two.x_got, dp, first_sums)

    twin_dp = links.c(dp)
    moved = home_two.middle()
    home_two.second(*moved)
    sums = jnp.concatenate(
        [first_sums[:1], second_sums[:1], first_sums[1:], second_sums[1:]], axis=0
    )
    sums = lax.dot_general(
        after(moved, sums), order_f, (((1,), (1,)), ((), ())), precision=lax.Precision.HIGHEST
    )

    def placed(both):
        size = both.shape[1] // 2
        return jnp.where(t == 0, both[0], jnp.concatenate([both[0, size:], both[0, :size]]))

    small = [sums.reshape(-1), placed(q_sums), placed(v_sums), placed(fc1b_sum)]
    small = jnp.concatenate(small).reshape(-1, 128)
    small_got = links.c(after(moved, small))
    twin_dp, small_got = after(moved, twin_dp, small_got)
    small = small + small_got
    small_got = links.flip(small, 1)
    *pieces, by_z = grad_qkv()
    pieces, by_z, home_two.y_last, home_two.x_last, small, small_got = after(
        (), pieces, by_z, home_two.y_last, home_two.x_last, small, small_got
    )

    home_qkv.first(pieces)
    by_z = links.z_sum(by_z.reshape(-1, heads_cols))
    small = small + small_got
    small_got = links.x(small)
    moved = home_two.last(pieces, True)
    enter_window(moved, home_qkv)
    moved, small, small_got, hidden_out, grad_sent_rows = after(
        (), home_qkv.middle(), small, small_got, hidden, grad_sent_rows
    )

    home_qkv.second(*moved)
    grad_got = links.x(grad_sent_rows)
    small = small + small_got
    small_got = links.y(small)
    out_near, out_sent = layer_out(hidden_out, w_fc2, y, outs[1], live, order_b)
    moved = home_qkv.last(out_near, False)
    moved, out_sent, small, small_got = after((), moved, out_sent, small, small_got)

    by_z = jnp.sum(after(moved, by_z).astype(f32), axis=0)
    v_got = links.x(by_z[quarter:].astype(bf16))
    out_got = links.x(out_sent)
    small = small + small_got
    bit = 2
    while bit < links.nz:
        small = small + links.flip(small, bit)
        bit *= 2
    by_x = by_z[:quarter] + v_got.astype(f32)
    by_x, small, out_got, grad_got, home_two.home, home_fc2.home = after(
        (), by_x, small, out_got, grad_got, home_two.home, home_fc2.home
    )
    v_got = links.y(by_x[block:].astype(bf16))
    g_v = (by_x[:block] + v_got.astype(f32)) * grad_scale
    small = small.reshape(-1) * grad_scale
    sums = small[: 6 * width].reshape(6, width)
    own = lambda first, size: lax.dynamic_slice_in_dim(small, first + t * size, size, 0)
    g_qkv = home_qkv.value(g_v, grad_scale)
    g_fc2 = home_fc2.value(moved, grad_scale)
    g_two = home_two.value(moved, grad_scale)

    def both_slots(near, got):
        return jnp.where(t == 0, jnp.stack([near, got]), jnp.stack([got, near]))

    return (
        both_slots(out_near, out_got),
        both_slots(grad_near, grad_got).astype(f32),
        jnp.concatenate([g_qkv, g_v], axis=1).reshape(block, 3, heads_cols),
        own(6 * width, heads_cols),
        own(6 * width + 2 * heads_cols, heads_cols),
        g_two[:, hidden_here:].T,
        g_two[:, :hidden_here],
        own(6 * width + 4 * heads_cols, hidden_here),
        g_fc2.T,
        sums[0:2],
        sums[2:4],
        sums[4:6],
    )


def solution(mesh):
    body = own_slot if fits_own_slot(mesh) else shared_slots
    return jax.shard_map(
        body,
        mesh=mesh,
        in_specs=(
            P("wide", "tp", None),
            P("wide", "tp", None),
            P("wide"),
            P("wide", None, "tp"),
            P("tp"),
            P("tp"),
            P("tp", "wide"),
            P("wide", "tp"),
            P("tp"),
            P("tp", "wide"),
            P(),
            P(),
            P(),
        ),
        out_specs=(
            P("wide", "tp", None),
            P("wide", "tp", None),
            P("wide", None, "tp"),
            P("tp"),
            P("tp"),
            P("tp", "wide"),
            P("wide", "tp"),
            P("tp"),
            P("tp", "wide"),
            P(),
            P(),
            P(),
        ),
        check_vma=False,
    )
```

```python
from functools import partial
import math

import jax
import jax.numpy as jnp
from jax import lax
from jax.experimental import pallas as pl
from jax.experimental.pallas import tpu as pltpu
from jax.sharding import PartitionSpec as P

HEAD_DIM = 64


norm_eps = 1e-06
root_half = 1.0 / math.sqrt(2.0)
inv_root_two_pi = 1.0 / math.sqrt(2.0 * math.pi)


def layer_norm(in_rows, gain_row, shift_row):
    row_mean = jnp.mean(in_rows, axis=-1, keepdims=True)
    centred = in_rows - row_mean
    spread = jnp.mean(centred * centred, axis=-1, keepdims=True)
    inverse = lax.rsqrt(spread + norm_eps)
    unit_rows = centred * inverse
    return (unit_rows * gain_row + shift_row, unit_rows, inverse)


def norm_back(grad_rows, unit_rows, inverse, gain_row):
    scaled = grad_rows * gain_row
    mean_one = jnp.mean(scaled, axis=-1, keepdims=True)
    second = jnp.mean(scaled * unit_rows, axis=-1, keepdims=True)
    return inverse * (scaled - mean_one - unit_rows * second)


def contract_last(left_op, right_op):
    return lax.dot_general(
        left_op, right_op, (((1,), (1,)), ((), ())), preferred_element_type=jnp.float32
    )


def contract_first(left_op, right_op):
    return lax.dot_general(
        left_op, right_op, (((0,), (0,)), ((), ())), preferred_element_type=jnp.float32
    )


def attend_block(query, key_rows, value_rows):
    scores = jnp.einsum("qhd,khd->hqk", query, key_rows, preferred_element_type=jnp.float32)
    row_max = jnp.max(scores, axis=-1, keepdims=True)
    weights = jnp.exp(scores - row_max)
    row_sum = jnp.sum(weights, axis=-1, keepdims=True)
    prob_rows = (weights / row_sum).astype(jnp.bfloat16)
    mixed_rows = jnp.einsum(
        "hqk,khd->qhd", prob_rows, value_rows, preferred_element_type=jnp.float32
    )
    return (mixed_rows, row_max[..., 0] + jnp.log(row_sum[..., 0]))


def attend_back(query, grad_rows, log_total, key_rows, value_rows):
    scores = jnp.einsum("qhd,khd->hqk", query, key_rows, preferred_element_type=jnp.float32)
    prob_rows = jnp.exp(scores - log_total[..., None])
    dprobs = jnp.einsum("qhd,khd->hqk", grad_rows, value_rows, preferred_element_type=jnp.float32)
    row_delta = jnp.sum(prob_rows * dprobs, axis=-1, keepdims=True)
    dscores = (prob_rows * (dprobs - row_delta)).astype(jnp.bfloat16)
    dquery = jnp.einsum("hqk,khd->qhd", dscores, key_rows, preferred_element_type=jnp.float32)
    d_keys = jnp.einsum("hqk,qhd->khd", dscores, query, preferred_element_type=jnp.float32)
    dvalues = jnp.einsum(
        "hqk,qhd->khd",
        prob_rows.astype(jnp.bfloat16),
        grad_rows,
        preferred_element_type=jnp.float32,
    )
    return (dquery, d_keys, dvalues)


def shared_slots(
    clips,
    cotangent,
    clip_live,
    qkv_weight,
    q_bias,
    v_bias,
    proj_weight,
    fc1_weight,
    fc1_bias,
    fc2_weight,
    ln_gains,
    ln_biases,
    out_bias,
):
    tp_count = lax.axis_size("tp")
    wide_count = lax.axis_size("wide")
    slot_count, shard_rows, width = clips.shape
    length = shard_rows * tp_count
    local_cols = qkv_weight.shape[2]
    heads_here = local_cols // HEAD_DIM
    hidden_here = fc1_weight.shape[1]
    q_scale = 1.0 / math.sqrt(HEAD_DIM)
    grad_scale = 1.0 / math.sqrt(wide_count * slot_count * length)
    block_rows = 512
    blocks = length // block_rows
    tp_place = lax.axis_index("tp")
    live_slots = clip_live.astype(jnp.float32)
    qv_bias = jnp.stack([q_bias, v_bias])
    own_weights = (qkv_weight, proj_weight, fc1_weight, fc2_weight)

    def one_slot(state_in, inputs):
        rows_in, cot_in, live_one = inputs
        tied_weights = lax.optimization_barrier((own_weights, rows_in))[0]
        w_qkv, w_proj, w_fc1, w_fc2 = (
            lax.all_gather(tied_weights[0], "wide", axis=0, tiled=True),
            lax.all_gather(tied_weights[1], "wide", axis=1, tiled=True),
            lax.all_gather(tied_weights[2], "wide", axis=0, tiled=True),
            lax.all_gather(tied_weights[3], "wide", axis=1, tiled=True),
        )
        x_rows = rows_in.astype(jnp.float32)
        norm_one, unit_one, inv_one = layer_norm(x_rows, ln_gains[0], ln_biases[0])
        h1_full = lax.all_gather(norm_one.astype(jnp.bfloat16), "tp", axis=0, tiled=True)
        qkv_flat = w_qkv.reshape(width, 3 * local_cols)
        projected = jnp.dot(h1_full, qkv_flat, preferred_element_type=jnp.float32).reshape(
            length, 3, local_cols
        )
        query = (
            ((projected[:, 0] + qv_bias[0]) * q_scale)
            .astype(jnp.bfloat16)
            .reshape(length, heads_here, HEAD_DIM)
        )
        key_rows = projected[:, 1].astype(jnp.bfloat16).reshape(length, heads_here, HEAD_DIM)
        value_rows = (
            (projected[:, 2] + qv_bias[1])
            .astype(jnp.bfloat16)
            .reshape(length, heads_here, HEAD_DIM)
        )
        query_blocks = query.reshape(blocks, block_rows, heads_here, HEAD_DIM)
        mixed_blocks, log_totals = lax.map(
            partial(attend_block, key_rows=key_rows, value_rows=value_rows), query_blocks
        )
        attn_out = mixed_blocks.reshape(length, local_cols).astype(jnp.bfloat16)
        attn_sum = lax.psum_scatter(
            jnp.dot(attn_out, w_proj, preferred_element_type=jnp.float32),
            "tp",
            scatter_dimension=0,
            tiled=True,
        )
        mid_rows = x_rows + attn_sum + out_bias[0]
        norm_two, unit_two, inv_two = layer_norm(mid_rows, ln_gains[1], ln_biases[1])
        h2_full = lax.all_gather(norm_two.astype(jnp.bfloat16), "tp", axis=0, tiled=True)
        pre_act = jnp.dot(h2_full, w_fc1, preferred_element_type=jnp.float32) + fc1_bias
        cdf_part = 0.5 * (1.0 + lax.erf(pre_act * root_half))
        hidden = (pre_act * cdf_part).astype(jnp.bfloat16)
        mlp_sum = lax.psum_scatter(
            jnp.dot(hidden, w_fc2, preferred_element_type=jnp.float32).astype(jnp.bfloat16),
            "tp",
            scatter_dimension=0,
            tiled=True,
        ).astype(jnp.float32)
        block_out = (live_one * (mid_rows + mlp_sum + out_bias[1])).astype(jnp.bfloat16)
        out_grad = live_one * cot_in.astype(jnp.float32)
        out_full = lax.all_gather(out_grad.astype(jnp.bfloat16), "tp", axis=0, tiled=True)
        g_fc2 = contract_first(hidden, out_full)
        act_grad = contract_last(out_full, w_fc2)
        slope = cdf_part + pre_act * jnp.exp(-0.5 * pre_act * pre_act) * inv_root_two_pi
        pre_grad = act_grad * slope
        pre_grad_b = pre_grad.astype(jnp.bfloat16)
        g_fc1 = contract_first(h2_full, pre_grad_b)
        g_fc1b = jnp.sum(pre_grad, axis=0)
        norm_two_grad = lax.psum_scatter(
            contract_last(pre_grad_b, w_fc1), "tp", scatter_dimension=0, tiled=True
        )
        mid_grad = out_grad + norm_back(norm_two_grad, unit_two, inv_two, ln_gains[1])
        attn_full = lax.all_gather(mid_grad.astype(jnp.bfloat16), "tp", axis=0, tiled=True)
        g_proj = contract_first(attn_out, attn_full)
        mixed_grad = (
            contract_last(attn_full, w_proj)
            .astype(jnp.bfloat16)
            .reshape(blocks, block_rows, heads_here, HEAD_DIM)
        )

        def back_block(block_state, pieces):
            query_b, grad_b, lse_b = pieces
            d_query, d_keys, d_values = attend_back(query_b, grad_b, lse_b, key_rows, value_rows)
            return ((block_state[0] + d_keys, block_state[1] + d_values), d_query)

        empty_kv = jnp.zeros((length, heads_here, HEAD_DIM), jnp.float32)
        (key_grad, value_grad), query_grad = lax.scan(
            back_block, (empty_kv, empty_kv), (query_blocks, mixed_grad, log_totals)
        )
        query_grad = query_grad.reshape(length, local_cols) * q_scale
        key_grad = key_grad.reshape(length, local_cols)
        value_grad = value_grad.reshape(length, local_cols)
        g_qvb = jnp.stack([jnp.sum(query_grad, axis=0), jnp.sum(value_grad, axis=0)])
        proj_grads = (
            jnp.stack([query_grad, key_grad, value_grad], axis=1)
            .astype(jnp.bfloat16)
            .reshape(length, 3 * local_cols)
        )
        g_qkv = contract_first(h1_full, proj_grads).reshape(width, 3, local_cols)
        norm_one_grad = lax.psum_scatter(
            contract_last(proj_grads, qkv_flat).astype(jnp.bfloat16),
            "tp",
            scatter_dimension=0,
            tiled=True,
        ).astype(jnp.float32)
        in_grad = mid_grad + norm_back(norm_one_grad, unit_one, inv_one, ln_gains[0])
        gain_part = jnp.stack(
            [jnp.sum(norm_one_grad * unit_one, axis=0), jnp.sum(norm_two_grad * unit_two, axis=0)]
        )
        shift_part = jnp.stack([jnp.sum(norm_one_grad, axis=0), jnp.sum(norm_two_grad, axis=0)])
        bias_part = jnp.stack([jnp.sum(mid_grad, axis=0), jnp.sum(out_grad, axis=0)])
        summed = (
            lax.psum_scatter(
                g_qkv.astype(jnp.bfloat16), "wide", scatter_dimension=0, tiled=True
            ).astype(jnp.float32),
            lax.psum_scatter(
                g_proj.astype(jnp.bfloat16), "wide", scatter_dimension=1, tiled=True
            ).astype(jnp.float32),
            lax.psum_scatter(
                g_fc1.astype(jnp.bfloat16), "wide", scatter_dimension=0, tiled=True
            ).astype(jnp.float32),
            lax.psum_scatter(
                g_fc2.astype(jnp.bfloat16), "wide", scatter_dimension=1, tiled=True
            ).astype(jnp.float32),
        )
        weight_acc = jax.tree.map(jnp.add, state_in[0], summed)
        vector_acc = jax.tree.map(
            jnp.add, state_in[1], (gain_part, shift_part, bias_part, g_qvb, g_fc1b)
        )
        return ((weight_acc, vector_acc), (block_out, in_grad))

    weight_zero = tuple((jnp.zeros(shard_in.shape, jnp.float32) for shard_in in own_weights))
    vector_zero = (
        jnp.zeros((2, width), jnp.float32),
        jnp.zeros((2, width), jnp.float32),
        jnp.zeros((2, width), jnp.float32),
        jnp.zeros((2, local_cols), jnp.float32),
        jnp.zeros((hidden_here,), jnp.float32),
    )
    (weight_sums, vector_acc), (block_out, clips_grad) = lax.scan(
        one_slot, (weight_zero, vector_zero), (clips, cotangent, live_slots)
    )
    gain_acc, shift_acc, bias_acc, qvb_acc, fc1b_acc = vector_acc
    qvb_pad = lax.dynamic_update_slice(
        jnp.zeros((2, width), jnp.float32), qvb_acc, (0, tp_place * local_cols)
    )
    fc1b_pad = lax.dynamic_update_slice(
        jnp.zeros((hidden_here * tp_count,), jnp.float32), fc1b_acc, (tp_place * hidden_here,)
    )
    gain_sum, shift_sum, bias_sum, qvb_sum, fc1b_sum = lax.psum(
        (gain_acc, shift_acc, bias_acc, qvb_pad, fc1b_pad), ("wide", "tp")
    )
    qvb_own = lax.dynamic_slice_in_dim(qvb_sum, tp_place * local_cols, local_cols, 1)
    fc1b_own = lax.dynamic_slice_in_dim(fc1b_sum, tp_place * hidden_here, hidden_here, 0)
    return (
        block_out,
        clips_grad,
        weight_sums[0] * grad_scale,
        qvb_own[0] * grad_scale,
        qvb_own[1] * grad_scale,
        weight_sums[1] * grad_scale,
        weight_sums[2] * grad_scale,
        fc1b_own * grad_scale,
        weight_sums[3] * grad_scale,
        gain_sum * grad_scale,
        shift_sum * grad_scale,
        bias_sum * grad_scale,
    )


AXES = ("wide", "tp")
PAIR = 128
TILE = 512
MIB = 1024 * 1024
GRANT = {"project": 60, "hidden_back": 60, "heads_back": 60, "layer_out": 60, "join_heads": 30, "expand": 36, "enter": 30, "enter_cot": 30, "grad_fc2": 36}
WIDE = 1024
bf16 = jnp.bfloat16
f32 = jnp.float32


def fits_own_slot(mesh):
    return mesh.shape["tp"] == 2 and mesh.shape["wide"] % 4 == 0


def nt_dot(left_op, right_op):
    return lax.dot_general(
        left_op, right_op, (((1,), (1,)), ((), ())), preferred_element_type=f32
    )


def nn_dot(left_op, right_op):
    return lax.dot_general(
        left_op, right_op, (((1,), (0,)), ((), ())), preferred_element_type=f32
    )


def kernel_call(body, name, grid, in_specs, out_specs, out_shape, scratch=(), scalars=0):
    return pl.pallas_call(
        body,
        grid_spec=pltpu.PrefetchScalarGridSpec(
            num_scalar_prefetch=scalars,
            grid=grid,
            in_specs=in_specs,
            out_specs=out_specs,
            scratch_shapes=list(scratch),
        ),
        out_shape=out_shape,
        compiler_params=pltpu.CompilerParams(vmem_limit_bytes=GRANT.get(name, 60) * MIB),
        cost_estimate=pl.CostEstimate(flops=1, bytes_accessed=1, transcendentals=0),
        name=name,
    )


def whole(shape):
    return pl.BlockSpec(shape, lambda *at: (0,) * len(shape))


def array(*shape, dtype=bf16):
    return jax.ShapeDtypeStruct(shape, dtype)


def norm_stats(rows):
    row_mean = jnp.mean(rows, axis=-1, keepdims=True)
    centred = rows - row_mean
    spread = jnp.mean(centred * centred, axis=-1, keepdims=True)
    inverse = lax.rsqrt(spread + norm_eps)
    return centred * inverse, inverse


NEAR = (0, 2, 5, 7)
FAR = (1, 3, 4, 6, 8, 9)


class Pieces:
    def __init__(self, pieces, columns, first=0, tile=WIDE):
        self.pieces, self.columns, self.first = pieces, columns, first
        self.tile = min(tile, columns)
        self.tiles = columns // self.tile
        self.args = list(pieces)
        self.specs = [pl.BlockSpec(memory_space=pl.ANY)] * len(pieces)
        rows = sum(pieces[i].shape[0] for i in NEAR)
        self.scratch = [
            pltpu.VMEM((2, rows, columns), bf16),
            pltpu.SemaphoreType.DMA((self.tiles, len(pieces))),
        ]

    def copies(self, refs, side, tile, w_ref, sems):
        at, found = 0, []
        for index in FAR if side else NEAR:
            rows = self.pieces[index].shape[0]
            found.append(
                pltpu.make_async_copy(
                    refs[index].at[:, pl.ds(self.first + tile * self.tile, self.tile)],
                    w_ref.at[side, pl.ds(at, rows), pl.ds(tile * self.tile, self.tile)],
                    sems.at[tile, index],
                )
            )
            at += rows
        return found

    def start(self, refs, w_ref, sems):
        for side in range(2):
            for tile in range(self.tiles):
                for copy in self.copies(refs, side, tile, w_ref, sems):
                    copy.start()

    def wait(self, refs, side, tile, w_ref, sems):
        for copy in self.copies(refs, side, tile, w_ref, sems):
            copy.wait()

    def get(self, refs, side, tile, w_ref, sems):
        self.wait(refs, side, tile, w_ref, sems)
        return w_ref[side, :, pl.ds(tile * self.tile, self.tile)]

    def each_step(self, step, refs, w_ref, sems, work):
        pl.when(step == 0)(lambda: self.start(refs, w_ref, sems))
        for side in range(2):
            for tile in range(self.tiles):

                @pl.when(step == side * self.tiles + tile)
                def _():
                    work(side, tile, self.get(refs, side, tile, w_ref, sems))


def enter_kernel(own_ref, got_ref, order_ref, gain_ref, shift_ref, x_ref, h_ref, ht_ref):
    half = own_ref.shape[0]
    for part, ref in enumerate((own_ref, got_ref)):
        rows = nn_dot(ref[...], order_ref[...])
        here = pl.ds(part * half, half)
        x_ref[here, :] = rows.astype(bf16)
        unit, _ = norm_stats(rows)
        normed = (unit * gain_ref[...] + shift_ref[...]).astype(bf16)
        h_ref[here, :] = normed
        ht_ref[:, here] = normed.T


def enter(own, got, order_b, gain, shift):
    half, width = own.shape
    length = 2 * half
    return kernel_call(
        enter_kernel,
        "enter",
        (1,),
        [whole((half, width))] * 2 + [whole((width, width))] + [whole((1, width))] * 2,
        [whole((length, width))] * 2 + [whole((width, length))],
        [array(length, width)] * 2 + [array(width, length)],
    )(own, got, order_b, gain, shift)


def cot_kernel(own_ref, got_ref, order_ref, live_ref, e_ref, et_ref):
    half = own_ref.shape[0]
    for part, ref in enumerate((own_ref, got_ref)):
        rows = (live_ref[...] * nn_dot(ref[...], order_ref[...])).astype(bf16)
        here = pl.ds(part * half, half)
        e_ref[here, :] = rows
        et_ref[:, here] = rows.T


def enter_cot(own, got, order_b, live):
    half, width = own.shape
    length = 2 * half
    return kernel_call(
        cot_kernel,
        "enter_cot",
        (1,),
        [whole((half, width))] * 2 + [whole((width, width)), whole((1, width))],
        [whole((length, width)), whole((width, length))],
        [array(length, width), array(width, length)],
    )(own, got, order_b, live)


def project(h, pieces, biases):
    length, width = h.shape
    each = pieces[0].shape[1] // 3
    load = Pieces(pieces, 3 * each, 0, each)
    scales = (1.0 / math.sqrt(HEAD_DIM), None, None)

    def body(h_ref, bias_ref, *refs):
        refs, (out_ref, w_ref, sems) = refs[:-3], refs[-3:]

        def work(side, tile, weight):
            acc = nn_dot(h_ref[...], weight) + bias_ref[0]
            out_ref[0] = (acc if scales[tile] is None else acc * scales[tile]).astype(bf16)

        load.each_step(pl.program_id(0), refs, w_ref, sems, work)

    return kernel_call(
        body,
        "project",
        (6,),
        [whole((length, width)), pl.BlockSpec((1, 1, each), lambda s: (s // 3, 0, s % 3))]
        + load.specs,
        pl.BlockSpec((1, length, each), lambda s: (s % 3, 0, s // 3)),
        array(3, length, width),
        load.scratch,
    )(h, biases, *load.args)


def attend_kernel(q_ref, k_ref, v_ref, o_ref, lse_ref):
    pair = pl.program_id(0)
    rows = q_ref.shape[1]
    lanes = lax.broadcasted_iota(jnp.int32, (rows, PAIR), 1)
    keys = k_ref[0]
    values = v_ref[0]
    total = jnp.zeros((rows, PAIR), f32)
    for half in range(2):
        mask = (lanes // HEAD_DIM) == half
        query = jnp.where(mask, q_ref[0], jnp.zeros_like(keys))
        scores = nt_dot(query, keys)
        row_max = jnp.max(scores, axis=-1, keepdims=True)
        weights = jnp.exp(scores - row_max)
        row_sum = jnp.sum(weights, axis=-1, keepdims=True)
        probs = (weights * (1.0 / row_sum)).astype(bf16)
        mixed = nn_dot(probs, values)
        total = jnp.where(mask, mixed, total)
        lse = row_max + jnp.log(row_sum)
        lse_ref[...] = jnp.where(lanes == 2 * pair + half, lse, lse_ref[...])
    o_ref[...] = total.astype(bf16)


def head_spec(length, index):
    return pl.BlockSpec((1, length, PAIR), lambda i: (index, 0, i))


def attend_fwd(qkv):
    _, length, width = qkv.shape
    return kernel_call(
        attend_kernel,
        "attend_fwd",
        (width // PAIR,),
        [head_spec(length, j) for j in range(3)],
        [pl.BlockSpec((length, PAIR), lambda i: (0, i)), whole((length, PAIR))],
        [array(length, width), array(length, PAIR, dtype=f32)],
    )(qkv, qkv, qkv)


def join_heads(attn, x, pieces, first, bias, gain, shift):
    length, width = x.shape
    load = Pieces(pieces, TILE, first)

    def body(attn_ref, x_ref, bias_ref, gain_ref, shift_ref, *refs):
        refs, (y_ref, h_ref, ht_ref, w_ref, sems) = refs[:-5], refs[-5:]
        load.start(refs, w_ref, sems)
        load.wait(refs, 0, 0, w_ref, sems)
        load.wait(refs, 1, 0, w_ref, sems)
        half = length // 2
        for part in range(2):
            here = pl.ds(part * half, half)
            rows = nt_dot(attn_ref[here, :TILE], w_ref[0]) + nt_dot(attn_ref[here, TILE:], w_ref[1])
            rows = x_ref[here, :].astype(f32) + rows + bias_ref[...]
            y_ref[here, :] = rows
            unit, _ = norm_stats(rows)
            normed = (unit * gain_ref[...] + shift_ref[...]).astype(bf16)
            h_ref[here, :] = normed
            ht_ref[:, here] = normed.T

    return kernel_call(
        body,
        "join_heads",
        (1,),
        [whole((length, width))] * 2 + [whole((1, width))] * 3 + load.specs,
        [whole((length, width))] * 2 + [whole((width, length))],
        [array(length, width, dtype=f32), array(length, width), array(width, length)],
        load.scratch,
    )(attn, x, bias, gain, shift, *load.args)


def expand(h, pieces, bias, hidden):
    length, width = h.shape
    load = Pieces(pieces, hidden)

    def body(h_ref, bias_ref, *refs):
        refs, (g_ref, slope_ref, w_ref, sems) = refs[:-4], refs[-4:]

        def work(side, tile, weight):
            pre = nn_dot(h_ref[...], weight) + bias_ref[...]
            cdf = 0.5 * (1.0 + lax.erf(pre * root_half))
            g_ref[...] = (pre * cdf).astype(bf16)
            density = jnp.exp(-0.5 * pre * pre) * inv_root_two_pi
            slope_ref[...] = (cdf + pre * density).astype(bf16)

        load.each_step(pl.program_id(0), refs, w_ref, sems, work)

    block = pl.BlockSpec((length, WIDE), lambda s: (0, s))
    return kernel_call(
        body,
        "expand",
        (2 * load.tiles,),
        [whole((length, width)), pl.BlockSpec((1, WIDE), lambda s: (0, s))] + load.specs,
        [block] * 2,
        [array(length, 2 * hidden)] * 2,
        load.scratch,
    )(h, bias, *load.args)


def hidden_back(e, slope, pieces):
    length, width = e.shape
    hidden = pieces[0].shape[1]
    load = Pieces(pieces, hidden)

    def body(e_ref, slope_ref, *refs):
        refs, (du_ref, sum_ref, w_ref, sems) = refs[:-4], refs[-4:]

        def work(side, tile, weight):
            du = nn_dot(e_ref[...], weight) * slope_ref[...].astype(f32)
            du_ref[...] = du.astype(bf16)
            sum_ref[...] = jnp.sum(du, axis=0, keepdims=True)

        load.each_step(pl.program_id(0), refs, w_ref, sems, work)

    block = pl.BlockSpec((length, WIDE), lambda s: (0, s))
    row = pl.BlockSpec((1, WIDE), lambda s: (0, s))
    return kernel_call(
        body,
        "hidden_back",
        (2 * load.tiles,),
        [whole((length, width)), block] + load.specs,
        [block, row],
        [array(length, 2 * hidden), array(1, 2 * hidden, dtype=f32)],
        load.scratch,
    )(e, slope, *load.args)


def heads_back(da, pieces, first):
    length, width = da.shape
    load = Pieces(pieces, TILE, first)

    def body(da_ref, *refs):
        refs, (out_ref, w_ref, sems) = refs[:-3], refs[-3:]
        load.start(refs, w_ref, sems)
        for side in range(2):
            load.wait(refs, side, 0, w_ref, sems)
            out_ref[:, pl.ds(side * TILE, TILE)] = nn_dot(da_ref[...], w_ref[side]).astype(bf16)

    return kernel_call(
        body,
        "heads_back",
        (1,),
        [whole((length, width))] + load.specs,
        whole((length, 2 * TILE)),
        array(length, 2 * TILE),
        load.scratch,
    )(da, *load.args)


def contract_back(rows, rows_specs, left_of, load, extras, finish, name, outs):
    count = len(extras)
    length, width = extras[0].shape

    def body(*refs):
        rows_refs, refs = refs[: len(rows)], refs[len(rows) :]
        extra_refs, refs = refs[:count], refs[count:]
        w_refs, refs = refs[: len(load.args)], refs[len(load.args) :]
        out_refs, refs = refs[: len(outs)], refs[len(outs) :]
        w_ref, sems, acc_ref, extra_sems = refs[:4]
        held = refs[4:]
        copies = [
            pltpu.make_async_copy(source, target, extra_sems.at[i])
            for i, (source, target) in enumerate(zip(extra_refs, held))
        ]

        def work(side, tile, weight):
            term = nt_dot(left_of(rows_refs), weight)
            if side == 0 and tile == 0:
                for copy in copies:
                    copy.start()
                acc_ref[...] = term
            else:
                acc_ref[...] += term
            if side == 1 and tile == load.tiles - 1:
                for copy in copies:
                    copy.wait()
                finish(acc_ref, held, out_refs)

        load.each_step(pl.program_id(0), w_refs, w_ref, sems, work)

    return kernel_call(
        body,
        name,
        (2 * load.tiles,),
        rows_specs + [pl.BlockSpec(memory_space=pl.ANY)] * count + load.specs,
        [whole(o.shape) for o in outs],
        outs,
        load.scratch
        + [pltpu.VMEM((length, width), f32), pltpu.SemaphoreType.DMA((count,))]
        + [pltpu.VMEM(extra.shape, extra.dtype) for extra in extras],
    )(*rows, *extras, *load.args)


def to_home(rows, order_ref):
    return nt_dot(rows.astype(bf16), order_ref[...]).astype(bf16)


def layer_out(hidden, pieces, y, bias, live, order_b):
    length, width = y.shape
    half = length // 2

    def finish(acc_ref, ins, outs):
        y_ref, bias_ref, live_ref, order_ref = ins
        for part in range(2):
            here = pl.ds(part * half, half)
            rows = live_ref[...] * (y_ref[here, :] + acc_ref[here, :] + bias_ref[...])
            outs[part][...] = to_home(rows, order_ref)

    return contract_back(
        [hidden],
        [pl.BlockSpec((length, WIDE), lambda s, *_: (0, s))],
        lambda refs: refs[0][...],
        Pieces(pieces, pieces[0].shape[1]),
        (y, bias, live, order_b),
        finish,
        "layer_out",
        [array(half, width)] * 2,
    )


def second_back(du, pieces, hidden, y, e, gain):
    length, width = y.shape
    half = length // 2

    def finish(acc_ref, ins, outs):
        y_ref, e_ref, gain_ref = ins
        mid_ref, da_ref, dat_ref, dat_far_ref, sum_ref = outs
        sums = [jnp.zeros((1, width), f32)] * 4
        for part in range(2):
            here = pl.ds(part * half, half)
            unit, inverse = norm_stats(y_ref[here, :])
            grad = acc_ref[here, :]
            e_rows = e_ref[here, :].astype(f32)
            mid = e_rows + norm_back(grad, unit, inverse, gain_ref[...])
            mid_ref[here, :] = mid
            mid_b = mid.astype(bf16)
            da_ref[here, :] = mid_b
            dat_ref[:, here] = mid_b[:, : width // 2].T
            dat_far_ref[:, here] = mid_b[:, width // 2 :].T
            terms = (grad * unit, grad, mid, e_rows)
            sums = [s + jnp.sum(term, axis=0, keepdims=True) for s, term in zip(sums, terms)]
        sum_ref[...] = jnp.concatenate(sums, axis=0)

    return contract_back(
        [du],
        [pl.BlockSpec((length, WIDE), lambda s: (0, s))],
        lambda refs: refs[0][...],
        Pieces(pieces, hidden),
        (y, e, gain),
        finish,
        "second_back",
        [
            array(length, width, dtype=f32),
            array(length, width),
            array(width // 2, length),
            array(width // 2, length),
            array(4, width, dtype=f32),
        ],
    )


def first_back(dp, pieces, x, mid, gain, order_b):
    length, width = x.shape
    half = length // 2

    def finish(acc_ref, ins, outs):
        x_ref, mid_ref, gain_ref, order_ref = ins
        sum_ref = outs[2]
        sums = [jnp.zeros((1, width), f32)] * 2
        for part in range(2):
            here = pl.ds(part * half, half)
            unit, inverse = norm_stats(x_ref[here, :].astype(f32))
            grad = acc_ref[here, :]
            rows = mid_ref[here, :] + norm_back(grad, unit, inverse, gain_ref[...])
            outs[part][...] = to_home(rows, order_ref)
            terms = (grad * unit, grad)
            sums = [s + jnp.sum(term, axis=0, keepdims=True) for s, term in zip(sums, terms)]
        sum_ref[...] = jnp.concatenate(sums, axis=0)

    return contract_back(
        [dp],
        [pl.BlockSpec((3, length, width // 2), lambda s: (0, 0, s))],
        lambda refs: jnp.concatenate([refs[0][j] for j in range(3)], axis=1),
        Pieces(pieces, pieces[0].shape[1], 0, pieces[0].shape[1]),
        (x, mid, gain, order_b),
        finish,
        "first_back",
        [array(half, width)] * 2 + [array(2, width, dtype=f32)],
    )


def attend_back_kernel(q_ref, k_ref, v_ref, g_ref, lse_ref, dp_ref, qs_ref, vs_ref):
    pair = pl.program_id(0)
    rows = q_ref.shape[1]
    lanes = lax.broadcasted_iota(jnp.int32, (rows, PAIR), 1)
    sub = lax.broadcasted_iota(jnp.int32, (PAIR, rows), 0)
    query = q_ref[0]
    keys = k_ref[0]
    values = v_ref[0]
    grads = g_ref[...]
    blank = jnp.zeros_like(keys)
    keys_t = keys.T
    dq_t = jnp.zeros((PAIR, rows), f32)
    dk = jnp.zeros((rows, PAIR), f32)
    dv = jnp.zeros((rows, PAIR), f32)
    for half in range(2):
        mask = (lanes // HEAD_DIM) == half
        scores_t = nt_dot(jnp.where(mask, keys, blank), query)
        lse = lse_ref[pl.ds(2 * pair + half, 1), :]
        probs_t = jnp.exp(scores_t - lse)
        dprobs_t = nt_dot(jnp.where(mask, values, blank), grads)
        delta = jnp.sum(probs_t * dprobs_t, axis=0, keepdims=True)
        ds_t = (probs_t * (dprobs_t - delta)).astype(bf16)
        dv = jnp.where(mask, nn_dot(probs_t.astype(bf16), grads), dv)
        dk = jnp.where(mask, nn_dot(ds_t, query), dk)
        dq_t = jnp.where((sub // HEAD_DIM) == half, nn_dot(keys_t, ds_t), dq_t)
    dq = dq_t.T * (1.0 / math.sqrt(HEAD_DIM))
    dp_ref[0] = dq.astype(bf16)
    dp_ref[1] = dk.astype(bf16)
    dp_ref[2] = dv.astype(bf16)
    qs_ref[...] = jnp.sum(dq, axis=0, keepdims=True)
    vs_ref[...] = jnp.sum(dv, axis=0, keepdims=True)


def attend_bwd(qkv, grads, lse_rows):
    _, length, width = qkv.shape
    row = pl.BlockSpec((1, PAIR), lambda i: (0, i))
    sums = array(1, width, dtype=f32)
    return kernel_call(
        attend_back_kernel,
        "attend_bwd",
        (width // PAIR,),
        [head_spec(length, j) for j in range(3)]
        + [pl.BlockSpec((length, PAIR), lambda i: (0, i)), whole((PAIR, length))],
        [pl.BlockSpec((3, length, PAIR), lambda i: (0, 0, i)), row, row],
        [array(3, length, width), sums, sums],
    )(qkv, qkv, qkv, grads, lse_rows)


def both_sides(args, specs, kinds, terms, name, tiles, width=TILE, z_first=0):
    count = len(args)
    half = args[0].shape[0] // 2
    mid = half // 4
    kept = tiles - 1 if z_first else tiles

    def body(*refs):
        x_ref, y_ref, k10_ref, k00_ref, k01_ref = refs[count : count + 5]
        step = pl.program_id(0)

        def apart(kind):
            left, right = terms(refs[:count], kind)
            acc = nn_dot(left, right).astype(bf16)
            size = acc.shape[0] // 2 // z_first
            for z in range(z_first):
                for ky in range(2):
                    first = (ky * z_first + z) * size
                    refs[-1][z, 0, pl.ds(ky * size, size), :] = acc[first : first + size]

        def run(kind, side):
            left, right = terms(refs[:count], kind)
            acc = nn_dot(left, right).astype(bf16)
            y_ref[...] = acc[3 * mid :]
            if side:
                x_ref[pl.ds(0, mid), :] = acc[:mid]
                x_ref[pl.ds(mid, mid), :] = acc[2 * mid : 3 * mid]
                k10_ref[...] = acc[mid : 2 * mid]
            else:
                k00_ref[...] = acc[: 2 * mid]
                k01_ref[...] = acc[2 * mid : 3 * mid]

        for side in range(2):
            for kind, first in enumerate(kinds):
                last = kinds[kind + 1] if kind + 1 < len(kinds) else tiles
                base = 0 if side else tiles
                here = (step >= base + first) & (step < base + min(last, kept))
                pl.when(here)(partial(run, kind, side))
        if z_first:
            pl.when(step % tiles == tiles - 1)(partial(apart, len(kinds) - 1))

    most = kept - 1
    far = lambda size: pl.BlockSpec((size, width), lambda s: (0, jnp.minimum(s, most)))
    near = lambda size: pl.BlockSpec(
        (size, width), lambda s: (0, jnp.minimum(jnp.maximum(s - tiles, 0), most))
    )
    both = pl.BlockSpec((mid, width), lambda s: (s // tiles, jnp.minimum(s % tiles, most)))
    sizes = (2 * mid, 2 * mid, mid, 2 * mid, mid)
    out_specs = [far(2 * mid), both, far(mid), near(2 * mid), near(mid)]
    shapes = [array(size, kept * width) for size in sizes]
    if z_first:
        each = half // z_first
        out_specs.append(
            pl.BlockSpec((z_first, 1, each, width), lambda s: (0, 1 - s // tiles, 0, 0))
        )
        shapes.append(array(z_first, 2, each, width))
    return kernel_call(body, name, (2 * tiles,), specs, out_specs, shapes)(*args)


def add_mid_kernel(k01_ref, rx_ref, k10_ref, ry_ref, y_ref, x_ref):
    half = k01_ref.shape[0]
    y_ref[...] = (k01_ref[...].astype(f32) + rx_ref[pl.ds(half, half), :].astype(f32)).astype(bf16)
    x_ref[...] = (k10_ref[...].astype(f32) + ry_ref[pl.ds(0, half), :].astype(f32)).astype(bf16)


def add_last_kernel(k00_ref, rx_ref, ry_ref, y2_ref, x2_ref, out_ref):
    half = y2_ref.shape[0]
    top, low = pl.ds(0, half), pl.ds(half, half)
    near = (rx_ref[top, :], y2_ref[...]), (ry_ref[low, :], x2_ref[...])
    for here, (one, two) in zip((top, low), near):
        total = k00_ref[here, :].astype(f32) + one.astype(f32) + two.astype(f32)
        out_ref[here, :] = total.astype(bf16)


def small_call(body, name, args, shapes):
    out_specs = [whole(s.shape) for s in shapes]
    return kernel_call(body, name, (1,), [whole(a.shape) for a in args], out_specs, shapes)(*args)


class Links:
    def __init__(self):
        self.nz = lax.axis_size("wide") // 4
        self.across = self.table(lambda z, y, c, x: (z, y, c, 1 - x))
        self.beside = self.table(lambda z, y, c, x: (z, 1 - y, c, x))
        self.twin = self.table(lambda z, y, c, x: (z, y, 1 - c, x))

    def table(self, source):
        pairs = []
        for z in range(self.nz):
            for y in range(2):
                for c in range(2):
                    for x in range(2):
                        zs, ys, cs, xs = source(z, y, c, x)
                        pairs.append(
                            (((zs * 2 + ys) * 2 + cs) * 2 + xs, ((z * 2 + y) * 2 + c) * 2 + x)
                        )
        return pairs

    def from_z(self, rows, step):
        shift = self.table(lambda z, y, c, x: ((z + step) % self.nz, y, c, x))
        return lax.ppermute(rows, AXES, shift)

    def z_groups(self):
        rest = [(y, c, x) for y in range(2) for c in range(2) for x in range(2)]
        return [
            [((z * 2 + y) * 2 + c) * 2 + x for z in range(self.nz)] for y, c, x in rest
        ]

    def z_sum_apart(self, rows):
        return lax.psum_scatter(
            rows, AXES, scatter_dimension=0, tiled=True, axis_index_groups=self.z_groups()
        )

    def z_sum(self, rows):
        got = lax.all_to_all(rows, AXES, 0, 0, tiled=True, axis_index_groups=self.z_groups())
        return got.reshape(self.nz, -1, rows.shape[1])

    def z_all(self, rows):
        return lax.all_gather(
            rows, AXES, axis=0, tiled=True, axis_index_groups=self.z_groups()
        )

    def x(self, rows):
        return lax.ppermute(rows, AXES, self.across)

    def y(self, rows):
        return lax.ppermute(rows, AXES, self.beside)

    def c(self, rows):
        return lax.ppermute(rows, AXES, self.twin)

    def flip(self, rows, bit):
        swap = self.table(lambda z, y, c, x: (z ^ bit, y, c, x))
        return lax.ppermute(rows, AXES, swap)


def after(done, *values):
    out = lax.optimization_barrier((values, done))[0]
    return out if len(values) > 1 else out[0]


def start_far(links, near):
    by_x, by_y = near
    cut = by_x.shape[0] // 2
    return links.x(by_y[:cut]), links.y(by_x[cut:])


class Home:
    def __init__(self, links):
        self.links = links

    def first(self, pieces):
        x_first, y_first, self.k10_low, self.k00, self.k01_top = pieces
        self.x_got, self.y_got = self.links.x(x_first), self.links.y(y_first)

    def middle(self):
        half = self.k01_top.shape[0]
        args = (self.k01_top, self.x_got, self.k10_low, self.y_got)
        shape = array(*self.k01_top.shape)
        out_y, out_x = small_call(add_mid_kernel, "add_mid", args, [shape, shape])
        return out_y, out_x

    def second(self, out_y, out_x):
        self.y_last, self.x_last = self.links.y(out_y), self.links.x(out_x)

    def last(self, done, apart):
        y_last, x_last = after(done, self.y_last, self.x_last)
        args = (self.k00, self.x_got, self.y_got, y_last, x_last)
        (total,) = small_call(add_last_kernel, "add_last", args, [array(*self.k00.shape)])
        self.home = self.links.z_sum_apart(total)[None] if apart else self.links.z_sum(total)
        return total

    def value(self, done, scale):
        return jnp.sum(after(done, self.home).astype(f32), axis=0) * scale


def own_slot(
    clips,
    cotangent,
    clip_live,
    qkv_weight,
    q_bias,
    v_bias,
    proj_weight,
    fc1_weight,
    fc1_bias,
    fc2_weight,
    ln_gains,
    ln_biases,
    out_bias,
):
    links = Links()
    slot_count, shard_rows, width = clips.shape
    wide_count = lax.axis_size("wide")
    length = 2 * shard_rows
    block = qkv_weight.shape[0]
    heads_cols = qkv_weight.shape[2]
    hidden_here = fc1_weight.shape[1]
    grad_scale = 1.0 / math.sqrt(wide_count * slot_count * length)
    wide_at = lax.axis_index("wide")
    t = lax.axis_index("tp")
    z_at, y_at, c_at = wide_at // 4, (wide_at // 2) % 2, wide_at % 2
    qkv_cols = 3 * heads_cols
    pick = lambda both, at: lax.dynamic_index_in_dim(both, at, 0, keepdims=False)
    row = lambda vector: vector.reshape(1, -1)

    sent_rows = jnp.concatenate([pick(clips, 1 - t), pick(cotangent, 1 - t)], axis=0)
    q_shard, sent_rows = after((), qkv_weight.reshape(block, qkv_cols), sent_rows)
    two_shard = jnp.concatenate([fc1_weight, proj_weight.T], axis=1)
    along_two = links.z_all(two_shard)
    steps_one = [links.from_z(q_shard, k) for k in range(1, links.nz)]
    got_rows = links.x(sent_rows)
    far_small = jnp.concatenate([q_bias, v_bias, fc1_bias]).reshape(-1, 128)
    far_small = links.x(far_small).reshape(-1)

    spot = jnp.arange(width)
    rel = spot // block
    kc, ky, kz = rel // (2 * links.nz), (rel // links.nz) % 2, rel % links.nz
    home = (kz * 2 + (y_at ^ ky)) * 2 + (c_at ^ kc)
    order = spot[:, None] == (home * block + spot % block)[None, :]
    order_b = order.astype(bf16)
    order_f = order.astype(f32)
    vectors = jnp.dot(
        jnp.concatenate([ln_gains, ln_biases, out_bias], axis=0),
        order_f,
        precision=lax.Precision.HIGHEST,
    )
    gains, shifts, outs = (
        (vectors[2 * i : 2 * i + 1], vectors[2 * i + 1 : 2 * i + 2]) for i in range(3)
    )
    live = jnp.full((1, width), pick(clip_live, t).astype(f32))
    along_one = jnp.zeros((links.nz * block, qkv_cols), bf16)
    for step, piece in enumerate([q_shard] + steps_one):
        at = (z_at + step) % links.nz * block
        along_one = lax.dynamic_update_slice(along_one, piece, (at, 0))
    got_rows, far_small = after(along_one, got_rows, far_small)
    near_one = links.x(along_one), links.y(along_one)
    x, h1, h1_t = enter(pick(clips, t), got_rows[:shard_rows], order_b, gains[0], shifts[0])
    e, e_t = enter_cot(pick(cotangent, t), got_rows[shard_rows:], order_b, live)
    half = width // 2
    twin_rows = jnp.concatenate([e_t[half:], h1_t[half:]], axis=0)
    near_one, along_two, twin_rows, fc2_turned = after(
        (twin_rows, h1, e), near_one, along_two, twin_rows, fc2_weight.T
    )
    along_three = links.z_all(after(along_two, fc2_turned))
    far_one = start_far(links, near_one)
    other_one = [links.c(piece) for piece in (after(near_one, along_one), *near_one)]
    other_one, along_two = after((), other_one, along_two)
    near_two = links.x(along_two), links.y(along_two)
    far_one, twin_rows = after(other_one, far_one, twin_rows)
    other_one += [links.c(piece) for piece in far_one]
    twin_rows = links.c(twin_rows)
    twin_rows, other_one = after((), twin_rows, other_one)
    w_one = [along_one, *near_one, *far_one, *other_one]
    zero_row = jnp.zeros((heads_cols,), f32)
    biases = jnp.stack(
        [
            jnp.concatenate([q_bias, zero_row, v_bias]),
            jnp.concatenate(
                [far_small[:heads_cols], zero_row, far_small[heads_cols : 2 * heads_cols]]
            ),
        ]
    )[:, None]
    fc1_biases = row(jnp.concatenate([fc1_bias, far_small[2 * heads_cols :]]))
    qkv = project(h1, w_one, biases)
    attn, lse = attend_fwd(qkv)

    near_two, lse_rows = after(attn, near_two, lse.T)
    far_two = start_far(links, near_two)
    other_two = [links.c(piece) for piece in (after(near_two, along_two), *near_two)]
    other_two, along_three = after((), other_two, along_three)

    near_three = links.x(along_three), links.y(along_three)
    far_two = after(other_two, far_two)
    other_two += [links.c(piece) for piece in far_two]
    w_two = [along_two, *near_two, *far_two, *other_two]
    y, h2, h2_t = join_heads(attn, x, w_two, hidden_here, outs[0], gains[1], shifts[1])
    hidden, slope = expand(h2, w_two, fc1_biases, hidden_here)
    near_three, hidden, slope, h2_t, along_three = after(
        (), near_three, hidden, slope, h2_t, along_three
    )

    far_three = start_far(links, near_three)
    twin_hidden = links.c(hidden)
    other_three = [links.c(piece) for piece in (along_three, near_three[0])]
    far_three, twin_hidden, other_three, near_three, h2_sent, attn_sent = after(
        (), far_three, twin_hidden, other_three, near_three, h2_t[half:], attn
    )

    quarter = width // 8
    stack = lambda one, two: jnp.concatenate([one[...], two[...]], axis=0)
    join = lambda one, two: jnp.concatenate([one[...], two[...]], axis=1)
    tiles = hidden_here // TILE
    left_at = lambda at: pl.BlockSpec((half, length), lambda s: (at, 0))

    def tile_spec(count):
        def at(s):
            tile = jnp.minimum(s % count, tiles - 1)
            return (0, jnp.where(s < count, tiles, 0) + tile)

        return pl.BlockSpec((length, TILE), at)

    attn_spec = lambda count: pl.BlockSpec((length, TILE), lambda s: (0, 1 - s // count))

    def grad_fc2():
        terms = lambda refs, kind: (join(*refs[:2]), stack(*refs[2:]))
        args = [e_t, twin_rows, hidden, twin_hidden]
        specs = [left_at(0), left_at(0)] + [tile_spec(tiles)] * 2
        return both_sides(args, specs, (0,), terms, "grad_fc2", tiles)

    def grad_two():
        count = tiles + 1

        def terms(refs, kind):
            return join(*refs[4 * kind :][:2]), stack(*refs[4 * kind + 2 :][:2])

        args = [h2_t, twin_h2, du, twin_du, da_t, twin_da, attn, twin_attn]
        specs = [left_at(0)] * 2 + [tile_spec(count)] * 2
        specs += [left_at(0)] * 2 + [attn_spec(count)] * 2
        return both_sides(args, specs, (0, tiles), terms, "grad_two", count)

    def grad_qkv():
        narrow = TILE // 2
        count = qkv_cols // narrow

        def terms(refs, kind):
            return join(*refs[:2]), jnp.concatenate([refs[2][0], refs[3][0]], axis=0)

        def at(s):
            tile, side = s % count, 1 - s // count
            return (tile // 2, 0, 2 * side + tile % 2)

        args = [h1_t, twin_rows, dp, twin_dp]
        specs = [left_at(0), left_at(1)] + [pl.BlockSpec((1, length, narrow), at)] * 2
        return both_sides(args, specs, (0,), terms, "grad_qkv", count, narrow, links.nz)

    def enter_window(done, *homes):
        for home in homes:
            home.x_got, home.y_got = after(done, home.x_got, home.y_got)

    home_fc2, home_two, home_qkv = Home(links), Home(links), Home(links)

    other_three += [links.c(piece) for piece in (near_three[1], *far_three)]
    twin_h2 = links.c(h2_sent)
    pieces = grad_fc2()
    pieces, other_three, twin_h2, attn_sent = after(
        (), pieces, other_three, twin_h2, attn_sent
    )
    w_fc2 = [along_three, *near_three, *far_three, *other_three]

    home_fc2.first(pieces)
    twin_attn = links.c(attn_sent)
    du, fc1b_sum = hidden_back(e, slope, w_fc2)
    mid, da, da_t, da_t_far, second_sums = second_back(du, w_two, hidden_here, y, e, gains[1])
    enter_window(da, home_fc2)
    du, da, da_t, da_t_far, twin_attn = after(
        home_fc2.x_got, du, da, da_t, da_t_far, twin_attn
    )

    twin_du = links.c(du)
    twin_da = links.c(da_t_far)
    home_fc2.second(*home_fc2.middle())
    d_heads = heads_back(da, w_two, hidden_here)
    twin_du, twin_da = after(d_heads, twin_du, twin_da)
    pieces = grad_two()
    pieces, d_heads, home_fc2.y_last, home_fc2.x_last = after(
        (), pieces, d_heads, home_fc2.y_last, home_fc2.x_last
    )

    home_two.first(pieces)
    moved = home_fc2.last(pieces, True)
    dp, q_sums, v_sums = attend_bwd(qkv, after(moved, d_heads), lse_rows)
    grad_near, grad_sent_rows, first_sums = first_back(
        dp, w_one, x, mid, gains[0], order_b
    )
    enter_window(grad_near, home_two)
    dp, first_sums = after(home_two.x_got, dp, first_sums)

    twin_dp = links.c(dp)
    moved = home_two.middle()
    home_two.second(*moved)
    sums = jnp.concatenate(
        [first_sums[:1], second_sums[:1], first_sums[1:], second_sums[1:]], axis=0
    )
    sums = lax.dot_general(
        after(moved, sums), order_f, (((1,), (1,)), ((), ())), precision=lax.Precision.HIGHEST
    )

    def placed(both):
        size = both.shape[1] // 2
        return jnp.where(t == 0, both[0], jnp.concatenate([both[0, size:], both[0, :size]]))

    small = [sums.reshape(-1), placed(q_sums), placed(v_sums), placed(fc1b_sum)]
    small = jnp.concatenate(small).reshape(-1, 128)
    small_got = links.c(after(moved, small))
    twin_dp, small_got = after(moved, twin_dp, small_got)
    small = small + small_got
    small_got = links.flip(small, 1)
    *pieces, by_z = grad_qkv()
    pieces, by_z, home_two.y_last, home_two.x_last, small, small_got = after(
        (), pieces, by_z, home_two.y_last, home_two.x_last, small, small_got
    )

    home_qkv.first(pieces)
    by_z = links.z_sum(by_z.reshape(-1, by_z.shape[-1]))
    small = small + small_got
    small_got = links.x(small)
    moved = home_two.last(pieces, True)
    enter_window(moved, home_qkv)
    moved, small, small_got, hidden_out, grad_sent_rows = after(
        (), home_qkv.middle(), small, small_got, hidden, grad_sent_rows
    )

    home_qkv.second(*moved)
    grad_got = links.x(grad_sent_rows)
    small = small + small_got
    small_got = links.y(small)
    out_near, out_sent = layer_out(hidden_out, w_fc2, y, outs[1], live, order_b)
    moved = home_qkv.last(out_near, False)
    moved, out_sent, small, small_got = after((), moved, out_sent, small, small_got)

    by_z = jnp.sum(after(moved, by_z).astype(f32), axis=0)
    v_got = links.x(by_z[quarter:].astype(bf16))
    out_got = links.x(out_sent)
    small = small + small_got
    bit = 2
    while bit < links.nz:
        small = small + links.flip(small, bit)
        bit *= 2
    by_x = by_z[:quarter] + v_got.astype(f32)
    by_x, small, out_got, grad_got, home_two.home, home_fc2.home = after(
        (), by_x, small, out_got, grad_got, home_two.home, home_fc2.home
    )
    v_got = links.y(by_x[block:].astype(bf16))
    g_v = (by_x[:block] + v_got.astype(f32)) * grad_scale
    small = small.reshape(-1) * grad_scale
    sums = small[: 6 * width].reshape(6, width)
    own = lambda first, size: lax.dynamic_slice_in_dim(small, first + t * size, size, 0)
    g_qkv = home_qkv.value(g_v, grad_scale)
    g_fc2 = home_fc2.value(moved, grad_scale)
    g_two = home_two.value(moved, grad_scale)

    def both_slots(near, got):
        return jnp.where(t == 0, jnp.stack([near, got]), jnp.stack([got, near]))

    return (
        both_slots(out_near, out_got),
        both_slots(grad_near, grad_got).astype(f32),
        jnp.concatenate([g_qkv, g_v], axis=1).reshape(block, 3, heads_cols),
        own(6 * width, heads_cols),
        own(6 * width + 2 * heads_cols, heads_cols),
        g_two[:, hidden_here:].T,
        g_two[:, :hidden_here],
        own(6 * width + 4 * heads_cols, hidden_here),
        g_fc2.T,
        sums[0:2],
        sums[2:4],
        sums[4:6],
    )


def solution(mesh):
    body = own_slot if fits_own_slot(mesh) else shared_slots
    return jax.shard_map(
        body,
        mesh=mesh,
        in_specs=(
            P("wide", "tp", None),
            P("wide", "tp", None),
            P("wide"),
            P("wide", None, "tp"),
            P("tp"),
            P("tp"),
            P("tp", "wide"),
            P("wide", "tp"),
            P("tp"),
            P("tp", "wide"),
            P(),
            P(),
            P(),
        ),
        out_specs=(
            P("wide", "tp", None),
            P("wide", "tp", None),
            P("wide", None, "tp"),
            P("tp"),
            P("tp"),
            P("tp", "wide"),
            P("wide", "tp"),
            P("tp"),
            P("tp", "wide"),
            P(),
            P(),
            P(),
        ),
        check_vma=False,
    )
```

```python
from functools import partial
import math

import jax
import jax.numpy as jnp
from jax import lax
from jax.experimental import pallas as pl
from jax.experimental.pallas import tpu as pltpu
from jax.sharding import PartitionSpec as P

HEAD_DIM = 64


norm_eps = 1e-06
root_half = 1.0 / math.sqrt(2.0)
inv_root_two_pi = 1.0 / math.sqrt(2.0 * math.pi)


def layer_norm(in_rows, gain_row, shift_row):
    row_mean = jnp.mean(in_rows, axis=-1, keepdims=True)
    centred = in_rows - row_mean
    spread = jnp.mean(centred * centred, axis=-1, keepdims=True)
    inverse = lax.rsqrt(spread + norm_eps)
    unit_rows = centred * inverse
    return (unit_rows * gain_row + shift_row, unit_rows, inverse)


def norm_back(grad_rows, unit_rows, inverse, gain_row):
    scaled = grad_rows * gain_row
    mean_one = jnp.mean(scaled, axis=-1, keepdims=True)
    second = jnp.mean(scaled * unit_rows, axis=-1, keepdims=True)
    return inverse * (scaled - mean_one - unit_rows * second)


def contract_last(left_op, right_op):
    return lax.dot_general(
        left_op, right_op, (((1,), (1,)), ((), ())), preferred_element_type=jnp.float32
    )


def contract_first(left_op, right_op):
    return lax.dot_general(
        left_op, right_op, (((0,), (0,)), ((), ())), preferred_element_type=jnp.float32
    )


def attend_block(query, key_rows, value_rows):
    scores = jnp.einsum("qhd,khd->hqk", query, key_rows, preferred_element_type=jnp.float32)
    row_max = jnp.max(scores, axis=-1, keepdims=True)
    weights = jnp.exp(scores - row_max)
    row_sum = jnp.sum(weights, axis=-1, keepdims=True)
    prob_rows = (weights / row_sum).astype(jnp.bfloat16)
    mixed_rows = jnp.einsum(
        "hqk,khd->qhd", prob_rows, value_rows, preferred_element_type=jnp.float32
    )
    return (mixed_rows, row_max[..., 0] + jnp.log(row_sum[..., 0]))


def attend_back(query, grad_rows, log_total, key_rows, value_rows):
    scores = jnp.einsum("qhd,khd->hqk", query, key_rows, preferred_element_type=jnp.float32)
    prob_rows = jnp.exp(scores - log_total[..., None])
    dprobs = jnp.einsum("qhd,khd->hqk", grad_rows, value_rows, preferred_element_type=jnp.float32)
    row_delta = jnp.sum(prob_rows * dprobs, axis=-1, keepdims=True)
    dscores = (prob_rows * (dprobs - row_delta)).astype(jnp.bfloat16)
    dquery = jnp.einsum("hqk,khd->qhd", dscores, key_rows, preferred_element_type=jnp.float32)
    d_keys = jnp.einsum("hqk,qhd->khd", dscores, query, preferred_element_type=jnp.float32)
    dvalues = jnp.einsum(
        "hqk,qhd->khd",
        prob_rows.astype(jnp.bfloat16),
        grad_rows,
        preferred_element_type=jnp.float32,
    )
    return (dquery, d_keys, dvalues)


def shared_slots(
    clips,
    cotangent,
    clip_live,
    qkv_weight,
    q_bias,
    v_bias,
    proj_weight,
    fc1_weight,
    fc1_bias,
    fc2_weight,
    ln_gains,
    ln_biases,
    out_bias,
):
    tp_count = lax.axis_size("tp")
    wide_count = lax.axis_size("wide")
    slot_count, shard_rows, width = clips.shape
    length = shard_rows * tp_count
    local_cols = qkv_weight.shape[2]
    heads_here = local_cols // HEAD_DIM
    hidden_here = fc1_weight.shape[1]
    q_scale = 1.0 / math.sqrt(HEAD_DIM)
    grad_scale = 1.0 / math.sqrt(wide_count * slot_count * length)
    block_rows = 512
    blocks = length // block_rows
    tp_place = lax.axis_index("tp")
    live_slots = clip_live.astype(jnp.float32)
    qv_bias = jnp.stack([q_bias, v_bias])
    own_weights = (qkv_weight, proj_weight, fc1_weight, fc2_weight)

    def one_slot(state_in, inputs):
        rows_in, cot_in, live_one = inputs
        tied_weights = lax.optimization_barrier((own_weights, rows_in))[0]
        w_qkv, w_proj, w_fc1, w_fc2 = (
            lax.all_gather(tied_weights[0], "wide", axis=0, tiled=True),
            lax.all_gather(tied_weights[1], "wide", axis=1, tiled=True),
            lax.all_gather(tied_weights[2], "wide", axis=0, tiled=True),
            lax.all_gather(tied_weights[3], "wide", axis=1, tiled=True),
        )
        x_rows = rows_in.astype(jnp.float32)
        norm_one, unit_one, inv_one = layer_norm(x_rows, ln_gains[0], ln_biases[0])
        h1_full = lax.all_gather(norm_one.astype(jnp.bfloat16), "tp", axis=0, tiled=True)
        qkv_flat = w_qkv.reshape(width, 3 * local_cols)
        projected = jnp.dot(h1_full, qkv_flat, preferred_element_type=jnp.float32).reshape(
            length, 3, local_cols
        )
        query = (
            ((projected[:, 0] + qv_bias[0]) * q_scale)
            .astype(jnp.bfloat16)
            .reshape(length, heads_here, HEAD_DIM)
        )
        key_rows = projected[:, 1].astype(jnp.bfloat16).reshape(length, heads_here, HEAD_DIM)
        value_rows = (
            (projected[:, 2] + qv_bias[1])
            .astype(jnp.bfloat16)
            .reshape(length, heads_here, HEAD_DIM)
        )
        query_blocks = query.reshape(blocks, block_rows, heads_here, HEAD_DIM)
        mixed_blocks, log_totals = lax.map(
            partial(attend_block, key_rows=key_rows, value_rows=value_rows), query_blocks
        )
        attn_out = mixed_blocks.reshape(length, local_cols).astype(jnp.bfloat16)
        attn_sum = lax.psum_scatter(
            jnp.dot(attn_out, w_proj, preferred_element_type=jnp.float32),
            "tp",
            scatter_dimension=0,
            tiled=True,
        )
        mid_rows = x_rows + attn_sum + out_bias[0]
        norm_two, unit_two, inv_two = layer_norm(mid_rows, ln_gains[1], ln_biases[1])
        h2_full = lax.all_gather(norm_two.astype(jnp.bfloat16), "tp", axis=0, tiled=True)
        pre_act = jnp.dot(h2_full, w_fc1, preferred_element_type=jnp.float32) + fc1_bias
        cdf_part = 0.5 * (1.0 + lax.erf(pre_act * root_half))
        hidden = (pre_act * cdf_part).astype(jnp.bfloat16)
        mlp_sum = lax.psum_scatter(
            jnp.dot(hidden, w_fc2, preferred_element_type=jnp.float32).astype(jnp.bfloat16),
            "tp",
            scatter_dimension=0,
            tiled=True,
        ).astype(jnp.float32)
        block_out = (live_one * (mid_rows + mlp_sum + out_bias[1])).astype(jnp.bfloat16)
        out_grad = live_one * cot_in.astype(jnp.float32)
        out_full = lax.all_gather(out_grad.astype(jnp.bfloat16), "tp", axis=0, tiled=True)
        g_fc2 = contract_first(hidden, out_full)
        act_grad = contract_last(out_full, w_fc2)
        slope = cdf_part + pre_act * jnp.exp(-0.5 * pre_act * pre_act) * inv_root_two_pi
        pre_grad = act_grad * slope
        pre_grad_b = pre_grad.astype(jnp.bfloat16)
        g_fc1 = contract_first(h2_full, pre_grad_b)
        g_fc1b = jnp.sum(pre_grad, axis=0)
        norm_two_grad = lax.psum_scatter(
            contract_last(pre_grad_b, w_fc1), "tp", scatter_dimension=0, tiled=True
        )
        mid_grad = out_grad + norm_back(norm_two_grad, unit_two, inv_two, ln_gains[1])
        attn_full = lax.all_gather(mid_grad.astype(jnp.bfloat16), "tp", axis=0, tiled=True)
        g_proj = contract_first(attn_out, attn_full)
        mixed_grad = (
            contract_last(attn_full, w_proj)
            .astype(jnp.bfloat16)
            .reshape(blocks, block_rows, heads_here, HEAD_DIM)
        )

        def back_block(block_state, pieces):
            query_b, grad_b, lse_b = pieces
            d_query, d_keys, d_values = attend_back(query_b, grad_b, lse_b, key_rows, value_rows)
            return ((block_state[0] + d_keys, block_state[1] + d_values), d_query)

        empty_kv = jnp.zeros((length, heads_here, HEAD_DIM), jnp.float32)
        (key_grad, value_grad), query_grad = lax.scan(
            back_block, (empty_kv, empty_kv), (query_blocks, mixed_grad, log_totals)
        )
        query_grad = query_grad.reshape(length, local_cols) * q_scale
        key_grad = key_grad.reshape(length, local_cols)
        value_grad = value_grad.reshape(length, local_cols)
        g_qvb = jnp.stack([jnp.sum(query_grad, axis=0), jnp.sum(value_grad, axis=0)])
        proj_grads = (
            jnp.stack([query_grad, key_grad, value_grad], axis=1)
            .astype(jnp.bfloat16)
            .reshape(length, 3 * local_cols)
        )
        g_qkv = contract_first(h1_full, proj_grads).reshape(width, 3, local_cols)
        norm_one_grad = lax.psum_scatter(
            contract_last(proj_grads, qkv_flat).astype(jnp.bfloat16),
            "tp",
            scatter_dimension=0,
            tiled=True,
        ).astype(jnp.float32)
        in_grad = mid_grad + norm_back(norm_one_grad, unit_one, inv_one, ln_gains[0])
        gain_part = jnp.stack(
            [jnp.sum(norm_one_grad * unit_one, axis=0), jnp.sum(norm_two_grad * unit_two, axis=0)]
        )
        shift_part = jnp.stack([jnp.sum(norm_one_grad, axis=0), jnp.sum(norm_two_grad, axis=0)])
        bias_part = jnp.stack([jnp.sum(mid_grad, axis=0), jnp.sum(out_grad, axis=0)])
        summed = (
            lax.psum_scatter(
                g_qkv.astype(jnp.bfloat16), "wide", scatter_dimension=0, tiled=True
            ).astype(jnp.float32),
            lax.psum_scatter(
                g_proj.astype(jnp.bfloat16), "wide", scatter_dimension=1, tiled=True
            ).astype(jnp.float32),
            lax.psum_scatter(
                g_fc1.astype(jnp.bfloat16), "wide", scatter_dimension=0, tiled=True
            ).astype(jnp.float32),
            lax.psum_scatter(
                g_fc2.astype(jnp.bfloat16), "wide", scatter_dimension=1, tiled=True
            ).astype(jnp.float32),
        )
        weight_acc = jax.tree.map(jnp.add, state_in[0], summed)
        vector_acc = jax.tree.map(
            jnp.add, state_in[1], (gain_part, shift_part, bias_part, g_qvb, g_fc1b)
        )
        return ((weight_acc, vector_acc), (block_out, in_grad))

    weight_zero = tuple((jnp.zeros(shard_in.shape, jnp.float32) for shard_in in own_weights))
    vector_zero = (
        jnp.zeros((2, width), jnp.float32),
        jnp.zeros((2, width), jnp.float32),
        jnp.zeros((2, width), jnp.float32),
        jnp.zeros((2, local_cols), jnp.float32),
        jnp.zeros((hidden_here,), jnp.float32),
    )
    (weight_sums, vector_acc), (block_out, clips_grad) = lax.scan(
        one_slot, (weight_zero, vector_zero), (clips, cotangent, live_slots)
    )
    gain_acc, shift_acc, bias_acc, qvb_acc, fc1b_acc = vector_acc
    qvb_pad = lax.dynamic_update_slice(
        jnp.zeros((2, width), jnp.float32), qvb_acc, (0, tp_place * local_cols)
    )
    fc1b_pad = lax.dynamic_update_slice(
        jnp.zeros((hidden_here * tp_count,), jnp.float32), fc1b_acc, (tp_place * hidden_here,)
    )
    gain_sum, shift_sum, bias_sum, qvb_sum, fc1b_sum = lax.psum(
        (gain_acc, shift_acc, bias_acc, qvb_pad, fc1b_pad), ("wide", "tp")
    )
    qvb_own = lax.dynamic_slice_in_dim(qvb_sum, tp_place * local_cols, local_cols, 1)
    fc1b_own = lax.dynamic_slice_in_dim(fc1b_sum, tp_place * hidden_here, hidden_here, 0)
    return (
        block_out,
        clips_grad,
        weight_sums[0] * grad_scale,
        qvb_own[0] * grad_scale,
        qvb_own[1] * grad_scale,
        weight_sums[1] * grad_scale,
        weight_sums[2] * grad_scale,
        fc1b_own * grad_scale,
        weight_sums[3] * grad_scale,
        gain_sum * grad_scale,
        shift_sum * grad_scale,
        bias_sum * grad_scale,
    )


AXES = ("wide", "tp")
PAIR = 128
TILE = 512
MIB = 1024 * 1024
GRANT = {"project": 60, "hidden_back": 60, "heads_back": 60, "layer_out": 60, "join_heads": 30, "expand": 36, "enter": 30, "enter_cot": 30, "grad_fc2": 36}
WIDE = 1024
bf16 = jnp.bfloat16
f32 = jnp.float32


def fits_own_slot(mesh):
    return mesh.shape["tp"] == 2 and mesh.shape["wide"] % 4 == 0


def nt_dot(left_op, right_op):
    return lax.dot_general(
        left_op, right_op, (((1,), (1,)), ((), ())), preferred_element_type=f32
    )


def nn_dot(left_op, right_op):
    return lax.dot_general(
        left_op, right_op, (((1,), (0,)), ((), ())), preferred_element_type=f32
    )


def kernel_call(body, name, grid, in_specs, out_specs, out_shape, scratch=(), scalars=0):
    return pl.pallas_call(
        body,
        grid_spec=pltpu.PrefetchScalarGridSpec(
            num_scalar_prefetch=scalars,
            grid=grid,
            in_specs=in_specs,
            out_specs=out_specs,
            scratch_shapes=list(scratch),
        ),
        out_shape=out_shape,
        compiler_params=pltpu.CompilerParams(vmem_limit_bytes=GRANT.get(name, 60) * MIB),
        cost_estimate=pl.CostEstimate(flops=1, bytes_accessed=1, transcendentals=0),
        name=name,
    )


def whole(shape):
    return pl.BlockSpec(shape, lambda *at: (0,) * len(shape))


def array(*shape, dtype=bf16):
    return jax.ShapeDtypeStruct(shape, dtype)


def norm_stats(rows):
    row_mean = jnp.mean(rows, axis=-1, keepdims=True)
    centred = rows - row_mean
    spread = jnp.mean(centred * centred, axis=-1, keepdims=True)
    inverse = lax.rsqrt(spread + norm_eps)
    return centred * inverse, inverse


NEAR = (0, 2, 5, 7)
FAR = (1, 3, 4, 6, 8, 9)


class Pieces:
    def __init__(self, pieces, columns, first=0, tile=WIDE):
        self.pieces, self.columns, self.first = pieces, columns, first
        self.tile = min(tile, columns)
        self.tiles = columns // self.tile
        self.args = list(pieces)
        self.specs = [pl.BlockSpec(memory_space=pl.ANY)] * len(pieces)
        rows = sum(pieces[i].shape[0] for i in NEAR)
        self.scratch = [
            pltpu.VMEM((2, rows, columns), bf16),
            pltpu.SemaphoreType.DMA((self.tiles, len(pieces))),
        ]

    def copies(self, refs, side, tile, w_ref, sems):
        at, found = 0, []
        for index in FAR if side else NEAR:
            rows = self.pieces[index].shape[0]
            found.append(
                pltpu.make_async_copy(
                    refs[index].at[:, pl.ds(self.first + tile * self.tile, self.tile)],
                    w_ref.at[side, pl.ds(at, rows), pl.ds(tile * self.tile, self.tile)],
                    sems.at[tile, index],
                )
            )
            at += rows
        return found

    def start(self, refs, w_ref, sems):
        for side in range(2):
            for tile in range(self.tiles):
                for copy in self.copies(refs, side, tile, w_ref, sems):
                    copy.start()

    def wait(self, refs, side, tile, w_ref, sems):
        for copy in self.copies(refs, side, tile, w_ref, sems):
            copy.wait()

    def get(self, refs, side, tile, w_ref, sems):
        self.wait(refs, side, tile, w_ref, sems)
        return w_ref[side, :, pl.ds(tile * self.tile, self.tile)]

    def each_step(self, step, refs, w_ref, sems, work):
        pl.when(step == 0)(lambda: self.start(refs, w_ref, sems))
        for side in range(2):
            for tile in range(self.tiles):

                @pl.when(step == side * self.tiles + tile)
                def _():
                    work(side, tile, self.get(refs, side, tile, w_ref, sems))


def enter_kernel(own_ref, got_ref, order_ref, gain_ref, shift_ref, x_ref, h_ref, ht_ref):
    half = own_ref.shape[0]
    for part, ref in enumerate((own_ref, got_ref)):
        rows = nn_dot(ref[...], order_ref[...])
        here = pl.ds(part * half, half)
        x_ref[here, :] = rows.astype(bf16)
        unit, _ = norm_stats(rows)
        normed = (unit * gain_ref[...] + shift_ref[...]).astype(bf16)
        h_ref[here, :] = normed
        ht_ref[:, here] = normed.T


def enter(own, got, order_b, gain, shift):
    half, width = own.shape
    length = 2 * half
    return kernel_call(
        enter_kernel,
        "enter",
        (1,),
        [whole((half, width))] * 2 + [whole((width, width))] + [whole((1, width))] * 2,
        [whole((length, width))] * 2 + [whole((width, length))],
        [array(length, width)] * 2 + [array(width, length)],
    )(own, got, order_b, gain, shift)


def cot_kernel(own_ref, got_ref, order_ref, live_ref, e_ref, et_ref):
    half = own_ref.shape[0]
    for part, ref in enumerate((own_ref, got_ref)):
        rows = (live_ref[...] * nn_dot(ref[...], order_ref[...])).astype(bf16)
        here = pl.ds(part * half, half)
        e_ref[here, :] = rows
        et_ref[:, here] = rows.T


def enter_cot(own, got, order_b, live):
    half, width = own.shape
    length = 2 * half
    return kernel_call(
        cot_kernel,
        "enter_cot",
        (1,),
        [whole((half, width))] * 2 + [whole((width, width)), whole((1, width))],
        [whole((length, width)), whole((width, length))],
        [array(length, width), array(width, length)],
    )(own, got, order_b, live)


def project(h, pieces, biases):
    length, width = h.shape
    each = pieces[0].shape[1] // 3
    load = Pieces(pieces, 3 * each, 0, each)
    scales = (1.0 / math.sqrt(HEAD_DIM), None, None)

    def body(h_ref, bias_ref, *refs):
        refs, (out_ref, w_ref, sems) = refs[:-3], refs[-3:]

        def work(side, tile, weight):
            acc = nn_dot(h_ref[...], weight) + bias_ref[0]
            out_ref[0] = (acc if scales[tile] is None else acc * scales[tile]).astype(bf16)

        load.each_step(pl.program_id(0), refs, w_ref, sems, work)

    return kernel_call(
        body,
        "project",
        (6,),
        [whole((length, width)), pl.BlockSpec((1, 1, each), lambda s: (s // 3, 0, s % 3))]
        + load.specs,
        pl.BlockSpec((1, length, each), lambda s: (s % 3, 0, s // 3)),
        array(3, length, width),
        load.scratch,
    )(h, biases, *load.args)


def attend_kernel(q_ref, k_ref, v_ref, o_ref, lse_ref):
    pair = pl.program_id(0)
    rows = q_ref.shape[1]
    lanes = lax.broadcasted_iota(jnp.int32, (rows, PAIR), 1)
    keys = k_ref[0]
    values = v_ref[0]
    total = jnp.zeros((rows, PAIR), f32)
    for half in range(2):
        mask = (lanes // HEAD_DIM) == half
        query = jnp.where(mask, q_ref[0], jnp.zeros_like(keys))
        scores = nt_dot(query, keys)
        row_max = jnp.max(scores, axis=-1, keepdims=True)
        weights = jnp.exp(scores - row_max)
        row_sum = jnp.sum(weights, axis=-1, keepdims=True)
        probs = (weights * (1.0 / row_sum)).astype(bf16)
        mixed = nn_dot(probs, values)
        total = jnp.where(mask, mixed, total)
        lse = row_max + jnp.log(row_sum)
        lse_ref[...] = jnp.where(lanes == 2 * pair + half, lse, lse_ref[...])
    o_ref[...] = total.astype(bf16)


def head_spec(length, index):
    return pl.BlockSpec((1, length, PAIR), lambda i: (index, 0, i))


def attend_fwd(qkv):
    _, length, width = qkv.shape
    return kernel_call(
        attend_kernel,
        "attend_fwd",
        (width // PAIR,),
        [head_spec(length, j) for j in range(3)],
        [pl.BlockSpec((length, PAIR), lambda i: (0, i)), whole((length, PAIR))],
        [array(length, width), array(length, PAIR, dtype=f32)],
    )(qkv, qkv, qkv)


def join_heads(attn, x, pieces, first, bias, gain, shift):
    length, width = x.shape
    load = Pieces(pieces, TILE, first)

    def body(attn_ref, x_ref, bias_ref, gain_ref, shift_ref, *refs):
        refs, (y_ref, h_ref, ht_ref, w_ref, sems) = refs[:-5], refs[-5:]
        load.start(refs, w_ref, sems)
        load.wait(refs, 0, 0, w_ref, sems)
        load.wait(refs, 1, 0, w_ref, sems)
        half = length // 2
        for part in range(2):
            here = pl.ds(part * half, half)
            rows = nt_dot(attn_ref[here, :TILE], w_ref[0]) + nt_dot(attn_ref[here, TILE:], w_ref[1])
            rows = x_ref[here, :].astype(f32) + rows + bias_ref[...]
            y_ref[here, :] = rows
            unit, _ = norm_stats(rows)
            normed = (unit * gain_ref[...] + shift_ref[...]).astype(bf16)
            h_ref[here, :] = normed
            ht_ref[:, here] = normed.T

    return kernel_call(
        body,
        "join_heads",
        (1,),
        [whole((length, width))] * 2 + [whole((1, width))] * 3 + load.specs,
        [whole((length, width))] * 2 + [whole((width, length))],
        [array(length, width, dtype=f32), array(length, width), array(width, length)],
        load.scratch,
    )(attn, x, bias, gain, shift, *load.args)


def expand(h, pieces, bias, hidden):
    length, width = h.shape
    load = Pieces(pieces, hidden)

    def body(h_ref, bias_ref, *refs):
        refs, (g_ref, slope_ref, w_ref, sems) = refs[:-4], refs[-4:]

        def work(side, tile, weight):
            pre = nn_dot(h_ref[...], weight) + bias_ref[...]
            cdf = 0.5 * (1.0 + lax.erf(pre * root_half))
            g_ref[...] = (pre * cdf).astype(bf16)
            density = jnp.exp(-0.5 * pre * pre) * inv_root_two_pi
            slope_ref[...] = (cdf + pre * density).astype(bf16)

        load.each_step(pl.program_id(0), refs, w_ref, sems, work)

    block = pl.BlockSpec((length, WIDE), lambda s: (0, s))
    return kernel_call(
        body,
        "expand",
        (2 * load.tiles,),
        [whole((length, width)), pl.BlockSpec((1, WIDE), lambda s: (0, s))] + load.specs,
        [block] * 2,
        [array(length, 2 * hidden)] * 2,
        load.scratch,
    )(h, bias, *load.args)


def hidden_back(e, slope, pieces):
    length, width = e.shape
    hidden = pieces[0].shape[1]
    load = Pieces(pieces, hidden)

    def body(e_ref, slope_ref, *refs):
        refs, (du_ref, sum_ref, w_ref, sems) = refs[:-4], refs[-4:]

        def work(side, tile, weight):
            du = nn_dot(e_ref[...], weight) * slope_ref[...].astype(f32)
            du_ref[...] = du.astype(bf16)
            sum_ref[...] = jnp.sum(du, axis=0, keepdims=True)

        load.each_step(pl.program_id(0), refs, w_ref, sems, work)

    block = pl.BlockSpec((length, WIDE), lambda s: (0, s))
    row = pl.BlockSpec((1, WIDE), lambda s: (0, s))
    return kernel_call(
        body,
        "hidden_back",
        (2 * load.tiles,),
        [whole((length, width)), block] + load.specs,
        [block, row],
        [array(length, 2 * hidden), array(1, 2 * hidden, dtype=f32)],
        load.scratch,
    )(e, slope, *load.args)


def heads_back(da, pieces, first):
    length, width = da.shape
    load = Pieces(pieces, TILE, first)

    def body(da_ref, *refs):
        refs, (out_ref, w_ref, sems) = refs[:-3], refs[-3:]
        load.start(refs, w_ref, sems)
        for side in range(2):
            load.wait(refs, side, 0, w_ref, sems)
            out_ref[:, pl.ds(side * TILE, TILE)] = nn_dot(da_ref[...], w_ref[side]).astype(bf16)

    return kernel_call(
        body,
        "heads_back",
        (1,),
        [whole((length, width))] + load.specs,
        whole((length, 2 * TILE)),
        array(length, 2 * TILE),
        load.scratch,
    )(da, *load.args)


def contract_back(rows, rows_specs, left_of, load, extras, finish, name, outs):
    count = len(extras)
    length, width = extras[0].shape

    def body(*refs):
        rows_refs, refs = refs[: len(rows)], refs[len(rows) :]
        extra_refs, refs = refs[:count], refs[count:]
        w_refs, refs = refs[: len(load.args)], refs[len(load.args) :]
        out_refs, refs = refs[: len(outs)], refs[len(outs) :]
        w_ref, sems, acc_ref, extra_sems = refs[:4]
        held = refs[4:]
        copies = [
            pltpu.make_async_copy(source, target, extra_sems.at[i])
            for i, (source, target) in enumerate(zip(extra_refs, held))
        ]

        def work(side, tile, weight):
            term = nt_dot(left_of(rows_refs), weight)
            if side == 0 and tile == 0:
                for copy in copies:
                    copy.start()
                acc_ref[...] = term
            else:
                acc_ref[...] += term
            if side == 1 and tile == load.tiles - 1:
                for copy in copies:
                    copy.wait()
                finish(acc_ref, held, out_refs)

        load.each_step(pl.program_id(0), w_refs, w_ref, sems, work)

    return kernel_call(
        body,
        name,
        (2 * load.tiles,),
        rows_specs + [pl.BlockSpec(memory_space=pl.ANY)] * count + load.specs,
        [whole(o.shape) for o in outs],
        outs,
        load.scratch
        + [pltpu.VMEM((length, width), f32), pltpu.SemaphoreType.DMA((count,))]
        + [pltpu.VMEM(extra.shape, extra.dtype) for extra in extras],
    )(*rows, *extras, *load.args)


def to_home(rows, order_ref):
    return nt_dot(rows.astype(bf16), order_ref[...]).astype(bf16)


def layer_out(hidden, pieces, y, bias, live, order_b):
    length, width = y.shape
    half = length // 2

    def finish(acc_ref, ins, outs):
        y_ref, bias_ref, live_ref, order_ref = ins
        for part in range(2):
            here = pl.ds(part * half, half)
            rows = live_ref[...] * (y_ref[here, :] + acc_ref[here, :] + bias_ref[...])
            outs[part][...] = to_home(rows, order_ref)

    return contract_back(
        [hidden],
        [pl.BlockSpec((length, WIDE), lambda s, *_: (0, s))],
        lambda refs: refs[0][...],
        Pieces(pieces, pieces[0].shape[1]),
        (y, bias, live, order_b),
        finish,
        "layer_out",
        [array(half, width)] * 2,
    )


def second_back(du, pieces, hidden, y, e, gain):
    length, width = y.shape
    half = length // 2

    def finish(acc_ref, ins, outs):
        y_ref, e_ref, gain_ref = ins
        mid_ref, da_ref, dat_ref, dat_far_ref, sum_ref = outs
        sums = [jnp.zeros((1, width), f32)] * 4
        for part in range(2):
            here = pl.ds(part * half, half)
            unit, inverse = norm_stats(y_ref[here, :])
            grad = acc_ref[here, :]
            e_rows = e_ref[here, :].astype(f32)
            mid = e_rows + norm_back(grad, unit, inverse, gain_ref[...])
            mid_ref[here, :] = mid
            mid_b = mid.astype(bf16)
            da_ref[here, :] = mid_b
            dat_ref[:, here] = mid_b[:, : width // 2].T
            dat_far_ref[:, here] = mid_b[:, width // 2 :].T
            terms = (grad * unit, grad, mid, e_rows)
            sums = [s + jnp.sum(term, axis=0, keepdims=True) for s, term in zip(sums, terms)]
        sum_ref[...] = jnp.concatenate(sums, axis=0)

    return contract_back(
        [du],
        [pl.BlockSpec((length, WIDE), lambda s: (0, s))],
        lambda refs: refs[0][...],
        Pieces(pieces, hidden),
        (y, e, gain),
        finish,
        "second_back",
        [
            array(length, width, dtype=f32),
            array(length, width),
            array(width // 2, length),
            array(width // 2, length),
            array(4, width, dtype=f32),
        ],
    )


def first_back(dp, pieces, x, mid, gain, order_b):
    length, width = x.shape
    half = length // 2

    def finish(acc_ref, ins, outs):
        x_ref, mid_ref, gain_ref, order_ref = ins
        sum_ref = outs[2]
        sums = [jnp.zeros((1, width), f32)] * 2
        for part in range(2):
            here = pl.ds(part * half, half)
            unit, inverse = norm_stats(x_ref[here, :].astype(f32))
            grad = acc_ref[here, :]
            rows = mid_ref[here, :] + norm_back(grad, unit, inverse, gain_ref[...])
            outs[part][...] = to_home(rows, order_ref)
            terms = (grad * unit, grad)
            sums = [s + jnp.sum(term, axis=0, keepdims=True) for s, term in zip(sums, terms)]
        sum_ref[...] = jnp.concatenate(sums, axis=0)

    return contract_back(
        [dp],
        [pl.BlockSpec((3, length, width // 2), lambda s: (0, 0, s))],
        lambda refs: jnp.concatenate([refs[0][j] for j in range(3)], axis=1),
        Pieces(pieces, pieces[0].shape[1], 0, pieces[0].shape[1]),
        (x, mid, gain, order_b),
        finish,
        "first_back",
        [array(half, width)] * 2 + [array(2, width, dtype=f32)],
    )


def attend_back_kernel(q_ref, k_ref, v_ref, g_ref, lse_ref, dp_ref, qs_ref, vs_ref):
    pair = pl.program_id(0)
    rows = q_ref.shape[1]
    lanes = lax.broadcasted_iota(jnp.int32, (rows, PAIR), 1)
    sub = lax.broadcasted_iota(jnp.int32, (PAIR, rows), 0)
    query = q_ref[0]
    keys = k_ref[0]
    values = v_ref[0]
    grads = g_ref[...]
    blank = jnp.zeros_like(keys)
    keys_t = keys.T
    dq_t = jnp.zeros((PAIR, rows), f32)
    dk = jnp.zeros((rows, PAIR), f32)
    dv = jnp.zeros((rows, PAIR), f32)
    for half in range(2):
        mask = (lanes // HEAD_DIM) == half
        scores_t = nt_dot(jnp.where(mask, keys, blank), query)
        lse = lse_ref[pl.ds(2 * pair + half, 1), :]
        probs_t = jnp.exp(scores_t - lse)
        dprobs_t = nt_dot(jnp.where(mask, values, blank), grads)
        delta = jnp.sum(probs_t * dprobs_t, axis=0, keepdims=True)
        ds_t = (probs_t * (dprobs_t - delta)).astype(bf16)
        dv = jnp.where(mask, nn_dot(probs_t.astype(bf16), grads), dv)
        dk = jnp.where(mask, nn_dot(ds_t, query), dk)
        dq_t = jnp.where((sub // HEAD_DIM) == half, nn_dot(keys_t, ds_t), dq_t)
    dq = dq_t.T * (1.0 / math.sqrt(HEAD_DIM))
    dp_ref[0] = dq.astype(bf16)
    dp_ref[1] = dk.astype(bf16)
    dp_ref[2] = dv.astype(bf16)
    qs_ref[...] = jnp.sum(dq, axis=0, keepdims=True)
    vs_ref[...] = jnp.sum(dv, axis=0, keepdims=True)


def attend_bwd(qkv, grads, lse_rows):
    _, length, width = qkv.shape
    row = pl.BlockSpec((1, PAIR), lambda i: (0, i))
    sums = array(1, width, dtype=f32)
    return kernel_call(
        attend_back_kernel,
        "attend_bwd",
        (width // PAIR,),
        [head_spec(length, j) for j in range(3)]
        + [pl.BlockSpec((length, PAIR), lambda i: (0, i)), whole((PAIR, length))],
        [pl.BlockSpec((3, length, PAIR), lambda i: (0, 0, i)), row, row],
        [array(3, length, width), sums, sums],
    )(qkv, qkv, qkv, grads, lse_rows)


def both_sides(args, specs, kinds, terms, name, tiles, width=TILE, z_first=0):
    count = len(args)
    half = args[0].shape[0] // 2
    mid = half // 4
    kept = tiles - 1 if z_first else tiles

    def body(*refs):
        x_ref, y_ref, k10_ref, k00_ref, k01_ref = refs[count : count + 5]
        step = pl.program_id(0)

        def apart(kind):
            left, right = terms(refs[:count], kind)
            acc = nn_dot(left, right).astype(bf16)
            size = acc.shape[0] // 2 // z_first
            for z in range(z_first):
                for ky in range(2):
                    first = (ky * z_first + z) * size
                    refs[-1][z, 0, pl.ds(ky * size, size), :] = acc[first : first + size]

        def run(kind, side):
            left, right = terms(refs[:count], kind)
            acc = nn_dot(left, right).astype(bf16)
            y_ref[...] = acc[3 * mid :]
            if side:
                x_ref[pl.ds(0, mid), :] = acc[:mid]
                x_ref[pl.ds(mid, mid), :] = acc[2 * mid : 3 * mid]
                k10_ref[...] = acc[mid : 2 * mid]
            else:
                k00_ref[...] = acc[: 2 * mid]
                k01_ref[...] = acc[2 * mid : 3 * mid]

        for side in range(2):
            for kind, first in enumerate(kinds):
                last = kinds[kind + 1] if kind + 1 < len(kinds) else tiles
                base = 0 if side else tiles
                here = (step >= base + first) & (step < base + min(last, kept))
                pl.when(here)(partial(run, kind, side))
        if z_first:
            pl.when(step % tiles == tiles - 1)(partial(apart, len(kinds) - 1))

    most = kept - 1
    far = lambda size: pl.BlockSpec((size, width), lambda s: (0, jnp.minimum(s, most)))
    near = lambda size: pl.BlockSpec(
        (size, width), lambda s: (0, jnp.minimum(jnp.maximum(s - tiles, 0), most))
    )
    both = pl.BlockSpec((mid, width), lambda s: (s // tiles, jnp.minimum(s % tiles, most)))
    sizes = (2 * mid, 2 * mid, mid, 2 * mid, mid)
    out_specs = [far(2 * mid), both, far(mid), near(2 * mid), near(mid)]
    shapes = [array(size, kept * width) for size in sizes]
    if z_first:
        each = half // z_first
        out_specs.append(
            pl.BlockSpec((z_first, 1, each, width), lambda s: (0, 1 - s // tiles, 0, 0))
        )
        shapes.append(array(z_first, 2, each, width))
    return kernel_call(body, name, (2 * tiles,), specs, out_specs, shapes)(*args)


def add_mid_kernel(k01_ref, rx_ref, k10_ref, ry_ref, y_ref, x_ref):
    half = k01_ref.shape[0]
    y_ref[...] = (k01_ref[...].astype(f32) + rx_ref[pl.ds(half, half), :].astype(f32)).astype(bf16)
    x_ref[...] = (k10_ref[...].astype(f32) + ry_ref[pl.ds(0, half), :].astype(f32)).astype(bf16)


def add_last_kernel(k00_ref, rx_ref, ry_ref, y2_ref, x2_ref, out_ref):
    half = y2_ref.shape[0]
    top, low = pl.ds(0, half), pl.ds(half, half)
    near = (rx_ref[top, :], y2_ref[...]), (ry_ref[low, :], x2_ref[...])
    for here, (one, two) in zip((top, low), near):
        total = k00_ref[here, :].astype(f32) + one.astype(f32) + two.astype(f32)
        out_ref[here, :] = total.astype(bf16)


def small_call(body, name, args, shapes):
    out_specs = [whole(s.shape) for s in shapes]
    return kernel_call(body, name, (1,), [whole(a.shape) for a in args], out_specs, shapes)(*args)


class Links:
    def __init__(self):
        self.nz = lax.axis_size("wide") // 4
        self.across = self.table(lambda z, y, c, x: (z, y, c, 1 - x))
        self.beside = self.table(lambda z, y, c, x: (z, 1 - y, c, x))
        self.twin = self.table(lambda z, y, c, x: (z, y, 1 - c, x))

    def table(self, source):
        pairs = []
        for z in range(self.nz):
            for y in range(2):
                for c in range(2):
                    for x in range(2):
                        zs, ys, cs, xs = source(z, y, c, x)
                        pairs.append(
                            (((zs * 2 + ys) * 2 + cs) * 2 + xs, ((z * 2 + y) * 2 + c) * 2 + x)
                        )
        return pairs

    def from_z(self, rows, step):
        shift = self.table(lambda z, y, c, x: ((z + step) % self.nz, y, c, x))
        return lax.ppermute(rows, AXES, shift)

    def z_groups(self):
        rest = [(y, c, x) for y in range(2) for c in range(2) for x in range(2)]
        return [
            [((z * 2 + y) * 2 + c) * 2 + x for z in range(self.nz)] for y, c, x in rest
        ]

    def z_sum_apart(self, rows):
        return lax.psum_scatter(
            rows, AXES, scatter_dimension=0, tiled=True, axis_index_groups=self.z_groups()
        )

    def z_sum(self, rows):
        got = lax.all_to_all(rows, AXES, 0, 0, tiled=True, axis_index_groups=self.z_groups())
        return got.reshape(self.nz, -1, rows.shape[1])

    def z_all(self, rows):
        return lax.all_gather(
            rows, AXES, axis=0, tiled=True, axis_index_groups=self.z_groups()
        )

    def x(self, rows):
        return lax.ppermute(rows, AXES, self.across)

    def y(self, rows):
        return lax.ppermute(rows, AXES, self.beside)

    def c(self, rows):
        return lax.ppermute(rows, AXES, self.twin)

    def flip(self, rows, bit):
        swap = self.table(lambda z, y, c, x: (z ^ bit, y, c, x))
        return lax.ppermute(rows, AXES, swap)


def after(done, *values):
    out = lax.optimization_barrier((values, done))[0]
    return out if len(values) > 1 else out[0]


def start_far(links, near):
    by_x, by_y = near
    cut = by_x.shape[0] // 2
    return links.x(by_y[:cut]), links.y(by_x[cut:])


class Home:
    def __init__(self, links):
        self.links = links

    def first(self, pieces):
        x_first, y_first, self.k10_low, self.k00, self.k01_top = pieces
        self.x_got, self.y_got = self.links.x(x_first), self.links.y(y_first)

    def middle(self):
        half = self.k01_top.shape[0]
        args = (self.k01_top, self.x_got, self.k10_low, self.y_got)
        shape = array(*self.k01_top.shape)
        out_y, out_x = small_call(add_mid_kernel, "add_mid", args, [shape, shape])
        return out_y, out_x

    def second(self, out_y, out_x):
        self.y_last, self.x_last = self.links.y(out_y), self.links.x(out_x)

    def last(self, done, apart):
        y_last, x_last = after(done, self.y_last, self.x_last)
        args = (self.k00, self.x_got, self.y_got, y_last, x_last)
        (total,) = small_call(add_last_kernel, "add_last", args, [array(*self.k00.shape)])
        self.home = self.links.z_sum_apart(total)[None] if apart else self.links.z_sum(total)
        return total

    def value(self, done, scale):
        return jnp.sum(after(done, self.home).astype(f32), axis=0) * scale


def own_slot(
    clips,
    cotangent,
    clip_live,
    qkv_weight,
    q_bias,
    v_bias,
    proj_weight,
    fc1_weight,
    fc1_bias,
    fc2_weight,
    ln_gains,
    ln_biases,
    out_bias,
):
    links = Links()
    slot_count, shard_rows, width = clips.shape
    wide_count = lax.axis_size("wide")
    length = 2 * shard_rows
    block = qkv_weight.shape[0]
    heads_cols = qkv_weight.shape[2]
    hidden_here = fc1_weight.shape[1]
    grad_scale = 1.0 / math.sqrt(wide_count * slot_count * length)
    wide_at = lax.axis_index("wide")
    t = lax.axis_index("tp")
    z_at, y_at, c_at = wide_at // 4, (wide_at // 2) % 2, wide_at % 2
    qkv_cols = 3 * heads_cols
    pick = lambda both, at: lax.dynamic_index_in_dim(both, at, 0, keepdims=False)
    row = lambda vector: vector.reshape(1, -1)

    sent_rows = jnp.concatenate([pick(clips, 1 - t), pick(cotangent, 1 - t)], axis=0)
    q_shard, sent_rows = after((), qkv_weight.reshape(block, qkv_cols), sent_rows)
    two_shard = jnp.concatenate([fc1_weight, proj_weight.T], axis=1)
    along_two = links.z_all(two_shard)
    steps_one = [links.from_z(q_shard, k) for k in range(1, links.nz)]
    got_rows = links.x(sent_rows)
    far_small = jnp.concatenate([q_bias, v_bias, fc1_bias]).reshape(-1, 128)
    far_small = links.x(far_small).reshape(-1)

    spot = jnp.arange(width)
    rel = spot // block
    kc, ky, kz = rel // (2 * links.nz), (rel // links.nz) % 2, rel % links.nz
    home = (kz * 2 + (y_at ^ ky)) * 2 + (c_at ^ kc)
    order = spot[:, None] == (home * block + spot % block)[None, :]
    order_b = order.astype(bf16)
    order_f = order.astype(f32)
    vectors = jnp.dot(
        jnp.concatenate([ln_gains, ln_biases, out_bias], axis=0),
        order_f,
        precision=lax.Precision.HIGHEST,
    )
    gains, shifts, outs = (
        (vectors[2 * i : 2 * i + 1], vectors[2 * i + 1 : 2 * i + 2]) for i in range(3)
    )
    live = jnp.full((1, width), pick(clip_live, t).astype(f32))
    along_one = jnp.zeros((links.nz * block, qkv_cols), bf16)
    for step, piece in enumerate([q_shard] + steps_one):
        at = (z_at + step) % links.nz * block
        along_one = lax.dynamic_update_slice(along_one, piece, (at, 0))
    got_rows, far_small = after(along_one, got_rows, far_small)
    near_one = links.x(along_one), links.y(along_one)
    x, h1, h1_t = enter(pick(clips, t), got_rows[:shard_rows], order_b, gains[0], shifts[0])
    e, e_t = enter_cot(pick(cotangent, t), got_rows[shard_rows:], order_b, live)
    half = width // 2
    twin_rows = jnp.concatenate([e_t[half:], h1_t[half:]], axis=0)
    near_one, along_two, twin_rows, fc2_turned = after(
        (twin_rows, h1, e), near_one, along_two, twin_rows, fc2_weight.T
    )
    along_three = links.z_all(after(along_two, fc2_turned))
    far_one = start_far(links, near_one)
    other_one = [links.c(piece) for piece in (after(near_one, along_one), *near_one)]
    other_one, along_two = after((), other_one, along_two)
    near_two = links.x(along_two), links.y(along_two)
    far_one, twin_rows = after(other_one, far_one, twin_rows)
    other_one += [links.c(piece) for piece in far_one]
    twin_rows = links.c(twin_rows)
    twin_rows, other_one = after((), twin_rows, other_one)
    w_one = [along_one, *near_one, *far_one, *other_one]
    zero_row = jnp.zeros((heads_cols,), f32)
    biases = jnp.stack(
        [
            jnp.concatenate([q_bias, zero_row, v_bias]),
            jnp.concatenate(
                [far_small[:heads_cols], zero_row, far_small[heads_cols : 2 * heads_cols]]
            ),
        ]
    )[:, None]
    fc1_biases = row(jnp.concatenate([fc1_bias, far_small[2 * heads_cols :]]))
    qkv = project(h1, w_one, biases)
    attn, lse = attend_fwd(qkv)

    near_two, lse_rows = after(attn, near_two, lse.T)
    far_two = start_far(links, near_two)
    other_two = [links.c(piece) for piece in (after(near_two, along_two), *near_two)]
    other_two, along_three = after((), other_two, along_three)

    near_three = links.x(along_three), links.y(along_three)
    other_three = [links.c(along_three)]
    far_two = after(other_two, far_two)
    other_two += [links.c(piece) for piece in far_two]
    w_two = [along_two, *near_two, *far_two, *other_two]
    y, h2, h2_t = join_heads(attn, x, w_two, hidden_here, outs[0], gains[1], shifts[1])
    hidden, slope = expand(h2, w_two, fc1_biases, hidden_here)
    near_three, other_three, hidden, slope, h2_t = after(
        (), near_three, other_three, hidden, slope, h2_t
    )

    far_three = start_far(links, near_three)
    twin_hidden = links.c(hidden)
    other_three += [links.c(near_three[0])]
    twin_attn = links.c(attn)

    stack = lambda one, two: jnp.concatenate([one[...], two[...]], axis=0)
    join = lambda one, two: jnp.concatenate([one[...], two[...]], axis=1)
    tiles = hidden_here // TILE
    left_at = lambda at: pl.BlockSpec((half, length), lambda s: (at, 0))

    def tile_spec(count):
        def at(s):
            tile = jnp.minimum(s % count, tiles - 1)
            return (0, jnp.where(s < count, tiles, 0) + tile)

        return pl.BlockSpec((length, TILE), at)

    attn_spec = lambda count: pl.BlockSpec((length, TILE), lambda s: (0, 1 - s // count))

    def grad_fc2():
        terms = lambda refs, kind: (join(*refs[:2]), stack(*refs[2:]))
        args = [e_t, twin_rows, hidden, twin_hidden]
        specs = [left_at(0), left_at(0)] + [tile_spec(tiles)] * 2
        return both_sides(args, specs, (0,), terms, "grad_fc2", tiles)

    def grad_two():
        count = tiles + 1

        def terms(refs, kind):
            return join(*refs[4 * kind :][:2]), stack(*refs[4 * kind + 2 :][:2])

        args = [h2_t, twin_h2, du, twin_du, da_t, twin_da, attn, twin_attn]
        specs = [left_at(0)] * 2 + [tile_spec(count)] * 2
        specs += [left_at(0)] * 2 + [attn_spec(count)] * 2
        return both_sides(args, specs, (0, tiles), terms, "grad_two", count)

    def grad_qkv():
        narrow = TILE // 2
        count = qkv_cols // narrow

        def terms(refs, kind):
            return join(*refs[:2]), jnp.concatenate([refs[2][0], refs[3][0]], axis=0)

        def at(s):
            tile, side = s % count, 1 - s // count
            return (tile // 2, 0, 2 * side + tile % 2)

        args = [h1_t, twin_rows, dp, twin_dp]
        specs = [left_at(0), left_at(1)] + [pl.BlockSpec((1, length, narrow), at)] * 2
        return both_sides(args, specs, (0,), terms, "grad_qkv", count, narrow, links.nz)

    def enter_window(done, *homes):
        for home in homes:
            home.x_got, home.y_got = after(done, home.x_got, home.y_got)

    home_fc2, home_two, home_qkv = Home(links), Home(links), Home(links)

    pieces = grad_fc2()
    far_three, other_three, near_three, twin_attn, pieces, h2_sent = after(
        (), far_three, other_three, near_three, twin_attn, pieces, h2_t[half:]
    )

    home_fc2.first(pieces)
    other_three += [links.c(piece) for piece in (near_three[1], *far_three)]
    w_fc2 = [along_three, *near_three, *far_three, *other_three]
    du, fc1b_sum = hidden_back(e, slope, w_fc2)
    mid, da, da_t, da_t_far, second_sums = second_back(du, w_two, hidden_here, y, e, gains[1])
    enter_window(da, home_fc2)
    du, da, da_t, da_t_far = after(home_fc2.x_got, du, da, da_t, da_t_far)

    twin_du = links.c(du)
    twin_da, twin_h2 = links.c(da_t_far), links.c(h2_sent)
    home_fc2.second(*home_fc2.middle())
    d_heads = heads_back(da, w_two, hidden_here)
    twin_du, twin_da, twin_h2 = after(d_heads, twin_du, twin_da, twin_h2)
    pieces = grad_two()
    pieces, d_heads, home_fc2.y_last, home_fc2.x_last = after(
        (), pieces, d_heads, home_fc2.y_last, home_fc2.x_last
    )

    home_two.first(pieces)
    moved = home_fc2.last(pieces, True)
    dp, q_sums, v_sums = attend_bwd(qkv, after(moved, d_heads), lse_rows)
    grad_near, grad_sent_rows, first_sums = first_back(
        dp, w_one, x, mid, gains[0], order_b
    )
    enter_window(grad_near, home_two)
    dp, first_sums = after(home_two.x_got, dp, first_sums)

    twin_dp = links.c(dp)
    moved = home_two.middle()
    home_two.second(*moved)
    sums = jnp.concatenate(
        [first_sums[:1], second_sums[:1], first_sums[1:], second_sums[1:]], axis=0
    )
    sums = lax.dot_general(
        after(moved, sums), order_f, (((1,), (1,)), ((), ())), precision=lax.Precision.HIGHEST
    )

    def placed(both):
        size = both.shape[1] // 2
        return jnp.where(t == 0, both[0], jnp.concatenate([both[0, size:], both[0, :size]]))

    small = [sums.reshape(-1), placed(q_sums), placed(v_sums), placed(fc1b_sum)]
    small = jnp.concatenate(small).reshape(-1, 128)
    small_got = links.c(after(moved, small))
    twin_dp, small_got = after(moved, twin_dp, small_got)
    small = small + small_got
    small_got = links.flip(small, 1)
    *pieces, by_z = grad_qkv()
    pieces, by_z, home_two.y_last, home_two.x_last, small, small_got = after(
        (), pieces, by_z, home_two.y_last, home_two.x_last, small, small_got
    )

    home_qkv.first(pieces)
    by_z = links.z_sum(by_z.reshape(-1, by_z.shape[-1]))
    small = small + small_got
    small_got = links.x(small)
    moved = home_two.last(pieces, True)
    out_near, out_sent = layer_out(after(moved, hidden), w_fc2, y, outs[1], live, order_b)
    enter_window(out_near, home_qkv)
    moved, small, small_got, out_sent, grad_sent_rows = after(
        (), home_qkv.middle(), small, small_got, out_sent, grad_sent_rows
    )

    home_qkv.second(*moved)
    grad_got = links.x(grad_sent_rows)
    small = small + small_got
    small_got = links.y(small)
    moved = home_qkv.last((), False)
    moved, out_sent, small, small_got = after((), moved, out_sent, small, small_got)

    by_z = jnp.sum(after(moved, by_z).astype(f32), axis=0)
    by_z = by_z.reshape(2, 2, block, -1)
    v_got = links.y(by_z[:, 1].astype(bf16).reshape(2 * block, -1))
    out_got = links.x(out_sent)
    small = small + small_got
    bit = 2
    while bit < links.nz:
        small = small + links.flip(small, bit)
        bit *= 2
    by_y = by_z[:, 0].reshape(2 * block, -1) + v_got.astype(f32)
    by_y, small, grad_got, home_two.home, home_fc2.home = after(
        (), by_y, small, grad_got, home_two.home, home_fc2.home
    )
    v_got = links.x(by_y[block:].astype(bf16))
    g_v = (by_y[:block] + v_got.astype(f32)) * grad_scale
    small = small.reshape(-1) * grad_scale
    sums = small[: 6 * width].reshape(6, width)
    own = lambda first, size: lax.dynamic_slice_in_dim(small, first + t * size, size, 0)
    g_fc2 = home_fc2.value(moved, grad_scale)
    g_two = home_two.value(moved, grad_scale)
    g_fc2, g_proj, g_fc1 = g_fc2.T, g_two[:, hidden_here:].T, g_two[:, :hidden_here]
    g_v, g_fc2, g_proj, g_fc1, out_got = after((), g_v, g_fc2, g_proj, g_fc1, out_got)
    g_qkv = home_qkv.value(g_v, grad_scale)

    def both_slots(near, got):
        return jnp.where(t == 0, jnp.stack([near, got]), jnp.stack([got, near]))

    return (
        both_slots(out_near, out_got),
        both_slots(grad_near, grad_got).astype(f32),
        jnp.concatenate([g_qkv, g_v], axis=1).reshape(block, 3, heads_cols),
        own(6 * width, heads_cols),
        own(6 * width + 2 * heads_cols, heads_cols),
        g_proj,
        g_fc1,
        own(6 * width + 4 * heads_cols, hidden_here),
        g_fc2,
        sums[0:2],
        sums[2:4],
        sums[4:6],
    )


def solution(mesh):
    body = own_slot if fits_own_slot(mesh) else shared_slots
    return jax.shard_map(
        body,
        mesh=mesh,
        in_specs=(
            P("wide", "tp", None),
            P("wide", "tp", None),
            P("wide"),
            P("wide", None, "tp"),
            P("tp"),
            P("tp"),
            P("tp", "wide"),
            P("wide", "tp"),
            P("tp"),
            P("tp", "wide"),
            P(),
            P(),
            P(),
        ),
        out_specs=(
            P("wide", "tp", None),
            P("wide", "tp", None),
            P("wide", None, "tp"),
            P("tp"),
            P("tp"),
            P("tp", "wide"),
            P("wide", "tp"),
            P("tp"),
            P("tp", "wide"),
            P(),
            P(),
            P(),
        ),
        check_vma=False,
    )
```
